32 devices in a mesh: seq: 8 (over y, x, core), head: 4 (over z).
Axes of the slice: x: 2, y: 2, z: 4, core: 2. Of those that a mesh axis runs over, the one named last changes fastest.
Arguments:
- tokens: bfloat16 [32, 512, 1024], P('seq', 'head'), may hold values from -6 to 6
- lengths: int32 [32], P('seq'), may hold values from 128 to 512, as said below
- separators: int32 [32], P('seq'), may hold values from 32 to 383, as said below
- type_table: float32 [2, 1024], replicated, may hold values from -3 to 3
- project_in: bfloat16 [2, 1024, 3072], P(None, 'seq'), may hold values from -0.1875 to 0.1875
- project_out: bfloat16 [2, 1024, 1024], P(None, 'seq'), may hold values from -0.75 to 0.75
- up_weight: bfloat16 [2, 1024, 4096], P(None, 'seq', 'head'), may hold values from -0.1875 to 0.1875
- down_weight: bfloat16 [2, 4096, 1024], P(None, 'head', 'seq'), may hold values from -0.09375 to 0.09375
- first_norm_gain: float32 [2, 1024], replicated, may hold values from 0.5 to 1.5
- second_norm_gain: float32 [2, 1024], replicated, may hold values from 0.5 to 1.5
- query_bias: float32 [2, 1024], replicated, may hold values from -3 to 3
- value_bias: float32 [2, 1024], replicated, may hold values from -3 to 3
- output_bias: float32 [2, 1024], replicated, may hold values from -3 to 3
- first_norm_bias: float32 [2, 1024], replicated, may hold values from -3 to 3
- hidden_bias: float32 [2, 4096], replicated, may hold values from -3 to 3
- down_bias: float32 [2, 1024], replicated, may hold values from -3 to 3
- second_norm_bias: float32 [2, 1024], replicated, may hold values from -3 to 3
- cotangent: bfloat16 [32, 512, 1024], P('seq', 'head'), may hold values from -6 to 6
Outputs:
- activations: bfloat16 [32, 512, 1024], P('seq', 'head')
- input_grad: float32 [32, 512, 1024], P('seq', 'head')
- query_bias_grad: float32 [2, 1024], replicated
- value_bias_grad: float32 [2, 1024], replicated
- output_bias_grad: float32 [2, 1024], replicated
- first_norm_bias_grad: float32 [2, 1024], replicated
- hidden_bias_grad: float32 [2, 4096], replicated
- down_bias_grad: float32 [2, 1024], replicated
- second_norm_bias_grad: float32 [2, 1024], replicated
The draws below stay inside these ranges and needn't reach their ends.
Inputs may be any that keep to these rules, and one draw needn't show every extreme that they name: `lengths`: in the 4 rows of each index of seq (rows k * 4 to (k + 1) * 4 - 1), one row uses all 512 slots. `separators`: each row's separator lies between a quarter and three quarters of its length.
All inputs are finite; a program needn't handle non-finite values.
Results may differ from the reference program's by a relative error of at most 0.017.
Values may be sent and summed in bfloat16 or wider, within the bound.
A program may use at most 192 MiB of HBM per device.

```python
import math
import jax
import jax.numpy as jnp
from jax import lax

HEADS = 16
HEAD_DIM = 64
D = 1024
FF = 4096
SLOTS = 512
LAYERS = 2
ROWS_DEV = 4
ROWS = 32


def row_lengths(key):
    spread_key = jax.random.fold_in(key, 11)
    pick_key = jax.random.fold_in(key, 12)
    drawn = jax.random.randint(spread_key, (ROWS,), SLOTS // 4, SLOTS + 1)
    chosen = jax.random.randint(pick_key, (ROWS // ROWS_DEV, 1), 0, ROWS_DEV)
    full = (jnp.arange(ROWS_DEV)[None, :] == chosen).reshape(ROWS)
    return jnp.where(full, SLOTS, drawn).astype(jnp.int32)


def draw_lengths(key, part):
    return row_lengths(key)


def draw_separators(key, part):
    totals = row_lengths(key)
    key = jax.random.fold_in(key, 3)
    return jax.random.randint(key, (ROWS,), totals // 4, totals // 2 + totals // 4).astype(jnp.int32)


def block_scale(stream_key, shape, cuts, least, high):
    loudness, own = 1.0, jax.random.fold_in(stream_key, 6)
    for position, parts in cuts:
        draws = jnp.exp(jax.random.uniform(jax.random.fold_in(own, position), (parts,), jnp.float32, least / len(cuts), high / len(cuts)))
        loudness = loudness * jnp.repeat(draws, shape[position] // parts).reshape([-1 if axis == position else 1 for axis in range(len(shape))])
    return loudness


def centred(stream_key, shape, scale, bound, shards=(), held_as=jnp.bfloat16):
    values = scale * jax.random.normal(stream_key, shape, jnp.float32)
    if shards:
        values = values * block_scale(stream_key, shape, shards, -0.22, 0.18)
    return jnp.clip(values, -bound, bound).astype(held_as)


def setup_inputs(seed: int = 0) -> dict:
    key_list = jax.random.split(jax.random.key(seed), 19)
    tokens = centred(key_list[0], (ROWS, SLOTS, D), 1.0, 6.0, ((0, 8), (1, 4)))
    lengths = draw_lengths(jax.random.fold_in(key_list[18], 71), 0)
    separators = draw_separators(jax.random.fold_in(key_list[18], 71), 0)
    type_table = centred(key_list[3], (2, D), 0.5, 3.0, (), jnp.float32)
    project_in = centred(key_list[4], (LAYERS, D, 3 * D), D ** -0.5, 0.1875, ((1, 8),))
    project_out = centred(key_list[5], (LAYERS, D, D), (D // 16) ** -0.5, 0.75, ((1, 8),))
    up_weight = centred(key_list[6], (LAYERS, D, FF), D ** -0.5, 0.1875, ((1, 8), (2, 4)))
    down_weight = centred(key_list[7], (LAYERS, FF, D), FF ** -0.5, 0.09375, ((1, 4), (2, 8)))
    first_norm_gain = jnp.clip(1.0 + 0.1 * jax.random.normal(key_list[8], (LAYERS, D), jnp.float32), 0.5, 1.5)
    second_norm_gain = jnp.clip(1.0 + 0.1 * jax.random.normal(key_list[9], (LAYERS, D), jnp.float32), 0.5, 1.5)
    query_bias = centred(key_list[10], (LAYERS, D), 0.5, 3.0, (), jnp.float32)
    value_bias = centred(key_list[11], (LAYERS, D), 0.5, 3.0, (), jnp.float32)
    output_bias = centred(key_list[12], (LAYERS, D), 0.5, 3.0, (), jnp.float32)
    first_norm_bias = centred(key_list[13], (LAYERS, D), 0.5, 3.0, (), jnp.float32)
    hidden_bias = centred(key_list[14], (LAYERS, FF), 0.5, 3.0, (), jnp.float32)
    down_bias = centred(key_list[15], (LAYERS, D), 0.5, 3.0, (), jnp.float32)
    second_norm_bias = centred(key_list[16], (LAYERS, D), 0.5, 3.0, (), jnp.float32)
    cotangent = centred(key_list[17], (ROWS, SLOTS, D), 1.0, 6.0, ((0, 8), (1, 4)))
    return {"tokens": tokens, "lengths": lengths, "separators": separators, "type_table": type_table, "project_in": project_in, "project_out": project_out, "up_weight": up_weight, "down_weight": down_weight, "first_norm_gain": first_norm_gain, "second_norm_gain": second_norm_gain, "query_bias": query_bias, "value_bias": value_bias, "output_bias": output_bias, "first_norm_bias": first_norm_bias, "hidden_bias": hidden_bias, "down_bias": down_bias, "second_norm_bias": second_norm_bias, "cotangent": cotangent}


EPS = 1e-06
MASKED = -1000000000.0
HIGH = lax.Precision.HIGHEST

@jax.custom_vjp
def low(v):
    return lax.optimization_barrier(v.astype(jnp.bfloat16)).astype(jnp.float32)

@jax.custom_vjp
def low_back(v):
    return v

def low_keep(v):
    return (low(v), None)

def low_pass(kept, grad):
    return (grad,)

def back_keep(v):
    return (v, None)

def back_low(kept, grad):
    return (low(grad),)
low.defvjp(low_keep, low_pass)
low_back.defvjp(back_keep, back_low)

def layer_norm(total, gain, bias):
    mean = lax.optimization_barrier(jnp.mean(total, -1, keepdims=True))
    centered = total - mean
    spread = lax.optimization_barrier(jnp.mean(centered * centered, -1, keepdims=True))
    return centered * lax.rsqrt(spread + EPS) * gain + bias

def gelu_exact(value):
    return jax.nn.gelu(value, approximate=False)

def attend_row(packed):
    queries, keys, values, length = packed
    scores = jnp.einsum('qhd,khd->hqk', queries, keys, precision=HIGH) * HEAD_DIM ** (-0.5)
    valid = jnp.arange(SLOTS) < length
    scores = low_back(jnp.where(valid[None, None, :], scores, MASKED))
    peak = lax.optimization_barrier(jnp.max(scores, -1, keepdims=True))
    expo = jnp.exp(scores - peak)
    probs = expo / lax.optimization_barrier(jnp.sum(expo, -1, keepdims=True))
    return jnp.einsum('hqk,khd->qhd', low(probs), values, precision=HIGH)

def one_layer(state, lengths, weights, biases):
    project_in, project_out, up_weight, down_weight, first_gain, second_gain = weights
    query_bias, value_bias, output_bias, first_bias, hidden_bias, down_bias, second_bias = biases
    count = state.shape[0]
    flat = state.reshape(-1, D)
    joined = jnp.concatenate([query_bias, jnp.zeros_like(query_bias), value_bias])
    projected = low_back(low(jnp.dot(low(flat), project_in, precision=HIGH) + joined))
    projected = projected.reshape(count, SLOTS, 3, HEADS, HEAD_DIM)
    mixed = lax.map(jax.checkpoint(attend_row), (projected[:, :, 0], projected[:, :, 1], projected[:, :, 2], lengths))
    mixed = low_back(low(mixed.reshape(-1, D)))
    attn_out = low_back(jnp.dot(mixed, project_out, precision=HIGH)) + output_bias
    normed = layer_norm(flat + attn_out, first_gain, first_bias)
    hidden = low_back(jnp.dot(low(normed), up_weight, precision=HIGH)) + hidden_bias
    branch = low_back(jnp.dot(low(gelu_exact(hidden)), down_weight, precision=HIGH)) + down_bias
    return layer_norm(normed + branch, second_gain, second_bias).reshape(count, SLOTS, D)

def forward(tokens, lengths, separators, type_table, weights, biases):
    positions = jnp.arange(SLOTS)[None, :]
    second = (positions > separators[:, None]) & (positions < lengths[:, None])
    state = tokens + jnp.where(second[:, :, None], type_table[1], type_table[0])
    for layer in range(LAYERS):
        state = one_layer(state, lengths, tuple((w[layer] for w in weights)), tuple((b[layer] for b in biases)))
    return state

def reference(tokens, lengths, separators, type_table, project_in, project_out, up_weight, down_weight, first_norm_gain, second_norm_gain, query_bias, value_bias, output_bias, first_norm_bias, hidden_bias, down_bias, second_norm_bias, cotangent):
    weights = (project_in.astype(jnp.float32), project_out.astype(jnp.float32), up_weight.astype(jnp.float32), down_weight.astype(jnp.float32), first_norm_gain, second_norm_gain)
    biases = (query_bias, value_bias, output_bias, first_norm_bias, hidden_bias, down_bias, second_norm_bias)
    group = math.gcd(ROWS, 8)
    blocks = ROWS // group

    def group_step(totals, packed):
        rows_in, length_in, separator_in, grad_in = packed

        def run(row_block, bias_set):
            return forward(row_block, length_in, separator_in, type_table, weights, bias_set)
        output, back = jax.vjp(run, rows_in.astype(jnp.float32), biases)
        grad_rows, grad_biases = back(grad_in.astype(jnp.float32))
        totals = jax.tree.map(jnp.add, totals, grad_biases)
        return (totals, (output.astype(jnp.bfloat16), grad_rows))
    zeros = tuple((jnp.zeros_like(b) for b in biases))
    packed = (tokens.reshape(blocks, group, SLOTS, D), lengths.reshape(blocks, group), separators.reshape(blocks, group), cotangent.reshape(blocks, group, SLOTS, D))
    totals, (outputs, grads) = lax.scan(group_step, zeros, packed)
    return (outputs.reshape(ROWS, SLOTS, D), grads.reshape(ROWS, SLOTS, D), totals[0], totals[1], totals[2], totals[3], totals[4], totals[5], totals[6])
```

```python
import functools

import jax
import jax.numpy as jnp
from jax import lax
from jax.experimental import pallas as pl
from jax.experimental.pallas import tpu as pltpu
from jax.sharding import PartitionSpec as P

F32 = jnp.float32
BF16 = jnp.bfloat16
MESH = pl.DeviceIdType.MESH
HEAD_DIM = 64
LAYERS = 2
EPS = 1e-06
MASKED = -1000000000.0
ROOT_HALF = 0.7071067811865476
ROOT_TAU = 0.3989422804014327
RING = 4
WIDTH = 1024
SLOTS = 512
QUARTER = SLOTS // RING
CHUNK = 256


def nn(left, right):
    return jnp.dot(left, right, preferred_element_type=F32)


def nt(left, right):
    return lax.dot_general(left, right, (((1,), (1,)), ((), ())), preferred_element_type=F32)


def tn(left, right):
    return lax.dot_general(left, right, (((0,), (0,)), ((), ())), preferred_element_type=F32)


def place():
    s, z = lax.axis_index("seq"), lax.axis_index("head")
    c, x, y = lax.rem(s, 2), lax.rem(lax.div(s, 2), 2), lax.div(s, 4)
    return s, z, c, x, y


def peers(s, z, c, x, y):
    return (s + 2 - 4 * x, z), (s + 4 - 8 * y, z), (s + 1 - 2 * c, z)


def greet(near_x, near_y, twin, s, z):
    barrier = pltpu.get_barrier_semaphore()
    for device in (near_x, near_y, twin):
        pl.semaphore_signal(barrier, inc=1, device_id=device, device_id_type=MESH)
    for step in range(1, RING):
        pl.semaphore_signal(
            barrier, inc=1, device_id=(s, lax.rem(z + step, RING)), device_id_type=MESH
        )
    pl.semaphore_wait(barrier, 3 + RING - 1)


def forward_kernel(
    lengths_ref, separators_ref,
    tokens_ref, cot_ref, in_ref, out_ref, up_ref,
    down_ref, table_ref, gain1_ref, gain2_ref, qb_ref, vb_ref, ob_ref, b1_ref, hb_ref, db_ref, b2_ref,
    g_in, g_out, g_ff, cot_row, act_row, s_qkv, s_mix, s_expo, s_inv, s_n, s_rs, s_gp,
    tok_v, state_v, xb_v, qkv_v, mix_v, mixed_v, n_v, rs_v, normed_v, acc_v, active_v, gp_v, e_v, inv_v, w_v, dn_v,
    tok_s, tok_r, cot_s, cot_r, at_s, at_r, ff_s, ff_r, z_s, z_r, f_s, f_r, cc_s, cc_r,
    own_sem, dn_sem, w_sem, save_sem, e_sem, gp_sem,
):
    s, z, c, x, y = place()
    near_x, near_y, twin = peers(s, z, c, x, y)
    half = QUARTER // 2
    A, B = pl.ds(0, half), pl.ds(half, half)
    every = slice(None)
    sent = []

    def remote(src, dst, ss, rs, device):
        return pltpu.make_async_remote_copy(
            src_ref=src, dst_ref=dst, send_sem=ss, recv_sem=rs, device_id=device, device_id_type=MESH
        )

    def go(copy):
        copy.start()
        sent.append(copy)

    own = []
    for l in range(LAYERS):
        own.append((
            pltpu.make_async_copy(in_ref.at[l], g_in.at[l, y, x, c], own_sem.at[l, 0]),
            pltpu.make_async_copy(out_ref.at[l], g_out.at[l, y, x, c], own_sem.at[l, 1]),
            pltpu.make_async_copy(up_ref.at[l], g_ff.at[l, z, 0, y, x, c], own_sem.at[l, 2]),
        ))
    own_down = [
        pltpu.make_async_copy(dn_v.at[l], g_ff.at[l, z, 1, y, x, c], dn_sem.at[l]) for l in range(LAYERS)
    ]

    gathered = (g_in, g_out)
    shard = (in_ref, out_ref)

    def at_first(l, t):
        g = gathered[t]
        return (
            remote(shard[t].at[l, A], g.at[l, y, x, c, A], at_s.at[l, t, 0], at_r.at[l, t, 0], near_x),
            remote(shard[t].at[l, B], g.at[l, y, x, c, B], at_s.at[l, t, 1], at_r.at[l, t, 1], near_y),
        )

    def at_last(l, t):
        g = gathered[t]
        pair, pile = g.at[l, y, every, c, A], g.at[l, every, x, c, B]
        return (
            remote(pair, pair, at_s.at[l, t, 2], at_r.at[l, t, 2], near_y),
            remote(pile, pile, at_s.at[l, t, 3], at_r.at[l, t, 3], near_x),
        )

    def at_core(l, t):
        part = gathered[t].at[l, every, every, c]
        return remote(part, part, at_s.at[l, t, 4], at_r.at[l, t, 4], twin)

    def at_send(l, t):
        for copy in at_first(l, t):
            go(copy)

    def at_pass(l, t, side):
        at_first(l, t)[side].wait_recv()
        go(at_last(l, t)[side])

    def at_share(l, t):
        for copy in at_last(l, t):
            copy.wait_recv()
        go(at_core(l, t))

    def rank(i):
        near = z if i == 0 else None
        if i == 0:
            return near
        low = jnp.where(z < 2, z, RING - 1 - z)
        block = (1 - low) if i == 1 else i
        return jnp.where(z < 2, block, RING - 1 - block)

    def ff_part(l, block, side):
        return g_ff.at[l, block, every, y, every, c, A] if side == 0 else g_ff.at[l, block, every, every, x, c, B]

    def ff_first(l):
        a, b = g_ff.at[l, z, every, y, x, c, A], g_ff.at[l, z, every, y, x, c, B]
        return (
            remote(a, a, ff_s.at[l, 0], ff_r.at[l, 0], near_x),
            remote(b, b, ff_s.at[l, 1], ff_r.at[l, 1], near_y),
        )

    def ff_z(l, block, side, way):
        part = ff_part(l, block, side)
        beside = lax.rem(z + 1, RING) if way == 0 else lax.rem(z + RING - 1, RING)
        return remote(part, part, z_s.at[l, block, side, way], z_r.at[l, block, side], (s, beside))

    def ff_last(l, block, side):
        part = ff_part(l, block, side)
        return remote(part, part, f_s.at[l, block, side], f_r.at[l, block, side], near_y if side == 0 else near_x)

    def ff_core(l, block):
        part = g_ff.at[l, block, every, every, every, c]
        return remote(part, part, cc_s.at[l, block], cc_r.at[l, block], twin)

    right = z < RING - 1
    left = z > 0

    def ff_send(l):
        for copy in ff_first(l):
            go(copy)

    def ff_spread(l, side):
        ff_first(l)[side].wait_recv()
        pl.when(right)(ff_z(l, z, side, 0).start)
        pl.when(left)(ff_z(l, z, side, 1).start)

    def ff_cross(l, i, side):
        go(ff_last(l, rank(i), side))

    def ff_relay(l, i, side):
        block = rank(i)
        ff_z(l, block, side, 0).wait_recv()
        pl.when(jnp.logical_and(block < z, right))(ff_z(l, block, side, 0).start)
        pl.when(jnp.logical_and(block > z, left))(ff_z(l, block, side, 1).start)

    def ff_share(l, i):
        block = rank(i)
        for side in range(2):
            ff_last(l, block, side).wait_recv()
        go(ff_core(l, block))

    def ff_drain(l):
        for side in range(2):
            for block in range(RING):
                goes_right = jnp.logical_and(block <= z, right)
                goes_left = jnp.logical_and(block >= z, left)
                pl.when(goes_right)(ff_z(l, block, side, 0).wait_send)
                pl.when(goes_left)(ff_z(l, block, side, 1).wait_send)

    def row_copies(src, dst, ss, rs):
        here = dst.at[pl.ds(pl.multiple_of(z * QUARTER, QUARTER), QUARTER)]
        copies = []
        for step in range(1, RING):
            to = lax.rem(z + step, RING)
            copies.append(remote(src.at[to], here, ss.at[step], rs.at[step], (s, to)))
        return copies, pltpu.make_async_copy(src.at[z], here, ss.at[0])

    def load(slot, src, width=WIDTH):
        copy = pltpu.make_async_copy(src, w_v.at[slot], w_sem.at[slot])
        copy.start()
        return copy

    def weight(slot, cols):
        return w_v[slot, :, :, :, :, cols].reshape(WIDTH, CHUNK)

    def weight_rows(slot, half_index):
        return w_v[slot, half_index].reshape(SLOTS, WIDTH)

    saves = {}
    waiting = []

    def save(key, src, dst, sem):
        copy = pltpu.make_async_copy(src, dst, sem)
        copy.start()
        saves[key] = copy

    def settle(key):
        if key in saves:
            saves.pop(key).wait()

    def rows_loop(body, rows=64):
        def step(r, carry):
            body(pl.ds(pl.multiple_of(r * rows, rows), rows), r * rows)
            return carry
        lax.fori_loop(0, SLOTS // rows, step, 0)

    def norm_rows(total, gain, bias, rr, which):
        mean = jnp.sum(total, -1, keepdims=True) * (1.0 / WIDTH)
        centered = total - mean
        rs = lax.rsqrt(jnp.sum(centered * centered, -1, keepdims=True) * (1.0 / WIDTH) + EPS)
        n = centered * rs
        n_v[which, rr] = n.astype(BF16)
        rs_v[which, rr] = rs + jnp.zeros((64, 128), F32)
        return n * gain + bias

    def start_state():
        length, split = lengths_ref[z], separators_ref[z]

        def body(rr, base):
            pos = lax.broadcasted_iota(jnp.int32, (64, 1), 0) + base
            second = jnp.logical_and(pos > split, pos < length)
            kind = jnp.where(second, table_ref[1:2], table_ref[0:1])
            value = tok_v[rr].astype(F32) + kind
            state_v[rr] = value
            xb_v[rr] = value.astype(BF16)
        rows_loop(body)

    def project(l):
        settle("qkv")
        loads = [load(j, g_in.at[l, :, :, :, :, pl.ds(j * WIDTH, WIDTH)]) for j in range(3)]
        for j in range(3):
            loads[j].wait()
            for k in range(WIDTH // CHUNK):
                cols = pl.ds(k * CHUNK, CHUNK)
                value = nn(xb_v[...], weight(j, cols))
                if j == 0:
                    value = (value + qb_ref[l:l + 1, k * CHUNK:(k + 1) * CHUNK]).astype(BF16) * BF16(HEAD_DIM ** -0.5)
                elif j == 2:
                    value = value + vb_ref[l:l + 1, k * CHUNK:(k + 1) * CHUNK]
                qkv_v[:, pl.ds(j * WIDTH + k * CHUNK, CHUNK)] = value.astype(BF16)
        save("qkv", qkv_v, s_qkv.at[l], save_sem.at[0])

    pairs = WIDTH // (2 * HEAD_DIM)
    wide = 2 * HEAD_DIM

    def attend(l, first, last):
        bias = jnp.where(
            lax.broadcasted_iota(jnp.int32, (1, SLOTS), 1) < lengths_ref[z], 0.0, MASKED
        ).astype(F32)
        lane = lax.broadcasted_iota(jnp.int32, (SLOTS, wide), 1) < HEAD_DIM

        def e_save(p, slot):
            return (
                pltpu.make_async_copy(e_v.at[slot], s_expo.at[l, p], e_sem.at[slot, 0]),
                pltpu.make_async_copy(inv_v.at[slot], s_inv.at[l, p], e_sem.at[slot, 1]),
            )

        def step(p, carry):
            slot = lax.rem(p, 2)

            @pl.when(p >= 2)
            def _():
                for copy in e_save(p - 2, slot):
                    copy.wait()

            q = qkv_v[:, pl.ds(pl.multiple_of(p * wide, wide), wide)]
            k = qkv_v[:, pl.ds(pl.multiple_of(WIDTH + p * wide, wide), wide)]
            v = qkv_v[:, pl.ds(pl.multiple_of(2 * WIDTH + p * wide, wide), wide)]
            outs, invs = [], []
            for h in range(2):
                mine = jnp.where(lane, q, 0) if h == 0 else jnp.where(lane, 0, q)
                scores = nt(mine.astype(BF16), k) + bias
                expo = jnp.exp(scores - jnp.max(scores, -1, keepdims=True))
                inv = 1.0 / jnp.sum(expo, -1, keepdims=True)
                expo = expo.astype(BF16)
                e_v[slot, h] = expo
                invs.append(inv)
                outs.append(nn(expo, v) * inv)
            inv_v[slot] = jnp.where(lane, invs[0], invs[1])
            mixed = jnp.where(lane, outs[0], outs[1])
            mixed_v[:, pl.ds(pl.multiple_of(p * wide, wide), wide)] = mixed
            mix_v[:, pl.ds(pl.multiple_of(p * wide, wide), wide)] = mixed.astype(BF16)
            for copy in e_save(p, slot):
                copy.start()
            return carry

        lax.fori_loop(first, last, step, 0)
        if last == pairs:
            for p in (pairs - 2, pairs - 1):
                for copy in e_save(p, p % 2):
                    copy.wait()

    def attention_out(l):
        copy = load(3, g_out.at[l])
        copy.wait()
        for k in range(WIDTH // CHUNK):
            cols = pl.ds(k * CHUNK, CHUNK)
            acc_v[:, cols] = nn(mix_v[...], weight(3, cols))
        save("mix", mixed_v, s_mix.at[l], save_sem.at[1])
        settle("n0")
        settle("rs0")

        def body(rr, base):
            total = state_v[rr] + acc_v[rr] + ob_ref[l:l + 1]
            value = norm_rows(total, gain1_ref[l:l + 1], b1_ref[l:l + 1], rr, 0)
            normed_v[rr] = value
            xb_v[rr] = value.astype(BF16)
        rows_loop(body)
        save("n0", n_v.at[0], s_n.at[l, 0], save_sem.at[2])
        save("rs0", rs_v.at[0], s_rs.at[l, 0], save_sem.at[3])

    def feed_up(l, i):
        block = rank(i)
        ff_core(l, block).wait_recv()
        base = 2 * (i % 2)
        loads = [load(base + j, g_ff.at[l, block, j]) for j in range(2)]
        loads[0].wait()
        settle(("gp", i % 2))
        for k in range(WIDTH // CHUNK):
            cols = pl.ds(k * CHUNK, CHUNK)
            shift = hb_ref[l:l + 1, pl.ds(pl.multiple_of(block * WIDTH + k * CHUNK, CHUNK), CHUNK)]
            hidden = nn(xb_v[...], weight(base, cols)) + shift
            share = 0.5 + 0.5 * lax.erf(hidden * ROOT_HALF)
            active_v[:, cols] = (hidden * share).astype(BF16)
            slope = share + hidden * (jnp.exp(hidden * hidden * -0.5) * ROOT_TAU)
            gp_v[i % 2, :, cols] = slope.astype(BF16)
        save(("gp", i % 2), gp_v.at[i % 2], s_gp.at[l, block], gp_sem.at[i % 2])
        waiting.append(loads[1])

    def feed_down(l, i):
        base = 2 * (i % 2)
        waiting.pop().wait()
        for k in range(2):
            cols = pl.ds(k * SLOTS, SLOTS)
            value = nt(active_v[...], weight_rows(base + 1, k))
            if i == 0:
                acc_v[:, cols] = value
            else:
                acc_v[:, cols] += value

    def finish(l):
        settle("n1")
        settle("rs1")

        def body(rr, base):
            total = normed_v[rr] + acc_v[rr] + db_ref[l:l + 1]
            value = norm_rows(total, gain2_ref[l:l + 1], b2_ref[l:l + 1], rr, 1)
            state_v[rr] = value
            xb_v[rr] = value.astype(BF16)
        rows_loop(body)
        save("n1", n_v.at[1], s_n.at[l, 1], save_sem.at[4])
        save("rs1", rs_v.at[1], s_rs.at[l, 1], save_sem.at[5])

    greet(near_x, near_y, twin, s, z)
    for l in range(LAYERS):
        for copy in own[l]:
            copy.start()
    tok_copies, tok_own = row_copies(tokens_ref, tok_v, tok_s, tok_r)
    for copy in tok_copies:
        go(copy)
    tok_own.start()
    at_send(0, 1)
    for l in range(LAYERS):
        dn_v[l] = down_ref[l].T
        own_down[l].start()
    at_send(0, 0)
    own[0][2].wait()
    own_down[0].wait()
    ff_send(0)
    ff_spread(0, 0)
    own[1][2].wait()
    own_down[1].wait()
    ff_send(1)
    own[0][0].wait()
    at_pass(0, 0, 0)
    at_pass(0, 0, 1)
    at_send(1, 0)
    ff_spread(0, 1)
    ff_relay(0, 1, 1)
    ff_spread(1, 0)
    own[1][0].wait()
    at_pass(1, 0, 1)
    at_pass(1, 0, 0)
    at_share(0, 0)
    own[0][1].wait()
    at_pass(0, 1, 0)
    ff_cross(0, 0, 1)
    ff_relay(0, 2, 0)
    ff_relay(1, 1, 0)
    ff_cross(0, 1, 1)
    tok_own.wait()
    for copy in tok_copies:
        copy.wait_recv()
    start_state()
    ff_relay(0, 1, 0)
    ff_cross(0, 0, 0)
    at_send(1, 1)
    ff_relay(0, 2, 1)
    ff_relay(0, 3, 1)
    ff_cross(0, 1, 0)
    at_core(0, 0).wait_recv()
    project(0)
    ff_cross(0, 2, 1)
    attend(0, 0, 2)
    ff_cross(0, 2, 0)
    attend(0, 2, 4)
    at_pass(0, 1, 1)
    ff_spread(1, 1)
    attend(0, 4, 6)
    ff_share(0, 0)
    at_share(1, 0)
    ff_cross(0, 3, 1)
    ff_relay(0, 3, 0)
    ff_cross(0, 3, 0)
    at_share(0, 1)
    attend(0, 6, 8)
    ff_cross(1, 0, 1)
    ff_relay(1, 2, 0)
    ff_share(0, 1)
    ff_cross(1, 0, 0)
    at_core(0, 1).wait_recv()
    attention_out(0)
    feed_up(0, 0)
    ff_share(0, 2)
    feed_down(0, 0)
    feed_up(0, 1)
    ff_cross(1, 1, 0)
    ff_relay(1, 2, 1)
    own[1][1].wait()
    at_pass(1, 1, 1)
    ff_relay(1, 1, 1)
    ff_share(0, 3)
    feed_down(0, 1)
    at_pass(1, 1, 0)
    feed_up(0, 2)
    ff_cross(1, 1, 1)
    feed_down(0, 2)
    feed_up(0, 3)
    feed_down(0, 3)
    finish(0)
    ff_relay(1, 3, 0)
    ff_cross(1, 2, 1)
    ff_cross(1, 2, 0)
    at_core(1, 0).wait_recv()
    project(1)
    ff_share(1, 0)
    settle("mix")
    attend(1, 0, 2)
    at_share(1, 1)
    attend(1, 2, 4)
    attend(1, 4, 6)
    ff_relay(1, 3, 1)
    ff_cross(1, 3, 0)
    ff_cross(1, 3, 1)
    attend(1, 6, 8)
    ff_share(1, 1)
    at_core(1, 1).wait_recv()
    attention_out(1)
    feed_up(1, 0)
    ff_share(1, 2)
    feed_down(1, 0)
    feed_up(1, 1)
    cot_copies, cot_own = row_copies(cot_ref, cot_row, cot_s, cot_r)
    for copy in cot_copies:
        go(copy)
    cot_own.start()
    ff_share(1, 3)
    feed_down(1, 1)
    feed_up(1, 2)
    feed_down(1, 2)
    feed_up(1, 3)
    feed_down(1, 3)
    finish(1)
    save("act", xb_v, act_row, save_sem.at[6])
    for key in list(saves):
        settle(key)
    cot_own.wait()
    for copy in cot_copies:
        copy.wait_recv()
    for copy in sent:
        copy.wait_send()
    for l in range(LAYERS):
        ff_drain(l)


def forward(lengths, separators, tokens, cotangent, project_in, project_out, up, down, small):
    shape = jax.ShapeDtypeStruct
    dma = pltpu.SemaphoreType.DMA
    vmem = lambda *dims_type: pltpu.VMEM(dims_type[:-1], dims_type[-1])
    L = LAYERS
    pairs = WIDTH // (2 * HEAD_DIM)
    out_shape = (
        shape((L, 2, 2, 2, QUARTER, 3 * WIDTH), BF16),
        shape((L, 2, 2, 2, QUARTER, WIDTH), BF16),
        shape((L, RING, 2, 2, 2, 2, QUARTER, WIDTH), BF16),
        shape((SLOTS, WIDTH), BF16),
        shape((SLOTS, WIDTH), BF16),
        shape((L, SLOTS, 3 * WIDTH), BF16),
        shape((L, SLOTS, WIDTH), F32),
        shape((L, pairs, 2, SLOTS, SLOTS), BF16),
        shape((L, pairs, SLOTS, 2 * HEAD_DIM), F32),
        shape((L, 2, SLOTS, WIDTH), BF16),
        shape((L, 2, SLOTS, 128), F32),
        shape((L, RING, SLOTS, WIDTH), BF16),
    )
    anywhere = pl.BlockSpec(memory_space=pl.ANY)
    scalar = pl.BlockSpec(memory_space=pltpu.SMEM)
    inside = pl.BlockSpec(memory_space=pltpu.VMEM)
    return pl.pallas_call(
        forward_kernel,
        out_shape=out_shape,
        in_specs=[scalar] * 2 + [anywhere] * 5 + [inside] * (2 + len(small) - 1),
        out_specs=[anywhere] * len(out_shape),
        scratch_shapes=[
            vmem(SLOTS, WIDTH, BF16), vmem(SLOTS, WIDTH, F32), vmem(SLOTS, WIDTH, BF16),
            vmem(SLOTS, 3 * WIDTH, BF16), vmem(SLOTS, WIDTH, BF16), vmem(SLOTS, WIDTH, F32),
            vmem(2, SLOTS, WIDTH, BF16), vmem(2, SLOTS, 128, F32), vmem(SLOTS, WIDTH, F32), vmem(SLOTS, WIDTH, F32),
            vmem(SLOTS, WIDTH, BF16), vmem(2, SLOTS, WIDTH, BF16), vmem(2, 2, SLOTS, SLOTS, BF16),
            vmem(2, SLOTS, 2 * HEAD_DIM, F32), vmem(4, 2, 2, 2, QUARTER, WIDTH, BF16),
            vmem(L, QUARTER, WIDTH, BF16),
            dma((RING,)), dma((RING,)), dma((RING,)), dma((RING,)),
            dma((L, 2, 5)), dma((L, 2, 5)), dma((L, 2)), dma((L, 2)),
            dma((L, RING, 2, 2)), dma((L, RING, 2)), dma((L, RING, 2)), dma((L, RING, 2)),
            dma((L, RING)), dma((L, RING)),
            dma((L, 3)), dma((L,)), dma((4,)), dma((7,)), dma((2, 2)), dma((2,)),
        ],
        compiler_params=pltpu.CompilerParams(
            collective_id=0, has_side_effects=True, vmem_limit_bytes=56 << 20
        ),
        cost_estimate=pl.CostEstimate(flops=30 * 10**9, bytes_accessed=150 << 20, transcendentals=10**7),
    )(lengths, separators, tokens, cotangent, project_in, project_out, up, down, *small)


TOTAL_ROWS = 32


def sum_row(l, kind):
    if l == 0:
        return kind if kind < 2 else 6 + kind
    return 16 + kind


def backward_kernel(
    gain1_ref, gain2_ref,
    w_in, w_out, w_ff, cot_row, act_row, s_qkv, s_mix, s_expo, s_inv, s_n, s_rs, s_gp,
    act_out, grad_out, sums_out,
    g_v, gs_v, acc_v, low_v, gh_v, gm_v, gp_v, gproj_v, out_v, n_v, rs_v, slope_v, qkv_v, mix_v, e_v, inv_v,
    ff_v, wout_v, win_v, part_v, sum_v, got_v, gotz_v,
    a_s, a_r, o_s, o_r, r_s, r_r, z_s, z_r,
    ff_sem, w_sem, n_sem, slope_sem, e_sem, row_sem, own_sem,
):
    s, z, c, x, y = place()
    near_x, near_y, twin = peers(s, z, c, x, y)
    wide = 2 * HEAD_DIM
    pairs = WIDTH // wide
    sent = []

    def remote(src, dst, ss, rs, device):
        return pltpu.make_async_remote_copy(
            src_ref=src, dst_ref=dst, send_sem=ss, recv_sem=rs, device_id=device, device_id_type=MESH
        )

    def go(copy):
        copy.start()
        sent.append(copy)

    def fetch(src, dst, sem):
        return pltpu.make_async_copy(src, dst, sem)

    layers = list(reversed(range(LAYERS)))

    def norm_loads(l):
        return [fetch(s_n.at[l, k], n_v.at[k], n_sem.at[k]) for k in range(2)] + [
            fetch(s_rs.at[l, k], rs_v.at[k], n_sem.at[2 + k]) for k in range(2)
        ]

    def block_loads(l, i):
        slot = i % 2
        return [
            fetch(w_ff.at[l, i, 1], ff_v.at[slot, 1], ff_sem.at[slot, 1]),
            fetch(s_gp.at[l, i], slope_v.at[slot], slope_sem.at[slot]),
            fetch(w_ff.at[l, i, 0], ff_v.at[slot, 0], ff_sem.at[slot, 0]),
        ]

    def out_load(l):
        return fetch(w_out.at[l], wout_v, w_sem.at[0])

    def in_load(l):
        return fetch(w_in.at[l], win_v, w_sem.at[1])

    def row_loads(l):
        return [fetch(s_qkv.at[l], qkv_v, row_sem.at[0]), fetch(s_mix.at[l], mix_v, row_sem.at[1])]

    depth = 4

    def expo_loads(step):
        l, p, slot = LAYERS - 1 - lax.div(step, pairs), lax.rem(step, pairs), lax.rem(step, depth)
        return (
            fetch(s_expo.at[l, p], e_v.at[slot], e_sem.at[slot, 0]),
            fetch(s_inv.at[l, p], inv_v.at[slot], e_sem.at[slot, 1]),
        )

    def start(copies):
        for copy in copies:
            copy.start()

    def wait(copies):
        for copy in copies:
            copy.wait()

    def reduce_stage(which, first, rows, stage):
        here = pl.ds(first, rows)
        if stage > 0 and stage < 4:
            remote(sum_v.at[stage - 1, here], got_v.at[which, stage - 1, here], r_s.at[which, stage - 1],
                   r_r.at[which, stage - 1], twin).wait_recv()
            sum_v[stage, here] = sum_v[stage - 1, here] + got_v[which, stage - 1, here]
        if stage < 3:
            go(remote(sum_v.at[stage, here], got_v.at[which, stage, here], r_s.at[which, stage],
                      r_r.at[which, stage], (twin, near_x, near_y)[stage]))
        elif stage == 3:
            gotz_v[which, z, here] = sum_v[3, here]
            for step in range(1, RING):
                to = lax.rem(z + step, RING)
                go(remote(sum_v.at[3, here], gotz_v.at[which, z, here], z_s.at[which, step], z_r.at[which, step],
                          (s, to)))
        else:
            for step in range(1, RING):
                to = lax.rem(z + step, RING)
                remote(sum_v.at[3, here], gotz_v.at[which, z, here], z_s.at[which, step], z_r.at[which, step],
                       (s, to)).wait_recv()
            total = gotz_v[which, 0, here]
            for k in range(1, RING):
                total = total + gotz_v[which, k, here]
            sums_out[here] = total

    def fold(value):
        total = value[0:8]
        for k in range(1, value.shape[0] // 8):
            total = total + value[8 * k:8 * k + 8]
        return total

    def rows_loop(body, rows=64):
        def step(r, carry):
            body(pl.ds(pl.multiple_of(r * rows, rows), rows))
            return carry
        lax.fori_loop(0, SLOTS // rows, step, 0)

    def put(at, value):
        sum_v[0, pl.ds(at, 1)] = value

    def norm_back(grad, gain, which, rr):
        n = n_v[which, rr].astype(F32)
        u = grad * gain
        mean = jnp.sum(u, -1, keepdims=True) * (1.0 / WIDTH)
        tilt = jnp.sum(u * n, -1, keepdims=True) * (1.0 / WIDTH)
        return (u - mean - n * tilt) * rs_v[which, rr, 0:1]

    def layer_back(l, last):
        row = functools.partial(sum_row, l)
        wait(norm_loads(l)[1::2])
        part_v[...] = jnp.zeros_like(part_v)

        def second(rr):
            grad = g_v[rr]
            part_v[0] += fold(grad)
            out = norm_back(grad, gain2_ref[l:l + 1], 1, rr)
            part_v[1] += fold(out)
            gs_v[rr] = out
            low_v[rr] = out.astype(BF16)
        rows_loop(second)
        put(row(5), jnp.sum(part_v[0], 0, keepdims=True))
        put(row(4), jnp.sum(part_v[1], 0, keepdims=True))

        for i in range(RING):
            slot = i % 2
            loads = block_loads(l, i)
            wait(loads[:2])
            for k in range(WIDTH // CHUNK):
                cols = pl.ds(k * CHUNK, CHUNK)
                value = nn(low_v[...], ff_v[slot, 1, :, cols]) * slope_v[slot, :, cols].astype(F32)
                sum_v[0, pl.ds(row(6 + i), 1), cols] = jnp.sum(value, 0, keepdims=True)
                gh_v[:, cols] = value.astype(BF16)
            loads[2].wait()
            for k in range(2):
                cols = pl.ds(k * SLOTS, SLOTS)
                value = nt(gh_v[...], ff_v[slot, 0, pl.ds(k * SLOTS, SLOTS)])
                if i == 0:
                    acc_v[:, cols] = value
                else:
                    acc_v[:, cols] += value
            if i + 2 < RING:
                start(block_loads(l, i + 2))
            elif not last:
                start(block_loads(l - 1, i - 2))

        wait(norm_loads(l)[0::2])
        part_v[...] = jnp.zeros_like(part_v)

        def first(rr):
            grad = gs_v[rr] + acc_v[rr]
            part_v[0] += fold(grad)
            out = norm_back(grad, gain1_ref[l:l + 1], 0, rr)
            part_v[1] += fold(out)
            gs_v[rr] = out
            low_v[rr] = out.astype(BF16)
        rows_loop(first)
        put(row(3), jnp.sum(part_v[0], 0, keepdims=True))
        put(row(2), jnp.sum(part_v[1], 0, keepdims=True))
        if not last:
            start(norm_loads(l - 1))

        out_load(l).wait()
        for k in range(2):
            gm_v[:, pl.ds(k * SLOTS, SLOTS)] = nt(low_v[...], wout_v[pl.ds(k * SLOTS, SLOTS)]).astype(BF16)
        if not last:
            out_load(l - 1).start()

        wait(row_loads(l))
        lane = lax.broadcasted_iota(jnp.int32, (SLOTS, wide), 1) < HEAD_DIM
        offset = layers.index(l) * pairs

        def attend(p, carry):
            step = offset + p
            slot = lax.rem(step, depth)
            for copy in expo_loads(step):
                copy.wait()
            at = lambda k: pl.ds(pl.multiple_of(k * WIDTH + p * wide, wide), wide)
            q, k, v = qkv_v[:, at(0)], qkv_v[:, at(1)], qkv_v[:, at(2)]
            gm = gm_v[:, at(0)].astype(F32) * inv_v[slot]
            mixed = mix_v[:, at(0)]
            gq, gk, gv = [], [], []
            for h in range(2):
                mine = lane if h == 0 else jnp.logical_not(lane)
                low = jnp.where(mine, gm, 0.0).astype(BF16)
                inner = jnp.sum(low.astype(F32) * mixed, -1, keepdims=True)
                expo = e_v[slot, h]
                gs = (expo.astype(F32) * (nt(low, v) - inner)).astype(BF16)
                gq.append(nn(gs, k))
                gk.append(tn(gs, q))
                gv.append(tn(expo, low))
            gq = (jnp.where(lane, gq[0], gq[1]) * (HEAD_DIM ** -0.5)).astype(BF16)
            gv = (gv[0] + gv[1]).astype(BF16)
            gproj_v[:, at(0)] = gq
            gproj_v[:, at(1)] = jnp.where(lane, gk[0], gk[1]).astype(BF16)
            gproj_v[:, at(2)] = gv
            sum_v[0, pl.ds(row(0), 1), at(0)] = jnp.sum(gq.astype(F32), 0, keepdims=True)
            sum_v[0, pl.ds(row(1), 1), at(0)] = jnp.sum(gv.astype(F32), 0, keepdims=True)

            @pl.when(step + depth < LAYERS * pairs)
            def _():
                for copy in expo_loads(step + depth):
                    copy.start()
            return carry

        if not last:
            lax.fori_loop(0, pairs, attend, 0)
            start(row_loads(l - 1))
            in_load(l).wait()
            for k in range(WIDTH // CHUNK):
                cols = pl.ds(k * CHUNK, CHUNK)
                g_v[:, cols] = gs_v[:, cols] + nt(gproj_v[...], win_v[pl.ds(k * CHUNK, CHUNK)])
            in_load(l - 1).start()
        else:
            reduce_stage(0, 8, TOTAL_ROWS - 8, 0)
            for stage in range(1, 5):
                lax.fori_loop((stage - 1) * 2, stage * 2, attend, 0)
                reduce_stage(0, 8, TOTAL_ROWS - 8, stage)
            reduce_stage(1, 0, 8, 0)
            in_load(l).wait()
            for k in range(WIDTH // CHUNK):
                cols = pl.ds(k * CHUNK, CHUNK)
                out_v[:, cols] = (gs_v[:, cols] + nt(gproj_v[...], win_v[pl.ds(k * CHUNK, CHUNK)])).astype(BF16)
                for step in range(1, RING):
                    go(grad_copy(step, k))
                grad_own(k).start()
                if k > 0:
                    reduce_stage(1, 0, 8, k)

    def part(to):
        return pl.ds(pl.multiple_of(to * QUARTER, QUARTER), QUARTER)

    def act_copy(step):
        to = lax.rem(z + step, RING)
        return remote(act_row.at[part(to)], act_out.at[z], a_s.at[step], a_r.at[step], (s, to))

    def act_own():
        return fetch(act_row.at[part(z)], act_out.at[z], own_sem.at[0])

    def grad_copy(step, k):
        to, cols = lax.rem(z + step, RING), pl.ds(k * CHUNK, CHUNK)
        return remote(out_v.at[part(to), cols], grad_out.at[z, :, cols], o_s.at[step, k], o_r.at[step, k], (s, to))

    def grad_own(k):
        cols = pl.ds(k * CHUNK, CHUNK)
        return fetch(out_v.at[part(z), cols], grad_out.at[z, :, cols], own_sem.at[1 + k])

    top = LAYERS - 1
    cot = fetch(cot_row, out_v, row_sem.at[2])
    cot.start()
    start(norm_loads(top)[1::2])
    start(block_loads(top, 0))
    start(block_loads(top, 1))
    start(norm_loads(top)[0::2])
    out_load(top).start()
    start(row_loads(top))
    for step in range(depth):
        start(expo_loads(jnp.int32(step)))
    in_load(top).start()
    greet(near_x, near_y, twin, s, z)
    for step in range(1, RING):
        go(act_copy(step))
    act_own().start()
    sum_v[0] = jnp.zeros((TOTAL_ROWS, WIDTH), F32)
    cot.wait()

    def widen(rr):
        g_v[rr] = out_v[rr].astype(F32)
    rows_loop(widen)
    for l in layers:
        layer_back(l, l == 0)
    reduce_stage(1, 0, 8, 4)
    act_own().wait()
    for step in range(1, RING):
        act_copy(step).wait_recv()
    for k in range(WIDTH // CHUNK):
        grad_own(k).wait()
        for step in range(1, RING):
            grad_copy(step, k).wait_recv()
    for copy in sent:
        copy.wait_send()


def backward(gains, weights, saved, cot_row, act_row):
    shape = jax.ShapeDtypeStruct
    dma = pltpu.SemaphoreType.DMA
    vmem = lambda *dims_type: pltpu.VMEM(dims_type[:-1], dims_type[-1])
    rows = TOTAL_ROWS
    chunks = WIDTH // CHUNK
    anywhere = pl.BlockSpec(memory_space=pl.ANY)
    inside = pl.BlockSpec(memory_space=pltpu.VMEM)
    return pl.pallas_call(
        backward_kernel,
        out_shape=(
            shape((RING, QUARTER, WIDTH), BF16), shape((RING, QUARTER, WIDTH), BF16), shape((rows, WIDTH), F32),
        ),
        in_specs=[inside] * 2 + [anywhere] * 12,
        out_specs=[anywhere, anywhere, inside],
        scratch_shapes=[
            vmem(SLOTS, WIDTH, F32), vmem(SLOTS, WIDTH, F32), vmem(SLOTS, WIDTH, F32),
            vmem(SLOTS, WIDTH, BF16), vmem(SLOTS, WIDTH, BF16), vmem(SLOTS, WIDTH, BF16), vmem(8, 128, BF16),
            vmem(SLOTS, 3 * WIDTH, BF16), vmem(SLOTS, WIDTH, BF16),
            vmem(2, SLOTS, WIDTH, BF16), vmem(2, SLOTS, 128, F32), vmem(2, SLOTS, WIDTH, BF16),
            vmem(SLOTS, 3 * WIDTH, BF16), vmem(SLOTS, WIDTH, F32),
            vmem(4, 2, SLOTS, SLOTS, BF16), vmem(4, SLOTS, 128, F32),
            vmem(2, 2, WIDTH, WIDTH, BF16), vmem(WIDTH, WIDTH, BF16), vmem(WIDTH, 3 * WIDTH, BF16),
            vmem(2, 8, WIDTH, F32), vmem(4, rows, WIDTH, F32), vmem(2, 3, rows, WIDTH, F32),
            vmem(2, RING, rows, WIDTH, F32),
            dma((RING,)), dma((RING,)), dma((RING, chunks)), dma((RING, chunks)),
            dma((2, 3)), dma((2, 3)), dma((2, RING)), dma((2, RING)),
            dma((2, 2)), dma((2,)), dma((4,)), dma((2,)), dma((4, 2)), dma((3,)), dma((1 + chunks,)),
        ],
        compiler_params=pltpu.CompilerParams(
            collective_id=1, has_side_effects=True, vmem_limit_bytes=60 << 20
        ),
        cost_estimate=pl.CostEstimate(flops=40 * 10**9, bytes_accessed=100 << 20, transcendentals=10**6),
    )(*gains, *weights, cot_row, act_row, *saved)


def whole_rows(
    tokens, lengths, separators, type_table, project_in, project_out, up_weight, down_weight, first_norm_gain,
    second_norm_gain, query_bias, value_bias, output_bias, first_norm_bias, hidden_bias, down_bias,
    second_norm_bias, cotangent,
):
    small = (
        type_table, first_norm_gain, second_norm_gain, query_bias, value_bias, output_bias, first_norm_bias,
        hidden_bias, down_bias, second_norm_bias,
    )
    g_in, g_out, g_ff, cot_row, act_row, *saved = forward(
        lengths, separators, tokens, cotangent, project_in, project_out, up_weight, down_weight, small
    )
    weights = (
        g_in.reshape(LAYERS, WIDTH, 3 * WIDTH),
        g_out.reshape(LAYERS, WIDTH, WIDTH),
        g_ff.reshape(LAYERS, RING, 2, WIDTH, WIDTH),
    )
    activations, grad, sums = backward((first_norm_gain, second_norm_gain), weights, saved, cot_row, act_row)

    def pick(kind, count=1):
        return jnp.stack([sums[sum_row(l, kind):sum_row(l, kind) + count].reshape(-1) for l in range(LAYERS)])

    return (
        activations, grad.astype(F32), pick(0), pick(1), pick(2), pick(3), pick(6, RING), pick(4), pick(5),
    )


def layer_norm(total, gain, bias):
    mean = jnp.mean(total, -1, keepdims=True)
    centered = total - mean
    spread = jnp.mean(centered * centered, -1, keepdims=True)
    return centered * lax.rsqrt(spread + EPS) * gain + bias


def gelu_exact(value):
    return jax.nn.gelu(value, approximate=False)


def contract_last(left, right):
    return lax.dot_general(
        left, right, (((1,), (1,)), ((), ())), preferred_element_type=jnp.float32
    )


def split_heads(block):
    return block.reshape(block.shape[0], -1, HEAD_DIM)


def masked_scores(queries, keys, length):
    scores = jnp.einsum(
        "qhd,khd->hqk", queries, keys, preferred_element_type=jnp.float32
    ) * HEAD_DIM ** (-0.5)
    valid = jnp.arange(keys.shape[0]) < length
    return jnp.where(valid[None, None, :], scores, MASKED)


def attend_forward(packed):
    projected, length = packed
    slots = projected.shape[0]
    queries = split_heads(projected[:, 0])
    keys = split_heads(projected[:, 1])
    values = split_heads(projected[:, 2])
    scores = masked_scores(queries, keys, length)
    peak = jnp.max(scores, -1, keepdims=True)
    expo = jnp.exp(scores - peak)
    total = jnp.sum(expo, -1, keepdims=True)
    probs = (expo / total).astype(jnp.bfloat16)
    mixed = jnp.einsum("hqk,khd->qhd", probs, values, preferred_element_type=jnp.float32)
    return (mixed.astype(jnp.bfloat16).reshape(slots, -1), (peak + jnp.log(total))[:, :, 0])


def attend_backward(packed):
    projected, length, log_total, grad_mixed = packed
    slots = projected.shape[0]
    queries = split_heads(projected[:, 0])
    keys = split_heads(projected[:, 1])
    values = split_heads(projected[:, 2])
    scores = masked_scores(queries, keys, length)
    probs = jnp.exp(scores - log_total[:, :, None])
    grad_out = split_heads(grad_mixed)
    grad_probs = jnp.einsum("qhd,khd->hqk", grad_out, values, preferred_element_type=jnp.float32)
    inner = jnp.sum(grad_probs * probs, -1, keepdims=True)
    grad_scores = (probs * (grad_probs - inner)).astype(jnp.bfloat16)
    scale = HEAD_DIM ** (-0.5)
    grad_queries = (
        jnp.einsum("hqk,khd->qhd", grad_scores, keys, preferred_element_type=jnp.float32) * scale
    )
    grad_keys = (
        jnp.einsum("hqk,qhd->khd", grad_scores, queries, preferred_element_type=jnp.float32) * scale
    )
    grad_values = jnp.einsum(
        "hqk,qhd->khd", probs.astype(jnp.bfloat16), grad_out, preferred_element_type=jnp.float32
    )
    stacked = jnp.stack([grad_queries, grad_keys, grad_values], 1)
    return stacked.reshape(slots, 3, -1).astype(jnp.bfloat16)


def feed_forward(rows, up_part, down_part, bias_part):
    hidden = jnp.dot(rows, up_part, preferred_element_type=jnp.float32) + bias_part
    active = gelu_exact(hidden).astype(jnp.bfloat16)
    return jnp.dot(active, down_part, preferred_element_type=jnp.float32)


def split_heads_plan(
    tokens,
    lengths,
    separators,
    type_table,
    project_in,
    project_out,
    up_weight,
    down_weight,
    first_norm_gain,
    second_norm_gain,
    query_bias,
    value_bias,
    output_bias,
    first_norm_bias,
    hidden_bias,
    down_bias,
    second_norm_bias,
    cotangent,
):
    row_count, slot_part, width = tokens.shape
    token_count = row_count * slot_part
    hidden_part = up_weight.shape[2]
    offset = lax.axis_index("head") * hidden_part
    positions = lax.axis_index("head") * slot_part + jnp.arange(slot_part)
    second = (positions[None, :] > separators[:, None]) & (positions[None, :] < lengths[:, None])
    state = tokens.astype(jnp.float32) + jnp.where(second[:, :, None], type_table[1], type_table[0])
    state = state.reshape(token_count, width)

    def fetch(layer):
        gathered = (
            lax.all_gather(project_in[layer], "seq", axis=0, tiled=True),
            lax.all_gather(project_out[layer], "seq", axis=0, tiled=True),
            lax.all_gather(up_weight[layer], "seq", axis=0, tiled=True),
            lax.all_gather(down_weight[layer], "seq", axis=1, tiled=True),
        )
        return (gathered[0], gathered[1], gathered[2], gathered[3])

    def layer_hidden_bias(layer):
        return lax.dynamic_slice_in_dim(hidden_bias[layer], offset, hidden_part, 0)

    saved = []
    for layer in range(LAYERS):
        weights = fetch(layer)
        inner_in, inner_out, up_part, down_part = weights
        joined = jnp.concatenate(
            [query_bias[layer], jnp.zeros_like(query_bias[layer]), value_bias[layer]]
        )
        projected = (
            jnp.dot(state.astype(jnp.bfloat16), inner_in, preferred_element_type=jnp.float32)
            + joined
        ).astype(jnp.bfloat16)
        heads = lax.all_to_all(
            projected.reshape(row_count, slot_part, 3, width),
            "head",
            split_axis=3,
            concat_axis=1,
            tiled=True,
        )
        mixed, log_total = lax.map(attend_forward, (heads, lengths))
        mixed = lax.all_to_all(mixed, "head", split_axis=1, concat_axis=2, tiled=True).reshape(
            token_count, width
        )
        first_sum = (
            state
            + jnp.dot(mixed, inner_out, preferred_element_type=jnp.float32)
            + output_bias[layer]
        )
        normed = layer_norm(first_sum, first_norm_gain[layer], first_norm_bias[layer])
        normed_low = normed.astype(jnp.bfloat16)
        bias_part = layer_hidden_bias(layer)
        rows_all = lax.all_gather(normed_low[None], "head", axis=0, tiled=True).reshape(-1, width)
        branch_out = lax.psum_scatter(
            feed_forward(rows_all, up_part, down_part, bias_part).astype(jnp.bfloat16),
            "head",
            scatter_dimension=0,
            tiled=True,
        ).astype(jnp.float32)
        second_sum = normed + branch_out + down_bias[layer]
        saved.append((heads, log_total, first_sum, second_sum, rows_all))
        state = layer_norm(second_sum, second_norm_gain[layer], second_norm_bias[layer])
    activations = state.astype(jnp.bfloat16).reshape(row_count, slot_part, width)
    grad = cotangent.astype(jnp.float32).reshape(token_count, width)
    query_grads = [None] * LAYERS
    value_grads = [None] * LAYERS
    output_grads = [None] * LAYERS
    first_grads = [None] * LAYERS
    hidden_grads = [None] * LAYERS
    down_grads = [None] * LAYERS
    second_grads = [None] * LAYERS
    for layer in reversed(range(LAYERS)):
        heads, log_total, first_sum, second_sum, rows_all = saved[layer]
        weights = fetch(layer)
        inner_in, inner_out, up_part, down_part = weights
        second_grads[layer] = jnp.sum(grad, 0)
        _, norm_back = jax.vjp(
            functools.partial(layer_norm, gain=second_norm_gain[layer], bias=second_norm_bias[layer]),
            second_sum,
        )
        grad_second = norm_back(grad)[0]
        down_grads[layer] = jnp.sum(grad_second, 0)
        grad_low = grad_second.astype(jnp.bfloat16)
        bias_part = layer_hidden_bias(layer)
        grad_rows = lax.all_gather(grad_low[None], "head", axis=0, tiled=True).reshape(-1, width)
        hidden = jnp.dot(rows_all, up_part, preferred_element_type=jnp.float32) + bias_part
        grad_active = contract_last(grad_rows, down_part)
        _, gelu_back = jax.vjp(gelu_exact, hidden)
        grad_hidden = gelu_back(grad_active)[0]
        hidden_local = jnp.sum(grad_hidden, 0)
        grad_hidden_low = grad_hidden.astype(jnp.bfloat16)
        hidden_grads[layer] = lax.dynamic_update_slice_in_dim(
            jnp.zeros_like(hidden_bias[layer]), hidden_local, offset, 0
        )
        grad_normed = grad_second + lax.psum_scatter(
            contract_last(grad_hidden_low, up_part).astype(jnp.bfloat16),
            "head",
            scatter_dimension=0,
            tiled=True,
        ).astype(jnp.float32)
        first_grads[layer] = jnp.sum(grad_normed, 0)
        _, norm_back = jax.vjp(
            functools.partial(layer_norm, gain=first_norm_gain[layer], bias=first_norm_bias[layer]), first_sum
        )
        grad_first = norm_back(grad_normed)[0]
        output_grads[layer] = jnp.sum(grad_first, 0)
        grad_mixed = contract_last(grad_first.astype(jnp.bfloat16), inner_out).astype(jnp.bfloat16)
        grad_heads = lax.all_to_all(
            grad_mixed.reshape(row_count, slot_part, width),
            "head",
            split_axis=2,
            concat_axis=1,
            tiled=True,
        )
        grad_projected = lax.map(attend_backward, (heads, lengths, log_total, grad_heads))
        grad_projected = lax.all_to_all(
            grad_projected, "head", split_axis=1, concat_axis=3, tiled=True
        ).reshape(token_count, 3 * width)
        query_grads[layer] = jnp.sum(grad_projected[:, :width], 0, dtype=jnp.float32)
        value_grads[layer] = jnp.sum(grad_projected[:, 2 * width :], 0, dtype=jnp.float32)
        grad = grad_first + contract_last(grad_projected, inner_in)
    summed = lax.psum(
        (
            jnp.stack(query_grads),
            jnp.stack(value_grads),
            jnp.stack(output_grads),
            jnp.stack(first_grads),
            jnp.stack(hidden_grads),
            jnp.stack(down_grads),
            jnp.stack(second_grads),
        ),
        ("seq", "head"),
    )
    input_grad = grad.reshape(row_count, slot_part, width)
    return (
        activations,
        input_grad,
        summed[0],
        summed[1],
        summed[2],
        summed[3],
        summed[4],
        summed[5],
        summed[6],
    )


def solution(mesh):
    placed = (
        P("seq", "head", None),
        P("seq"),
        P("seq"),
        P(),
        P(None, "seq", None),
        P(None, "seq", None),
        P(None, "seq", "head"),
        P(None, "head", "seq"),
        P(),
        P(),
        P(),
        P(),
        P(),
        P(),
        P(),
        P(),
        P(),
        P("seq", "head", None),
    )
    shape = dict(mesh.shape)
    fits = shape == {"seq": 8, "head": RING}
    return jax.shard_map(
        whole_rows if fits else split_heads_plan,
        mesh=mesh,
        in_specs=placed,
        out_specs=(
            P("seq", "head", None),
            P("seq", "head", None),
            P(),
            P(),
            P(),
            P(),
            P(),
            P(),
            P(),
        ),
        check_vma=False,
    )
```

```python
import functools

import jax
import jax.numpy as jnp
from jax import lax
from jax.experimental import pallas as pl
from jax.experimental.pallas import tpu as pltpu
from jax.sharding import PartitionSpec as P

F32 = jnp.float32
BF16 = jnp.bfloat16
MESH = pl.DeviceIdType.MESH
HEAD_DIM = 64
LAYERS = 2
EPS = 1e-06
MASKED = -1000000000.0
ROOT_HALF = 0.7071067811865476
ROOT_TAU = 0.3989422804014327
RING = 4
WIDTH = 1024
SLOTS = 512
QUARTER = SLOTS // RING
CHUNK = 256


def nn(left, right):
    return jnp.dot(left, right, preferred_element_type=F32)


def nt(left, right):
    return lax.dot_general(left, right, (((1,), (1,)), ((), ())), preferred_element_type=F32)


def tn(left, right):
    return lax.dot_general(left, right, (((0,), (0,)), ((), ())), preferred_element_type=F32)


def place():
    s, z = lax.axis_index("seq"), lax.axis_index("head")
    c, x, y = lax.rem(s, 2), lax.rem(lax.div(s, 2), 2), lax.div(s, 4)
    return s, z, c, x, y


def peers(s, z, c, x, y):
    return (s + 2 - 4 * x, z), (s + 4 - 8 * y, z), (s + 1 - 2 * c, z)


def greet(near_x, near_y, twin, s, z):
    barrier = pltpu.get_barrier_semaphore()
    for device in (near_x, near_y, twin):
        pl.semaphore_signal(barrier, inc=1, device_id=device, device_id_type=MESH)
    for step in range(1, RING):
        pl.semaphore_signal(
            barrier, inc=1, device_id=(s, lax.rem(z + step, RING)), device_id_type=MESH
        )
    pl.semaphore_wait(barrier, 3 + RING - 1)


def forward_kernel(
    lengths_ref, separators_ref,
    tokens_ref, cot_ref, in_ref, out_ref, up_ref,
    down_ref, table_ref, gain1_ref, gain2_ref, qb_ref, vb_ref, ob_ref, b1_ref, hb_ref, db_ref, b2_ref,
    g_in, g_out, g_ff, cot_row, act_row, s_qkv, s_mix, s_expo, s_inv, s_n, s_rs, s_gp,
    tok_v, state_v, xb_v, qkv_v, mix_v, mixed_v, n_v, rs_v, normed_v, acc_v, active_v, gp_v, e_v, inv_v, w_v, dn_v, up_v, in_v, out_v, cot_v,
    tok_s, tok_r, cot_s, cot_r, at_s, at_r, ff_s, ff_r, z_s, z_r, f_s, f_r, cc_s, cc_r,
    own_sem, put_sem, w_sem, save_sem, e_sem, gp_sem,
):
    s, z, c, x, y = place()
    near_x, near_y, twin = peers(s, z, c, x, y)
    half = QUARTER // 2
    A, B = pl.ds(0, half), pl.ds(half, half)
    every = slice(None)
    sent = []

    def remote(src, dst, ss, rs, device):
        return pltpu.make_async_remote_copy(
            src_ref=src, dst_ref=dst, send_sem=ss, recv_sem=rs, device_id=device, device_id_type=MESH
        )

    def go(copy):
        copy.start()
        sent.append(copy)

    def own_in(l):
        return [
            pltpu.make_async_copy(ref.at[l], held.at[l], own_sem.at[l, t])
            for t, (ref, held) in enumerate(((up_ref, up_v), (in_ref, in_v), (out_ref, out_v)))
        ]

    def own_out(l):
        places = (
            (up_v, g_ff.at[l, z, 0, y, x, c]), (in_v, g_in.at[l, y, x, c]), (out_v, g_out.at[l, y, x, c]),
            (dn_v, g_ff.at[l, z, 1, y, x, c]),
        )
        return [pltpu.make_async_copy(held.at[l], dst, put_sem.at[l, t]) for t, (held, dst) in enumerate(places)]

    gathered = (g_in, g_out)
    shard = (in_ref, out_ref)

    def at_first(l, t):
        g = gathered[t]
        return (
            remote(shard[t].at[l, A], g.at[l, y, x, c, A], at_s.at[l, t, 0], at_r.at[l, t, 0], near_x),
            remote(shard[t].at[l, B], g.at[l, y, x, c, B], at_s.at[l, t, 1], at_r.at[l, t, 1], near_y),
        )

    def at_last(l, t):
        g = gathered[t]
        pair, pile = g.at[l, y, every, c, A], g.at[l, every, x, c, B]
        return (
            remote(pair, pair, at_s.at[l, t, 2], at_r.at[l, t, 2], near_y),
            remote(pile, pile, at_s.at[l, t, 3], at_r.at[l, t, 3], near_x),
        )

    def at_core(l, t, side):
        part = gathered[t].at[l, every, every, c, (A, B)[side]]
        return remote(part, part, at_s.at[l, t, 4 + side], at_r.at[l, t, 4 + side], twin)

    def at_send(l, t):
        for copy in at_first(l, t):
            go(copy)

    def at_pass(l, t, side):
        at_first(l, t)[side].wait_recv()
        go(at_last(l, t)[side])

    def at_share(l, t, side):
        at_last(l, t)[side].wait_recv()
        go(at_core(l, t, side))

    def at_ready(l, t):
        for side in range(2):
            at_core(l, t, side).wait_recv()

    def rank(i):
        near = z if i == 0 else None
        if i == 0:
            return near
        low = jnp.where(z < 2, z, RING - 1 - z)
        block = (1 - low) if i == 1 else i
        return jnp.where(z < 2, block, RING - 1 - block)

    def ff_part(l, block, side):
        return g_ff.at[l, block, every, y, every, c, A] if side == 0 else g_ff.at[l, block, every, every, x, c, B]

    def ff_first(l):
        a, b = g_ff.at[l, z, every, y, x, c, A], g_ff.at[l, z, every, y, x, c, B]
        return (
            remote(a, a, ff_s.at[l, 0], ff_r.at[l, 0], near_x),
            remote(b, b, ff_s.at[l, 1], ff_r.at[l, 1], near_y),
        )

    def ff_z(l, block, side, way):
        part = ff_part(l, block, side)
        beside = lax.rem(z + 1, RING) if way == 0 else lax.rem(z + RING - 1, RING)
        return remote(part, part, z_s.at[l, block, side, way], z_r.at[l, block, side], (s, beside))

    def ff_last(l, block, side):
        part = ff_part(l, block, side)
        return remote(part, part, f_s.at[l, block, side], f_r.at[l, block, side], near_y if side == 0 else near_x)

    def ff_core(l, block, side):
        part = g_ff.at[l, block, every, every, every, c, (A, B)[side]]
        return remote(part, part, cc_s.at[l, block, side], cc_r.at[l, block, side], twin)

    right = z < RING - 1
    left = z > 0

    def ff_send(l):
        for copy in ff_first(l):
            go(copy)

    def ff_spread(l, side):
        ff_first(l)[side].wait_recv()
        pl.when(right)(ff_z(l, z, side, 0).start)
        pl.when(left)(ff_z(l, z, side, 1).start)

    def ff_cross(l, i, side):
        go(ff_last(l, rank(i), side))

    def ff_relay(l, i, side):
        block = rank(i)
        ff_z(l, block, side, 0).wait_recv()
        pl.when(jnp.logical_and(block < z, right))(ff_z(l, block, side, 0).start)
        pl.when(jnp.logical_and(block > z, left))(ff_z(l, block, side, 1).start)

    def ff_share(l, i, side):
        ff_last(l, rank(i), side).wait_recv()
        go(ff_core(l, rank(i), side))

    def ff_drain(l):
        for side in range(2):
            for block in range(RING):
                goes_right = jnp.logical_and(block <= z, right)
                goes_left = jnp.logical_and(block >= z, left)
                pl.when(goes_right)(ff_z(l, block, side, 0).wait_send)
                pl.when(goes_left)(ff_z(l, block, side, 1).wait_send)

    def row_copies(src, dst, ss, rs):
        here = dst.at[pl.ds(pl.multiple_of(z * QUARTER, QUARTER), QUARTER)]
        copies = []
        for step in range(1, RING):
            to = lax.rem(z + step, RING)
            copies.append(remote(src.at[to], here, ss.at[step], rs.at[step], (s, to)))
        return copies, here

    def load(slot, src, width=WIDTH):
        copy = pltpu.make_async_copy(src, w_v.at[slot], w_sem.at[slot])
        copy.start()
        return copy

    def weight(slot, cols):
        return w_v[slot, :, :, :, :, cols].reshape(WIDTH, CHUNK)

    def weight_rows(slot, half_index):
        return w_v[slot, half_index].reshape(SLOTS, WIDTH)

    saves = {}
    waiting = []

    def save(key, src, dst, sem):
        copy = pltpu.make_async_copy(src, dst, sem)
        copy.start()
        saves[key] = copy

    def settle(key):
        if key in saves:
            saves.pop(key).wait()

    def rows_loop(body, rows=64):
        def step(r, carry):
            body(pl.ds(pl.multiple_of(r * rows, rows), rows), r * rows)
            return carry
        lax.fori_loop(0, SLOTS // rows, step, 0)

    def norm_rows(total, gain, bias, rr, which):
        mean = jnp.sum(total, -1, keepdims=True) * (1.0 / WIDTH)
        centered = total - mean
        rs = lax.rsqrt(jnp.sum(centered * centered, -1, keepdims=True) * (1.0 / WIDTH) + EPS)
        n = centered * rs
        n_v[which, rr] = n.astype(BF16)
        rs_v[which, rr] = rs + jnp.zeros((64, 128), F32)
        return n * gain + bias

    def start_state():
        length, split = lengths_ref[z], separators_ref[z]

        def body(rr, base):
            pos = lax.broadcasted_iota(jnp.int32, (64, 1), 0) + base
            second = jnp.logical_and(pos > split, pos < length)
            kind = jnp.where(second, table_ref[1:2], table_ref[0:1])
            value = tok_v[rr].astype(F32) + kind
            state_v[rr] = value
            xb_v[rr] = value.astype(BF16)
        rows_loop(body)

    def project(l):
        settle("qkv")
        loads = [load(j, g_in.at[l, :, :, :, :, pl.ds(j * WIDTH, WIDTH)]) for j in range(3)]
        for j in range(3):
            loads[j].wait()
            for k in range(WIDTH // CHUNK):
                cols = pl.ds(k * CHUNK, CHUNK)
                value = nn(xb_v[...], weight(j, cols))
                if j == 0:
                    value = (value + qb_ref[l:l + 1, k * CHUNK:(k + 1) * CHUNK]).astype(BF16) * BF16(HEAD_DIM ** -0.5)
                elif j == 2:
                    value = value + vb_ref[l:l + 1, k * CHUNK:(k + 1) * CHUNK]
                qkv_v[:, pl.ds(j * WIDTH + k * CHUNK, CHUNK)] = value.astype(BF16)
        save("qkv", qkv_v, s_qkv.at[l], save_sem.at[0])

    pairs = WIDTH // (2 * HEAD_DIM)
    wide = 2 * HEAD_DIM

    def attend(l, first, last):
        bias = jnp.where(
            lax.broadcasted_iota(jnp.int32, (1, SLOTS), 1) < lengths_ref[z], 0.0, MASKED
        ).astype(F32)
        lane = lax.broadcasted_iota(jnp.int32, (SLOTS, wide), 1) < HEAD_DIM

        def e_save(p, slot):
            return (
                pltpu.make_async_copy(e_v.at[slot], s_expo.at[l, p], e_sem.at[slot, 0]),
                pltpu.make_async_copy(inv_v.at[slot], s_inv.at[l, p], e_sem.at[slot, 1]),
            )

        def step(p, carry):
            slot = lax.rem(p, 2)

            @pl.when(p >= 2)
            def _():
                for copy in e_save(p - 2, slot):
                    copy.wait()

            q = qkv_v[:, pl.ds(pl.multiple_of(p * wide, wide), wide)]
            k = qkv_v[:, pl.ds(pl.multiple_of(WIDTH + p * wide, wide), wide)]
            v = qkv_v[:, pl.ds(pl.multiple_of(2 * WIDTH + p * wide, wide), wide)]
            mine = (jnp.where(lane, q, jnp.zeros_like(q)), jnp.where(lane, jnp.zeros_like(q), q))
            scores = [nt(mine[h], k) + bias for h in range(2)]
            expo = [jnp.exp(part - jnp.max(part, -1, keepdims=True)) for part in scores]
            invs = [1.0 / jnp.sum(part, -1, keepdims=True) for part in expo]
            expo = [part.astype(BF16) for part in expo]
            for h in range(2):
                e_v[slot, h] = expo[h]
            outs = [nn(expo[h], v) * invs[h] for h in range(2)]
            inv_v[slot] = jnp.where(lane, invs[0], invs[1])
            mixed = jnp.where(lane, outs[0], outs[1])
            mixed_v[:, pl.ds(pl.multiple_of(p * wide, wide), wide)] = mixed
            mix_v[:, pl.ds(pl.multiple_of(p * wide, wide), wide)] = mixed.astype(BF16)
            for copy in e_save(p, slot):
                copy.start()
            return carry

        lax.fori_loop(first, last, step, 0)
        if last == pairs:
            for p in (pairs - 2, pairs - 1):
                for copy in e_save(p, p % 2):
                    copy.wait()

    def attention_out(l):
        copy = load(3, g_out.at[l])
        copy.wait()
        for k in range(WIDTH // CHUNK):
            cols = pl.ds(k * CHUNK, CHUNK)
            acc_v[:, cols] = nn(mix_v[...], weight(3, cols))
        settle("mix")
        save("mix", mixed_v, s_mix.at[l], save_sem.at[1])
        settle("n0")
        settle("rs0")

        def body(rr, base):
            total = state_v[rr] + acc_v[rr] + ob_ref[l:l + 1]
            value = norm_rows(total, gain1_ref[l:l + 1], b1_ref[l:l + 1], rr, 0)
            normed_v[rr] = value
            xb_v[rr] = value.astype(BF16)
        rows_loop(body)
        save("n0", n_v.at[0], s_n.at[l, 0], save_sem.at[2])
        save("rs0", rs_v.at[0], s_rs.at[l, 0], save_sem.at[3])

    def feed_up(l, i):
        block = rank(i)
        for side in range(2):
            ff_core(l, block, side).wait_recv()
        base = 2 * (i % 2)
        loads = [load(base + j, g_ff.at[l, block, j]) for j in range(2)]
        loads[0].wait()
        settle(("gp", i % 2))
        for k in range(WIDTH // CHUNK):
            cols = pl.ds(k * CHUNK, CHUNK)
            shift = hb_ref[l:l + 1, pl.ds(pl.multiple_of(block * WIDTH + k * CHUNK, CHUNK), CHUNK)]
            hidden = nn(xb_v[...], weight(base, cols)) + shift
            share = 0.5 + 0.5 * lax.erf(hidden * ROOT_HALF)
            active_v[:, cols] = (hidden * share).astype(BF16)
            slope = share + hidden * (jnp.exp(hidden * hidden * -0.5) * ROOT_TAU)
            gp_v[i % 2, :, cols] = slope.astype(BF16)
        save(("gp", i % 2), gp_v.at[i % 2], s_gp.at[l, block], gp_sem.at[i % 2])
        waiting.append(loads[1])

    def feed_down(l, i):
        base = 2 * (i % 2)
        waiting.pop().wait()
        for k in range(2):
            cols = pl.ds(k * SLOTS, SLOTS)
            value = nt(active_v[...], weight_rows(base + 1, k))
            if i == 0:
                acc_v[:, cols] = value
            else:
                acc_v[:, cols] += value

    def finish(l):
        settle("n1")
        settle("rs1")

        def body(rr, base):
            total = normed_v[rr] + acc_v[rr] + db_ref[l:l + 1]
            value = norm_rows(total, gain2_ref[l:l + 1], b2_ref[l:l + 1], rr, 1)
            state_v[rr] = value
            xb_v[rr] = value.astype(BF16)
        rows_loop(body)
        save("n1", n_v.at[1], s_n.at[l, 1], save_sem.at[4])
        save("rs1", rs_v.at[1], s_rs.at[l, 1], save_sem.at[5])

    greet(near_x, near_y, twin, s, z)
    tok_copies, tok_here = row_copies(tokens_ref, tok_v, tok_s, tok_r)
    for copy in tok_copies:
        go(copy)
    tok_own = pltpu.make_async_copy(tokens_ref.at[z], tok_here, tok_s.at[0])
    tok_own.start()
    at_send(0, 0)
    at_send(0, 1)
    for l in range(LAYERS):
        for copy in own_in(l):
            copy.start()
    cot_in = pltpu.make_async_copy(cot_ref.at[z], cot_v, save_sem.at[7])
    cot_in.start()
    for l in range(LAYERS):
        dn_v[l] = down_ref[l].T
    for l in range(LAYERS):
        for copy in own_in(l):
            copy.wait()
        for copy in own_out(l):
            copy.start()
    cot_in.wait()
    own_out(0)[0].wait()
    own_out(0)[3].wait()
    ff_send(0)
    at_send(1, 0)
    ff_spread(0, 1)
    ff_spread(0, 0)
    ff_cross(0, 0, 0)
    own_out(0)[2].wait()
    at_pass(0, 1, 1)
    own_out(0)[1].wait()
    at_pass(0, 0, 1)
    ff_cross(0, 0, 1)
    ff_relay(0, 1, 1)
    at_pass(0, 0, 0)
    own_out(1)[0].wait()
    own_out(1)[3].wait()
    ff_send(1)
    ff_relay(0, 2, 1)
    at_pass(0, 1, 0)
    ff_relay(0, 1, 0)
    ff_relay(0, 2, 0)
    at_share(0, 1, 1)
    ff_cross(0, 1, 0)
    ff_cross(0, 2, 0)
    ff_cross(0, 2, 1)
    ff_relay(0, 3, 1)
    ff_cross(0, 1, 1)
    tok_own.wait()
    for copy in tok_copies:
        copy.wait_recv()
    start_state()
    at_share(0, 0, 0)
    at_send(1, 1)
    at_share(0, 0, 1)
    ff_spread(1, 0)
    ff_cross(0, 3, 1)
    ff_share(0, 0, 0)
    own_out(1)[1].wait()
    at_pass(1, 0, 0)
    at_ready(0, 0)
    project(0)
    ff_relay(0, 3, 0)
    ff_share(0, 1, 1)
    at_pass(1, 0, 1)
    ff_cross(0, 3, 0)
    ff_relay(1, 1, 0)
    ff_share(0, 2, 0)
    attend(0, 0, 2)
    ff_spread(1, 1)
    own_out(1)[2].wait()
    at_pass(1, 1, 0)
    attend(0, 2, 4)
    ff_share(0, 0, 1)
    at_share(0, 1, 0)
    ff_cross(1, 0, 0)
    attend(0, 4, 6)
    attend(0, 6, 8)
    ff_cross(1, 0, 1)
    ff_share(0, 2, 1)
    at_ready(0, 1)
    attention_out(0)
    at_share(1, 0, 0)
    ff_relay(1, 2, 0)
    ff_cross(1, 2, 0)
    feed_up(0, 0)
    ff_relay(1, 1, 1)
    at_pass(1, 1, 1)
    ff_share(0, 1, 0)
    feed_down(0, 0)
    ff_cross(1, 1, 1)
    feed_up(0, 1)
    ff_share(0, 3, 1)
    feed_down(0, 1)
    ff_share(0, 3, 0)
    ff_cross(1, 1, 0)
    ff_relay(1, 3, 0)
    at_share(1, 0, 1)
    feed_up(0, 2)
    feed_down(0, 2)
    feed_up(0, 3)
    feed_down(0, 3)
    finish(0)
    ff_share(1, 0, 1)
    ff_relay(1, 2, 1)
    ff_cross(1, 3, 0)
    ff_cross(1, 2, 1)
    at_ready(1, 0)
    project(1)
    settle("mix")
    attend(1, 0, 2)
    at_share(1, 1, 1)
    attend(1, 2, 4)
    attend(1, 4, 6)
    ff_relay(1, 3, 1)
    at_share(1, 1, 0)
    ff_share(1, 1, 1)
    ff_cross(1, 3, 1)
    attend(1, 6, 8)
    ff_share(1, 0, 0)
    ff_share(1, 1, 0)
    cot_copies, cot_here = row_copies(cot_ref, cot_row, cot_s, cot_r)
    for copy in cot_copies:
        go(copy)
    cot_own = pltpu.make_async_copy(cot_v, cot_here, cot_s.at[0])
    cot_own.start()
    at_ready(1, 1)
    attention_out(1)
    ff_share(1, 2, 1)
    feed_up(1, 0)
    feed_down(1, 0)
    ff_share(1, 2, 0)
    feed_up(1, 1)
    ff_share(1, 3, 0)
    feed_down(1, 1)
    ff_share(1, 3, 1)
    feed_up(1, 2)
    feed_down(1, 2)
    feed_up(1, 3)
    feed_down(1, 3)
    finish(1)
    save("act", xb_v, act_row, save_sem.at[6])
    for key in list(saves):
        settle(key)
    cot_own.wait()
    for copy in cot_copies:
        copy.wait_recv()
    for copy in sent:
        copy.wait_send()
    for l in range(LAYERS):
        ff_drain(l)


def forward(lengths, separators, tokens, cotangent, project_in, project_out, up, down, small):
    shape = jax.ShapeDtypeStruct
    dma = pltpu.SemaphoreType.DMA
    vmem = lambda *dims_type: pltpu.VMEM(dims_type[:-1], dims_type[-1])
    L = LAYERS
    pairs = WIDTH // (2 * HEAD_DIM)
    out_shape = (
        shape((L, 2, 2, 2, QUARTER, 3 * WIDTH), BF16),
        shape((L, 2, 2, 2, QUARTER, WIDTH), BF16),
        shape((L, RING, 2, 2, 2, 2, QUARTER, WIDTH), BF16),
        shape((SLOTS, WIDTH), BF16),
        shape((SLOTS, WIDTH), BF16),
        shape((L, SLOTS, 3 * WIDTH), BF16),
        shape((L, SLOTS, WIDTH), F32),
        shape((L, pairs, 2, SLOTS, SLOTS), BF16),
        shape((L, pairs, SLOTS, 2 * HEAD_DIM), F32),
        shape((L, 2, SLOTS, WIDTH), BF16),
        shape((L, 2, SLOTS, 128), F32),
        shape((L, RING, SLOTS, WIDTH), BF16),
    )
    anywhere = pl.BlockSpec(memory_space=pl.ANY)
    scalar = pl.BlockSpec(memory_space=pltpu.SMEM)
    inside = pl.BlockSpec(memory_space=pltpu.VMEM)
    return pl.pallas_call(
        forward_kernel,
        out_shape=out_shape,
        in_specs=[scalar] * 2 + [anywhere] * 5 + [inside] * (2 + len(small) - 1),
        out_specs=[anywhere] * len(out_shape),
        scratch_shapes=[
            vmem(SLOTS, WIDTH, BF16), vmem(SLOTS, WIDTH, F32), vmem(SLOTS, WIDTH, BF16),
            vmem(SLOTS, 3 * WIDTH, BF16), vmem(SLOTS, WIDTH, BF16), vmem(SLOTS, WIDTH, F32),
            vmem(2, SLOTS, WIDTH, BF16), vmem(2, SLOTS, 128, F32), vmem(SLOTS, WIDTH, F32), vmem(SLOTS, WIDTH, F32),
            vmem(SLOTS, WIDTH, BF16), vmem(2, SLOTS, WIDTH, BF16), vmem(2, 2, SLOTS, SLOTS, BF16),
            vmem(2, SLOTS, 2 * HEAD_DIM, F32), vmem(4, 2, 2, 2, QUARTER, WIDTH, BF16),
            vmem(L, QUARTER, WIDTH, BF16), vmem(L, QUARTER, WIDTH, BF16), vmem(L, QUARTER, 3 * WIDTH, BF16),
            vmem(L, QUARTER, WIDTH, BF16), vmem(QUARTER, WIDTH, BF16),
            dma((RING,)), dma((RING,)), dma((RING,)), dma((RING,)),
            dma((L, 2, 6)), dma((L, 2, 6)), dma((L, 2)), dma((L, 2)),
            dma((L, RING, 2, 2)), dma((L, RING, 2)), dma((L, RING, 2)), dma((L, RING, 2)),
            dma((L, RING, 2)), dma((L, RING, 2)),
            dma((L, 3)), dma((L, 4)), dma((4,)), dma((8,)), dma((2, 2)), dma((2,)),
        ],
        compiler_params=pltpu.CompilerParams(
            collective_id=0, has_side_effects=True, vmem_limit_bytes=56 << 20
        ),
        cost_estimate=pl.CostEstimate(flops=30 * 10**9, bytes_accessed=150 << 20, transcendentals=10**7),
    )(lengths, separators, tokens, cotangent, project_in, project_out, up, down, *small)


TOTAL_ROWS = 32


def sum_row(l, kind):
    if l == 0:
        return kind if kind < 2 else 6 + kind
    return 16 + kind


def backward_kernel(
    gain1_ref, gain2_ref,
    w_in, w_out, w_ff, cot_row, act_row, s_qkv, s_mix, s_expo, s_inv, s_n, s_rs, s_gp,
    act_out, grad_out, sums_out,
    g_v, gs_v, acc_v, low_v, gh_v, gm_v, gp_v, gproj_v, out_v, n_v, rs_v, slope_v, qkv_v, mix_v, e_v, inv_v,
    ff_v, wout_v, win_v, part_v, sum_v, got_v,
    a_s, a_r, o_s, o_r, r_s, r_r,
    ff_sem, w_sem, n_sem, slope_sem, e_sem, row_sem, own_sem,
):
    s, z, c, x, y = place()
    near_x, near_y, twin = peers(s, z, c, x, y)
    wide = 2 * HEAD_DIM
    pairs = WIDTH // wide
    sent = []

    def remote(src, dst, ss, rs, device):
        return pltpu.make_async_remote_copy(
            src_ref=src, dst_ref=dst, send_sem=ss, recv_sem=rs, device_id=device, device_id_type=MESH
        )

    def go(copy):
        copy.start()
        sent.append(copy)

    def fetch(src, dst, sem):
        return pltpu.make_async_copy(src, dst, sem)

    layers = list(reversed(range(LAYERS)))

    def norm_loads(l):
        return [fetch(s_n.at[l, k], n_v.at[k], n_sem.at[k]) for k in range(2)] + [
            fetch(s_rs.at[l, k], rs_v.at[k], n_sem.at[2 + k]) for k in range(2)
        ]

    def block_loads(l, i):
        slot = i % 2
        return [
            fetch(w_ff.at[l, i, 1], ff_v.at[slot, 1], ff_sem.at[slot, 1]),
            fetch(s_gp.at[l, i], slope_v.at[slot], slope_sem.at[slot]),
            fetch(w_ff.at[l, i, 0], ff_v.at[slot, 0], ff_sem.at[slot, 0]),
        ]

    def out_load(l):
        return fetch(w_out.at[l], wout_v, w_sem.at[0])

    def in_load(l):
        return fetch(w_in.at[l], win_v, w_sem.at[1])

    def row_loads(l):
        return [fetch(s_qkv.at[l], qkv_v, row_sem.at[0]), fetch(s_mix.at[l], mix_v, row_sem.at[1])]

    depth = 4

    def expo_loads(step):
        l, p, slot = LAYERS - 1 - lax.div(step, pairs), lax.rem(step, pairs), lax.rem(step, depth)
        return (
            fetch(s_expo.at[l, p], e_v.at[slot], e_sem.at[slot, 0]),
            fetch(s_inv.at[l, p], inv_v.at[slot], e_sem.at[slot, 1]),
        )

    def start(copies):
        for copy in copies:
            copy.start()

    def wait(copies):
        for copy in copies:
            copy.wait()

    near_z, far_z = (s, z + 1 - 2 * lax.rem(z, 2)), (s, lax.rem(z + 2, RING))
    partners = (near_z, far_z, twin, near_x, near_y)

    early, late, every = pl.ds(8, TOTAL_ROWS - 8), pl.ds(0, 8), pl.ds(0, TOTAL_ROWS)

    def swap(here, stage):
        which = 1 if here is late else 0
        return remote(sum_v.at[stage, here], got_v.at[stage, here], r_s.at[which, stage], r_r.at[which, stage],
                      partners[stage])

    def take(here, stage):
        swap(here, stage).wait_recv()
        sum_v[stage + 1, here] = sum_v[stage, here] + got_v[stage, here]

    def fold(value):
        total = value[0:8]
        for k in range(1, value.shape[0] // 8):
            total = total + value[8 * k:8 * k + 8]
        return total

    def rows_loop(body, rows=64):
        def step(r, carry):
            body(pl.ds(pl.multiple_of(r * rows, rows), rows))
            return carry
        lax.fori_loop(0, SLOTS // rows, step, 0)

    def put(at, value):
        sum_v[0, pl.ds(at, 1)] = value

    def norm_back(grad, gain, which, rr):
        n = n_v[which, rr].astype(F32)
        u = grad * gain
        mean = jnp.sum(u, -1, keepdims=True) * (1.0 / WIDTH)
        tilt = jnp.sum(u * n, -1, keepdims=True) * (1.0 / WIDTH)
        return (u - mean - n * tilt) * rs_v[which, rr, 0:1]

    def layer_back(l, last):
        row = functools.partial(sum_row, l)
        wait(norm_loads(l)[1::2])
        part_v[...] = jnp.zeros_like(part_v)

        def second(rr):
            grad = g_v[rr]
            part_v[0] += fold(grad)
            out = norm_back(grad, gain2_ref[l:l + 1], 1, rr)
            part_v[1] += fold(out)
            gs_v[rr] = out
            low_v[rr] = out.astype(BF16)
        rows_loop(second)
        put(row(5), jnp.sum(part_v[0], 0, keepdims=True))
        put(row(4), jnp.sum(part_v[1], 0, keepdims=True))

        for i in range(RING):
            slot = i % 2
            loads = block_loads(l, i)
            wait(loads[:2])
            for k in range(WIDTH // CHUNK):
                cols = pl.ds(k * CHUNK, CHUNK)
                value = nn(low_v[...], ff_v[slot, 1, :, cols]) * slope_v[slot, :, cols].astype(F32)
                sum_v[0, pl.ds(row(6 + i), 1), cols] = jnp.sum(value, 0, keepdims=True)
                gh_v[:, cols] = value.astype(BF16)
            loads[2].wait()
            for k in range(2):
                cols = pl.ds(k * SLOTS, SLOTS)
                value = nt(gh_v[...], ff_v[slot, 0, pl.ds(k * SLOTS, SLOTS)])
                if i == 0:
                    acc_v[:, cols] = value
                else:
                    acc_v[:, cols] += value
            if i + 2 < RING:
                start(block_loads(l, i + 2))
            elif not last:
                start(block_loads(l - 1, i - 2))

        wait(norm_loads(l)[0::2])
        part_v[...] = jnp.zeros_like(part_v)

        def first(rr):
            grad = gs_v[rr] + acc_v[rr]
            part_v[0] += fold(grad)
            out = norm_back(grad, gain1_ref[l:l + 1], 0, rr)
            part_v[1] += fold(out)
            gs_v[rr] = out
            low_v[rr] = out.astype(BF16)
        rows_loop(first)
        put(row(3), jnp.sum(part_v[0], 0, keepdims=True))
        put(row(2), jnp.sum(part_v[1], 0, keepdims=True))
        if not last:
            start(norm_loads(l - 1))

        out_load(l).wait()
        for k in range(2):
            gm_v[:, pl.ds(k * SLOTS, SLOTS)] = nt(low_v[...], wout_v[pl.ds(k * SLOTS, SLOTS)]).astype(BF16)
        if not last:
            out_load(l - 1).start()

        wait(row_loads(l))
        lane = lax.broadcasted_iota(jnp.int32, (SLOTS, wide), 1) < HEAD_DIM
        offset = layers.index(l) * pairs

        def attend(p, carry):
            step = offset + p
            slot = lax.rem(step, depth)
            for copy in expo_loads(step):
                copy.wait()
            at = lambda k: pl.ds(pl.multiple_of(k * WIDTH + p * wide, wide), wide)
            q, k, v = qkv_v[:, at(0)], qkv_v[:, at(1)], qkv_v[:, at(2)]
            gm = gm_v[:, at(0)].astype(F32) * inv_v[slot]
            mixed = mix_v[:, at(0)]
            mine = (lane, jnp.logical_not(lane))
            low = [jnp.where(m, gm, 0.0).astype(BF16) for m in mine]
            inner = [jnp.sum(part.astype(F32) * mixed, -1, keepdims=True) for part in low]
            gs = [
                (e_v[slot, h].astype(F32) * (nt(low[h], v) - inner[h])).astype(BF16) for h in range(2)
            ]
            both = jnp.concatenate([jnp.where(m, q, jnp.zeros_like(q)) for m in mine], 0)
            gk = tn(jnp.concatenate(gs, 0), both)
            gv = tn(e_v[slot].reshape(2 * SLOTS, SLOTS), jnp.concatenate(low, 0)).astype(BF16)
            gq = (jnp.where(lane, nn(gs[0], k), nn(gs[1], k)) * (HEAD_DIM ** -0.5)).astype(BF16)
            gproj_v[:, at(0)] = gq
            gproj_v[:, at(1)] = gk.astype(BF16)
            gproj_v[:, at(2)] = gv
            sum_v[0, pl.ds(row(0), 1), at(0)] = jnp.sum(gq.astype(F32), 0, keepdims=True)
            sum_v[0, pl.ds(row(1), 1), at(0)] = jnp.sum(gv.astype(F32), 0, keepdims=True)

            @pl.when(step + depth < LAYERS * pairs)
            def _():
                for copy in expo_loads(step + depth):
                    copy.start()
            return carry

        if not last:
            lax.fori_loop(0, pairs, attend, 0)
            start(row_loads(l - 1))
            in_load(l).wait()
            for k in range(WIDTH // CHUNK):
                cols = pl.ds(k * CHUNK, CHUNK)
                g_v[:, cols] = gs_v[:, cols] + nt(gproj_v[...], win_v[pl.ds(k * CHUNK, CHUNK)])
            in_load(l - 1).start()
        else:
            go(swap(early, 0))
            lax.fori_loop(0, pairs // 2, attend, 0)
            take(early, 0)
            go(swap(early, 1))
            lax.fori_loop(pairs // 2, pairs, attend, 0)
            go(swap(late, 0))
            in_load(l).wait()
            for k in range(WIDTH // CHUNK):
                cols = pl.ds(k * CHUNK, CHUNK)
                out_v[:, cols] = (gs_v[:, cols] + nt(gproj_v[...], win_v[pl.ds(k * CHUNK, CHUNK)])).astype(BF16)
                for step in range(1, RING):
                    go(grad_copy(step, k))
                grad_own(k).start()
                if k == 0:
                    take(late, 0)
                    go(swap(late, 1))
            take(early, 1)
            take(late, 1)
            for stage in range(2, 5):
                go(swap(every, stage))
                take(every, stage)
            sums_out[...] = sum_v[5]

    def part(to):
        return pl.ds(pl.multiple_of(to * QUARTER, QUARTER), QUARTER)

    def act_copy(step):
        to = lax.rem(z + step, RING)
        return remote(act_row.at[part(to)], act_out.at[z], a_s.at[step], a_r.at[step], (s, to))

    def act_own():
        held = gm_v.at[pl.ds(0, QUARTER)]
        return fetch(act_row.at[part(z)], held, own_sem.at[0]), fetch(held, act_out.at[z], own_sem.at[0])

    def grad_copy(step, k):
        to, cols = lax.rem(z + step, RING), pl.ds(k * CHUNK, CHUNK)
        return remote(out_v.at[part(to), cols], grad_out.at[z, :, cols], o_s.at[step, k], o_r.at[step, k], (s, to))

    def grad_own(k):
        cols = pl.ds(k * CHUNK, CHUNK)
        return fetch(out_v.at[part(z), cols], grad_out.at[z, :, cols], own_sem.at[1 + k])

    top = LAYERS - 1
    cot = fetch(cot_row, out_v, row_sem.at[2])
    cot.start()
    start(norm_loads(top)[1::2])
    start(block_loads(top, 0))
    start(block_loads(top, 1))
    start(norm_loads(top)[0::2])
    out_load(top).start()
    start(row_loads(top))
    for step in range(depth):
        start(expo_loads(jnp.int32(step)))
    in_load(top).start()
    greet(near_x, near_y, twin, s, z)
    for step in range(1, RING):
        go(act_copy(step))
    act_own()[0].start()
    sum_v[0] = jnp.zeros((TOTAL_ROWS, WIDTH), F32)
    cot.wait()

    def widen(rr):
        g_v[rr] = out_v[rr].astype(F32)
    rows_loop(widen)
    act_own()[0].wait()
    act_own()[1].start()
    act_own()[1].wait()
    for l in layers:
        layer_back(l, l == 0)
    for step in range(1, RING):
        act_copy(step).wait_recv()
    for k in range(WIDTH // CHUNK):
        grad_own(k).wait()
        for step in range(1, RING):
            grad_copy(step, k).wait_recv()
    for copy in sent:
        copy.wait_send()


def backward(gains, weights, saved, cot_row, act_row):
    shape = jax.ShapeDtypeStruct
    dma = pltpu.SemaphoreType.DMA
    vmem = lambda *dims_type: pltpu.VMEM(dims_type[:-1], dims_type[-1])
    rows = TOTAL_ROWS
    chunks = WIDTH // CHUNK
    anywhere = pl.BlockSpec(memory_space=pl.ANY)
    inside = pl.BlockSpec(memory_space=pltpu.VMEM)
    return pl.pallas_call(
        backward_kernel,
        out_shape=(
            shape((RING, QUARTER, WIDTH), BF16), shape((RING, QUARTER, WIDTH), BF16), shape((rows, WIDTH), F32),
        ),
        in_specs=[inside] * 2 + [anywhere] * 12,
        out_specs=[anywhere, anywhere, inside],
        scratch_shapes=[
            vmem(SLOTS, WIDTH, F32), vmem(SLOTS, WIDTH, F32), vmem(SLOTS, WIDTH, F32),
            vmem(SLOTS, WIDTH, BF16), vmem(SLOTS, WIDTH, BF16), vmem(SLOTS, WIDTH, BF16), vmem(8, 128, BF16),
            vmem(SLOTS, 3 * WIDTH, BF16), vmem(SLOTS, WIDTH, BF16),
            vmem(2, SLOTS, WIDTH, BF16), vmem(2, SLOTS, 128, F32), vmem(2, SLOTS, WIDTH, BF16),
            vmem(SLOTS, 3 * WIDTH, BF16), vmem(SLOTS, WIDTH, F32),
            vmem(4, 2, SLOTS, SLOTS, BF16), vmem(4, SLOTS, 128, F32),
            vmem(2, 2, WIDTH, WIDTH, BF16), vmem(WIDTH, WIDTH, BF16), vmem(WIDTH, 3 * WIDTH, BF16),
            vmem(2, 8, WIDTH, F32), vmem(6, rows, WIDTH, F32), vmem(5, rows, WIDTH, F32),
            dma((RING,)), dma((RING,)), dma((RING, chunks)), dma((RING, chunks)),
            dma((2, 5)), dma((2, 5)),
            dma((2, 2)), dma((2,)), dma((4,)), dma((2,)), dma((4, 2)), dma((3,)), dma((1 + chunks,)),
        ],
        compiler_params=pltpu.CompilerParams(
            collective_id=1, has_side_effects=True, vmem_limit_bytes=60 << 20
        ),
        cost_estimate=pl.CostEstimate(flops=40 * 10**9, bytes_accessed=100 << 20, transcendentals=10**6),
    )(*gains, *weights, cot_row, act_row, *saved)


def deliver_kernel(act_ref, grad_ref, sums_ref, act_out, grad_out, *small_outs):
    act_out[...] = act_ref[...]
    grad_out[...] = grad_ref[...].astype(F32)

    @pl.when(pl.program_id(0) == 0)
    def _():
        for out, kind in zip(small_outs, (0, 1, 2, 3, 6, 4, 5)):
            for l in range(LAYERS):
                for k in range(out.shape[1] // WIDTH):
                    at = sum_row(l, kind + k)
                    out[l:l + 1, k * WIDTH:(k + 1) * WIDTH] = sums_ref[at:at + 1]


def deliver(activations, grad, sums):
    shape = jax.ShapeDtypeStruct
    whole = lambda *dims: pl.BlockSpec(dims, lambda i: (0,) * len(dims))
    block = pl.BlockSpec((1, QUARTER, WIDTH), lambda i: (i, 0, 0))
    widths = [WIDTH] * 4 + [RING * WIDTH] + [WIDTH] * 2
    return pl.pallas_call(
        deliver_kernel,
        grid=(RING,),
        out_shape=[shape(grad.shape, BF16), shape(grad.shape, F32)] + [shape((LAYERS, w), F32) for w in widths],
        in_specs=[block, block, whole(TOTAL_ROWS, WIDTH)],
        out_specs=[block, block] + [whole(LAYERS, w) for w in widths],
    )(activations, grad, sums)


def whole_rows(
    tokens, lengths, separators, type_table, project_in, project_out, up_weight, down_weight, first_norm_gain,
    second_norm_gain, query_bias, value_bias, output_bias, first_norm_bias, hidden_bias, down_bias,
    second_norm_bias, cotangent,
):
    small = (
        type_table, first_norm_gain, second_norm_gain, query_bias, value_bias, output_bias, first_norm_bias,
        hidden_bias, down_bias, second_norm_bias,
    )
    g_in, g_out, g_ff, cot_row, act_row, *saved = forward(
        lengths, separators, tokens, cotangent, project_in, project_out, up_weight, down_weight, small
    )
    weights = (
        g_in.reshape(LAYERS, WIDTH, 3 * WIDTH),
        g_out.reshape(LAYERS, WIDTH, WIDTH),
        g_ff.reshape(LAYERS, RING, 2, WIDTH, WIDTH),
    )
    return tuple(deliver(*backward((first_norm_gain, second_norm_gain), weights, saved, cot_row, act_row)))


def layer_norm(total, gain, bias):
    mean = jnp.mean(total, -1, keepdims=True)
    centered = total - mean
    spread = jnp.mean(centered * centered, -1, keepdims=True)
    return centered * lax.rsqrt(spread + EPS) * gain + bias


def gelu_exact(value):
    return jax.nn.gelu(value, approximate=False)


def contract_last(left, right):
    return lax.dot_general(
        left, right, (((1,), (1,)), ((), ())), preferred_element_type=jnp.float32
    )


def split_heads(block):
    return block.reshape(block.shape[0], -1, HEAD_DIM)


def masked_scores(queries, keys, length):
    scores = jnp.einsum(
        "qhd,khd->hqk", queries, keys, preferred_element_type=jnp.float32
    ) * HEAD_DIM ** (-0.5)
    valid = jnp.arange(keys.shape[0]) < length
    return jnp.where(valid[None, None, :], scores, MASKED)


def attend_forward(packed):
    projected, length = packed
    slots = projected.shape[0]
    queries = split_heads(projected[:, 0])
    keys = split_heads(projected[:, 1])
    values = split_heads(projected[:, 2])
    scores = masked_scores(queries, keys, length)
    peak = jnp.max(scores, -1, keepdims=True)
    expo = jnp.exp(scores - peak)
    total = jnp.sum(expo, -1, keepdims=True)
    probs = (expo / total).astype(jnp.bfloat16)
    mixed = jnp.einsum("hqk,khd->qhd", probs, values, preferred_element_type=jnp.float32)
    return (mixed.astype(jnp.bfloat16).reshape(slots, -1), (peak + jnp.log(total))[:, :, 0])


def attend_backward(packed):
    projected, length, log_total, grad_mixed = packed
    slots = projected.shape[0]
    queries = split_heads(projected[:, 0])
    keys = split_heads(projected[:, 1])
    values = split_heads(projected[:, 2])
    scores = masked_scores(queries, keys, length)
    probs = jnp.exp(scores - log_total[:, :, None])
    grad_out = split_heads(grad_mixed)
    grad_probs = jnp.einsum("qhd,khd->hqk", grad_out, values, preferred_element_type=jnp.float32)
    inner = jnp.sum(grad_probs * probs, -1, keepdims=True)
    grad_scores = (probs * (grad_probs - inner)).astype(jnp.bfloat16)
    scale = HEAD_DIM ** (-0.5)
    grad_queries = (
        jnp.einsum("hqk,khd->qhd", grad_scores, keys, preferred_element_type=jnp.float32) * scale
    )
    grad_keys = (
        jnp.einsum("hqk,qhd->khd", grad_scores, queries, preferred_element_type=jnp.float32) * scale
    )
    grad_values = jnp.einsum(
        "hqk,qhd->khd", probs.astype(jnp.bfloat16), grad_out, preferred_element_type=jnp.float32
    )
    stacked = jnp.stack([grad_queries, grad_keys, grad_values], 1)
    return stacked.reshape(slots, 3, -1).astype(jnp.bfloat16)


def feed_forward(rows, up_part, down_part, bias_part):
    hidden = jnp.dot(rows, up_part, preferred_element_type=jnp.float32) + bias_part
    active = gelu_exact(hidden).astype(jnp.bfloat16)
    return jnp.dot(active, down_part, preferred_element_type=jnp.float32)


def split_heads_plan(
    tokens,
    lengths,
    separators,
    type_table,
    project_in,
    project_out,
    up_weight,
    down_weight,
    first_norm_gain,
    second_norm_gain,
    query_bias,
    value_bias,
    output_bias,
    first_norm_bias,
    hidden_bias,
    down_bias,
    second_norm_bias,
    cotangent,
):
    row_count, slot_part, width = tokens.shape
    token_count = row_count * slot_part
    hidden_part = up_weight.shape[2]
    offset = lax.axis_index("head") * hidden_part
    positions = lax.axis_index("head") * slot_part + jnp.arange(slot_part)
    second = (positions[None, :] > separators[:, None]) & (positions[None, :] < lengths[:, None])
    state = tokens.astype(jnp.float32) + jnp.where(second[:, :, None], type_table[1], type_table[0])
    state = state.reshape(token_count, width)

    def fetch(layer):
        gathered = (
            lax.all_gather(project_in[layer], "seq", axis=0, tiled=True),
            lax.all_gather(project_out[layer], "seq", axis=0, tiled=True),
            lax.all_gather(up_weight[layer], "seq", axis=0, tiled=True),
            lax.all_gather(down_weight[layer], "seq", axis=1, tiled=True),
        )
        return (gathered[0], gathered[1], gathered[2], gathered[3])

    def layer_hidden_bias(layer):
        return lax.dynamic_slice_in_dim(hidden_bias[layer], offset, hidden_part, 0)

    saved = []
    for layer in range(LAYERS):
        weights = fetch(layer)
        inner_in, inner_out, up_part, down_part = weights
        joined = jnp.concatenate(
            [query_bias[layer], jnp.zeros_like(query_bias[layer]), value_bias[layer]]
        )
        projected = (
            jnp.dot(state.astype(jnp.bfloat16), inner_in, preferred_element_type=jnp.float32)
            + joined
        ).astype(jnp.bfloat16)
        heads = lax.all_to_all(
            projected.reshape(row_count, slot_part, 3, width),
            "head",
            split_axis=3,
            concat_axis=1,
            tiled=True,
        )
        mixed, log_total = lax.map(attend_forward, (heads, lengths))
        mixed = lax.all_to_all(mixed, "head", split_axis=1, concat_axis=2, tiled=True).reshape(
            token_count, width
        )
        first_sum = (
            state
            + jnp.dot(mixed, inner_out, preferred_element_type=jnp.float32)
            + output_bias[layer]
        )
        normed = layer_norm(first_sum, first_norm_gain[layer], first_norm_bias[layer])
        normed_low = normed.astype(jnp.bfloat16)
        bias_part = layer_hidden_bias(layer)
        rows_all = lax.all_gather(normed_low[None], "head", axis=0, tiled=True).reshape(-1, width)
        branch_out = lax.psum_scatter(
            feed_forward(rows_all, up_part, down_part, bias_part).astype(jnp.bfloat16),
            "head",
            scatter_dimension=0,
            tiled=True,
        ).astype(jnp.float32)
        second_sum = normed + branch_out + down_bias[layer]
        saved.append((heads, log_total, first_sum, second_sum, rows_all))
        state = layer_norm(second_sum, second_norm_gain[layer], second_norm_bias[layer])
    activations = state.astype(jnp.bfloat16).reshape(row_count, slot_part, width)
    grad = cotangent.astype(jnp.float32).reshape(token_count, width)
    query_grads = [None] * LAYERS
    value_grads = [None] * LAYERS
    output_grads = [None] * LAYERS
    first_grads = [None] * LAYERS
    hidden_grads = [None] * LAYERS
    down_grads = [None] * LAYERS
    second_grads = [None] * LAYERS
    for layer in reversed(range(LAYERS)):
        heads, log_total, first_sum, second_sum, rows_all = saved[layer]
        weights = fetch(layer)
        inner_in, inner_out, up_part, down_part = weights
        second_grads[layer] = jnp.sum(grad, 0)
        _, norm_back = jax.vjp(
            functools.partial(layer_norm, gain=second_norm_gain[layer], bias=second_norm_bias[layer]),
            second_sum,
        )
        grad_second = norm_back(grad)[0]
        down_grads[layer] = jnp.sum(grad_second, 0)
        grad_low = grad_second.astype(jnp.bfloat16)
        bias_part = layer_hidden_bias(layer)
        grad_rows = lax.all_gather(grad_low[None], "head", axis=0, tiled=True).reshape(-1, width)
        hidden = jnp.dot(rows_all, up_part, preferred_element_type=jnp.float32) + bias_part
        grad_active = contract_last(grad_rows, down_part)
        _, gelu_back = jax.vjp(gelu_exact, hidden)
        grad_hidden = gelu_back(grad_active)[0]
        hidden_local = jnp.sum(grad_hidden, 0)
        grad_hidden_low = grad_hidden.astype(jnp.bfloat16)
        hidden_grads[layer] = lax.dynamic_update_slice_in_dim(
            jnp.zeros_like(hidden_bias[layer]), hidden_local, offset, 0
        )
        grad_normed = grad_second + lax.psum_scatter(
            contract_last(grad_hidden_low, up_part).astype(jnp.bfloat16),
            "head",
            scatter_dimension=0,
            tiled=True,
        ).astype(jnp.float32)
        first_grads[layer] = jnp.sum(grad_normed, 0)
        _, norm_back = jax.vjp(
            functools.partial(layer_norm, gain=first_norm_gain[layer], bias=first_norm_bias[layer]), first_sum
        )
        grad_first = norm_back(grad_normed)[0]
        output_grads[layer] = jnp.sum(grad_first, 0)
        grad_mixed = contract_last(grad_first.astype(jnp.bfloat16), inner_out).astype(jnp.bfloat16)
        grad_heads = lax.all_to_all(
            grad_mixed.reshape(row_count, slot_part, width),
            "head",
            split_axis=2,
            concat_axis=1,
            tiled=True,
        )
        grad_projected = lax.map(attend_backward, (heads, lengths, log_total, grad_heads))
        grad_projected = lax.all_to_all(
            grad_projected, "head", split_axis=1, concat_axis=3, tiled=True
        ).reshape(token_count, 3 * width)
        query_grads[layer] = jnp.sum(grad_projected[:, :width], 0, dtype=jnp.float32)
        value_grads[layer] = jnp.sum(grad_projected[:, 2 * width :], 0, dtype=jnp.float32)
        grad = grad_first + contract_last(grad_projected, inner_in)
    summed = lax.psum(
        (
            jnp.stack(query_grads),
            jnp.stack(value_grads),
            jnp.stack(output_grads),
            jnp.stack(first_grads),
            jnp.stack(hidden_grads),
            jnp.stack(down_grads),
            jnp.stack(second_grads),
        ),
        ("seq", "head"),
    )
    input_grad = grad.reshape(row_count, slot_part, width)
    return (
        activations,
        input_grad,
        summed[0],
        summed[1],
        summed[2],
        summed[3],
        summed[4],
        summed[5],
        summed[6],
    )


def solution(mesh):
    placed = (
        P("seq", "head", None),
        P("seq"),
        P("seq"),
        P(),
        P(None, "seq", None),
        P(None, "seq", None),
        P(None, "seq", "head"),
        P(None, "head", "seq"),
        P(),
        P(),
        P(),
        P(),
        P(),
        P(),
        P(),
        P(),
        P(),
        P("seq", "head", None),
    )
    shape = dict(mesh.shape)
    fits = shape == {"seq": 8, "head": RING}
    return jax.shard_map(
        whole_rows if fits else split_heads_plan,
        mesh=mesh,
        in_specs=placed,
        out_specs=(
            P("seq", "head", None),
            P("seq", "head", None),
            P(),
            P(),
            P(),
            P(),
            P(),
            P(),
            P(),
        ),
        check_vma=False,
    )
```

```python
import functools

import jax
import jax.numpy as jnp
from jax import lax
from jax.experimental import pallas as pl
from jax.experimental.pallas import tpu as pltpu
from jax.sharding import PartitionSpec as P

F32 = jnp.float32
BF16 = jnp.bfloat16
MESH = pl.DeviceIdType.MESH
HEAD_DIM = 64
LAYERS = 2
EPS = 1e-06
MASKED = -1000000000.0
ROOT_HALF = 0.7071067811865476
ROOT_TAU = 0.3989422804014327
RING = 4
WIDTH = 1024
SLOTS = 512
QUARTER = SLOTS // RING
CHUNK = 256


def nn(left, right):
    return jnp.dot(left, right, preferred_element_type=F32)


def nt(left, right):
    return lax.dot_general(left, right, (((1,), (1,)), ((), ())), preferred_element_type=F32)


def tn(left, right):
    return lax.dot_general(left, right, (((0,), (0,)), ((), ())), preferred_element_type=F32)


def place():
    s, z = lax.axis_index("seq"), lax.axis_index("head")
    c, x, y = lax.rem(s, 2), lax.rem(lax.div(s, 2), 2), lax.div(s, 4)
    return s, z, c, x, y


def peers(s, z, c, x, y):
    return (s + 2 - 4 * x, z), (s + 4 - 8 * y, z), (s + 1 - 2 * c, z)


def greet(near_x, near_y, twin, s, z):
    barrier = pltpu.get_barrier_semaphore()
    for device in [(s, lax.rem(z + step, RING)) for step in (2, 1, 3)] + [near_x, near_y, twin]:
        pl.semaphore_signal(barrier, inc=1, device_id=device, device_id_type=MESH)


def greeted():
    pl.semaphore_wait(pltpu.get_barrier_semaphore(), 3 + RING - 1)


def forward_kernel(
    lengths_ref, separators_ref,
    tokens_ref, cot_ref, in_ref, out_ref, up_ref, down_ref,
    table_in, gain1_in, gain2_in, qb_in, vb_in, ob_in, b1_in, hb_in, db_in, b2_in,
    g_in, g_out, g_ff, cot_row, act_row, s_qkv, s_mix, s_expo, s_inv, s_n, s_rs, s_gp,
    table_ref, gain1_ref, gain2_ref, qb_ref, vb_ref, ob_ref, b1_ref, hb_ref, db_ref, b2_ref, down_v,
    tok_v, state_v, xb_v, qkv_v, mix_v, mixed_v, n_v, rs_v, normed_v, acc_v, active_v, gp_v, e_v, inv_v, w_v, f_v, dn_v, up_v, in_v, out_v, cot_v,
    tok_s, tok_r, cot_s, cot_r, at_s, at_r, ff_s, ff_r, z_s, z_r, f_s, f_r, cc_s, cc_r,
    small_sem, own_sem, put_sem, ld_sem, w_sem, save_sem, e_sem, gp_sem,
):
    s, z, c, x, y = place()
    near_x, near_y, twin = peers(s, z, c, x, y)
    half = QUARTER // 2
    A, B = pl.ds(0, half), pl.ds(half, half)
    every = slice(None)
    sent = []

    def remote(src, dst, ss, rs, device):
        return pltpu.make_async_remote_copy(
            src_ref=src, dst_ref=dst, send_sem=ss, recv_sem=rs, device_id=device, device_id_type=MESH
        )

    def go(copy):
        copy.start()
        sent.append(copy)

    small_in = [
        pltpu.make_async_copy(src, dst, small_sem.at[k]) for k, (src, dst) in enumerate((
            (down_ref, down_v), (table_in, table_ref), (gain1_in, gain1_ref), (gain2_in, gain2_ref),
            (qb_in, qb_ref), (vb_in, vb_ref), (ob_in, ob_ref), (b1_in, b1_ref), (hb_in, hb_ref),
            (db_in, db_ref), (b2_in, b2_ref),
        ))
    ]

    def own_in(l):
        return [
            pltpu.make_async_copy(ref.at[l], held.at[l], own_sem.at[l, t])
            for t, (ref, held) in enumerate(((up_ref, up_v), (in_ref, in_v), (out_ref, out_v)))
        ]

    def own_out(l):
        places = (
            (up_v, g_ff.at[l, z, 0, y, x, c]), (in_v, g_in.at[l, y, x, c]), (out_v, g_out.at[l, y, x, c]),
            (dn_v, g_ff.at[l, z, 1, y, x, c]),
        )
        return [pltpu.make_async_copy(held.at[l], dst, put_sem.at[l, t]) for t, (held, dst) in enumerate(places)]

    gathered = (g_in, g_out)
    shard = (in_ref, out_ref)

    def at_first(l, t):
        g = gathered[t]
        return (
            remote(shard[t].at[l, A], g.at[l, y, x, c, A], at_s.at[l, t, 0], at_r.at[l, t, 0], near_x),
            remote(shard[t].at[l, B], g.at[l, y, x, c, B], at_s.at[l, t, 1], at_r.at[l, t, 1], near_y),
        )

    def at_last(l, t):
        g = gathered[t]
        pair, pile = g.at[l, y, every, c, A], g.at[l, every, x, c, B]
        return (
            remote(pair, pair, at_s.at[l, t, 2], at_r.at[l, t, 2], near_y),
            remote(pile, pile, at_s.at[l, t, 3], at_r.at[l, t, 3], near_x),
        )

    def at_core(l, t, side):
        part = gathered[t].at[l, every, every, c, (A, B)[side]]
        return remote(part, part, at_s.at[l, t, 4 + side], at_r.at[l, t, 4 + side], twin)

    def at_send(l, t):
        for copy in at_first(l, t):
            go(copy)

    def at_pass(l, t, side):
        at_first(l, t)[side].wait_recv()
        go(at_last(l, t)[side])

    def at_share(l, t, side):
        at_last(l, t)[side].wait_recv()
        go(at_core(l, t, side))

    def at_ready(l, t):
        for side in range(2):
            at_core(l, t, side).wait_recv()

    def rank(i):
        near = z if i == 0 else None
        if i == 0:
            return near
        low = jnp.where(z < 2, z, RING - 1 - z)
        block = (1 - low) if i == 1 else i
        return jnp.where(z < 2, block, RING - 1 - block)

    def ff_part(l, block, side, kind):
        return g_ff.at[l, block, kind, y, every, c, A] if side == 0 else g_ff.at[l, block, kind, every, x, c, B]

    def ff_first(l, side, kind):
        part = g_ff.at[l, z, kind, y, x, c, (A, B)[side]]
        return remote(part, part, ff_s.at[l, side, kind], ff_r.at[l, side, kind], (near_x, near_y)[side])

    def ff_z(l, block, side, kind, way):
        part = ff_part(l, block, side, kind)
        beside = lax.rem(z + 1, RING) if way == 0 else lax.rem(z + RING - 1, RING)
        return remote(part, part, z_s.at[way], z_r.at[l, block, side, kind], (s, beside))

    def ff_last(l, block, side, kind):
        part = ff_part(l, block, side, kind)
        return remote(part, part, f_s.at[0], f_r.at[l, block, side, kind], (near_y, near_x)[side])

    def ff_core(l, block, side, kind):
        part = g_ff.at[l, block, kind, every, every, c, (A, B)[side]]
        return remote(part, part, cc_s.at[0], cc_r.at[l, block, side, kind], twin)

    right = z < RING - 1
    left = z > 0

    def ff_send(l):
        for kind in range(2):
            for side in range(2):
                go(ff_first(l, side, kind))

    def ff_spread(l, side, kind):
        ff_first(l, side, kind).wait_recv()
        pl.when(right)(ff_z(l, z, side, kind, 0).start)
        pl.when(left)(ff_z(l, z, side, kind, 1).start)

    def ff_cross(l, i, side, kind):
        ff_last(l, rank(i), side, kind).start()

    def ff_relay(l, i, side, kind):
        block = rank(i)
        ff_z(l, block, side, kind, 0).wait_recv()
        pl.when(jnp.logical_and(block < z, right))(ff_z(l, block, side, kind, 0).start)
        pl.when(jnp.logical_and(block > z, left))(ff_z(l, block, side, kind, 1).start)

    def ff_share(l, i, side, kind):
        ff_last(l, rank(i), side, kind).wait_recv()
        ff_core(l, rank(i), side, kind).start()

    def ff_load(l, i, side, kind, parity):
        part = (every, every, c if parity == 0 else 1 - c, (A, B)[side])
        return pltpu.make_async_copy(
            g_ff.at[(l, rank(i), kind) + part], f_v.at[(kind, i) + part], ld_sem.at[kind, i, side, parity]
        )

    def ff_hold(l, i, side, kind):
        ff_load(l, i, side, kind, 0).start()

    def ff_take(l, i, kind):
        for side in range(2):
            ff_core(l, rank(i), side, kind).wait_recv()
            ff_load(l, i, side, kind, 1).start()

    def ff_held(l, i, kind):
        for side in range(2):
            for parity in range(2):
                ff_load(l, i, side, kind, parity).wait()

    def ff_drain():
        def drain(part, sem):
            remote(part, part, sem, z_r.at[0, 0, 0, 0], twin).wait_send()

        drain(g_ff.at[0, every, 0], f_s.at[0])
        drain(g_ff.at[0], cc_s.at[0])
        for blocks in range(1, RING):
            pl.when(z == blocks - 1)(functools.partial(drain, g_ff.at[0, pl.ds(0, blocks), 0], z_s.at[0]))
            pl.when(z == RING - blocks)(functools.partial(drain, g_ff.at[0, pl.ds(0, blocks), 0], z_s.at[1]))

    def row_copies(src, dst, ss, rs):
        here = dst.at[pl.ds(pl.multiple_of(z * QUARTER, QUARTER), QUARTER)]
        copies = []
        for step in range(1, RING):
            to = lax.rem(z + step, RING)
            copies.append(remote(src.at[to], here, ss.at[step], rs.at[step], (s, to)))
        return copies, here

    def load(slot, src, width=WIDTH):
        copy = pltpu.make_async_copy(src, w_v.at[slot], w_sem.at[slot])
        copy.start()
        return copy

    def weight(slot, cols):
        return w_v[slot, :, :, :, :, cols].reshape(WIDTH, CHUNK)

    saves = {}

    def save(key, src, dst, sem):
        copy = pltpu.make_async_copy(src, dst, sem)
        copy.start()
        saves[key] = copy

    def settle(key):
        if key in saves:
            saves.pop(key).wait()

    def rows_loop(body, rows=64):
        def step(r, carry):
            body(pl.ds(pl.multiple_of(r * rows, rows), rows), r * rows)
            return carry
        lax.fori_loop(0, SLOTS // rows, step, 0)

    def norm_rows(total, gain, bias, rr, which):
        mean = jnp.sum(total, -1, keepdims=True) * (1.0 / WIDTH)
        centered = total - mean
        rs = lax.rsqrt(jnp.sum(centered * centered, -1, keepdims=True) * (1.0 / WIDTH) + EPS)
        n = centered * rs
        n_v[which, rr] = n.astype(BF16)
        rs_v[which, rr] = rs + jnp.zeros((64, 128), F32)
        return n * gain + bias

    def start_state():
        length, split = lengths_ref[z], separators_ref[z]

        def body(rr, base):
            pos = lax.broadcasted_iota(jnp.int32, (64, 1), 0) + base
            second = jnp.logical_and(pos > split, pos < length)
            kind = jnp.where(second, table_ref[1:2], table_ref[0:1])
            value = tok_v[rr].astype(F32) + kind
            state_v[rr] = value
            xb_v[rr] = value.astype(BF16)
        rows_loop(body)

    def project(l):
        settle("qkv")
        loads = [load(j, g_in.at[l, :, :, :, :, pl.ds(j * WIDTH, WIDTH)]) for j in range(3)]
        for j in range(3):
            loads[j].wait()
            for k in range(WIDTH // CHUNK):
                cols = pl.ds(k * CHUNK, CHUNK)
                value = nn(xb_v[...], weight(j, cols))
                if j == 0:
                    value = (value + qb_ref[l:l + 1, k * CHUNK:(k + 1) * CHUNK]).astype(BF16) * BF16(HEAD_DIM ** -0.5)
                elif j == 2:
                    value = value + vb_ref[l:l + 1, k * CHUNK:(k + 1) * CHUNK]
                qkv_v[:, pl.ds(j * WIDTH + k * CHUNK, CHUNK)] = value.astype(BF16)
        save("qkv", qkv_v, s_qkv.at[l], save_sem.at[0])

    pairs = WIDTH // (2 * HEAD_DIM)
    wide = 2 * HEAD_DIM

    def attend(l, first, last):
        bias = jnp.where(
            lax.broadcasted_iota(jnp.int32, (1, SLOTS), 1) < lengths_ref[z], 0.0, MASKED
        ).astype(F32)
        lane = lax.broadcasted_iota(jnp.int32, (SLOTS, wide), 1) < HEAD_DIM

        def e_save(p, slot):
            return (
                pltpu.make_async_copy(e_v.at[slot], s_expo.at[l, p], e_sem.at[slot, 0]),
                pltpu.make_async_copy(inv_v.at[slot], s_inv.at[l, p], e_sem.at[slot, 1]),
            )

        def step(p, carry):
            slot = lax.rem(p, 2)

            @pl.when(p >= 2)
            def _():
                for copy in e_save(p - 2, slot):
                    copy.wait()

            q = qkv_v[:, pl.ds(pl.multiple_of(p * wide, wide), wide)]
            k = qkv_v[:, pl.ds(pl.multiple_of(WIDTH + p * wide, wide), wide)]
            v = qkv_v[:, pl.ds(pl.multiple_of(2 * WIDTH + p * wide, wide), wide)]
            mine = (jnp.where(lane, q, jnp.zeros_like(q)), jnp.where(lane, jnp.zeros_like(q), q))
            scores = [nt(mine[h], k) + bias for h in range(2)]
            expo = [jnp.exp(part - jnp.max(part, -1, keepdims=True)) for part in scores]
            invs = [1.0 / jnp.sum(part, -1, keepdims=True) for part in expo]
            expo = [part.astype(BF16) for part in expo]
            for h in range(2):
                e_v[slot, h] = expo[h]
            outs = [nn(expo[h], v) * invs[h] for h in range(2)]
            inv_v[slot] = jnp.where(lane, invs[0], invs[1])
            mixed = jnp.where(lane, outs[0], outs[1])
            mixed_v[:, pl.ds(pl.multiple_of(p * wide, wide), wide)] = mixed
            mix_v[:, pl.ds(pl.multiple_of(p * wide, wide), wide)] = mixed.astype(BF16)
            for copy in e_save(p, slot):
                copy.start()
            return carry

        lax.fori_loop(first, last, step, 0)
        if last == pairs:
            for p in (pairs - 2, pairs - 1):
                for copy in e_save(p, p % 2):
                    copy.wait()

    def attention_out(l):
        copy = load(3, g_out.at[l])
        copy.wait()
        for k in range(WIDTH // CHUNK):
            cols = pl.ds(k * CHUNK, CHUNK)
            acc_v[:, cols] = nn(mix_v[...], weight(3, cols))
        settle("mix")
        save("mix", mixed_v, s_mix.at[l], save_sem.at[1])
        settle("n0")
        settle("rs0")

        def body(rr, base):
            total = state_v[rr] + acc_v[rr] + ob_ref[l:l + 1]
            value = norm_rows(total, gain1_ref[l:l + 1], b1_ref[l:l + 1], rr, 0)
            normed_v[rr] = value
            xb_v[rr] = value.astype(BF16)
        rows_loop(body)
        save("n0", n_v.at[0], s_n.at[l, 0], save_sem.at[2])
        save("rs0", rs_v.at[0], s_rs.at[l, 0], save_sem.at[3])

    def feed_up(l, i):
        block = rank(i)
        ff_held(l, i, 0)
        settle(("gp", i % 2))
        for k in range(WIDTH // CHUNK):
            cols = pl.ds(k * CHUNK, CHUNK)
            shift = hb_ref[l:l + 1, pl.ds(pl.multiple_of(block * WIDTH + k * CHUNK, CHUNK), CHUNK)]
            hidden = nn(xb_v[...], f_v[0, i, :, :, :, :, cols].reshape(WIDTH, CHUNK)) + shift
            share = 0.5 + 0.5 * lax.erf(hidden * ROOT_HALF)
            active_v[:, cols] = (hidden * share).astype(BF16)
            slope = share + hidden * (jnp.exp(hidden * hidden * -0.5) * ROOT_TAU)
            gp_v[i % 2, :, cols] = slope.astype(BF16)
        save(("gp", i % 2), gp_v.at[i % 2], s_gp.at[l, block], gp_sem.at[i % 2])

    def feed_down(l, i):
        ff_held(l, i, 1)
        for k in range(2):
            cols = pl.ds(k * SLOTS, SLOTS)
            value = nt(active_v[...], f_v[1, i, k].reshape(SLOTS, WIDTH))
            if i == 0:
                acc_v[:, cols] = value
            else:
                acc_v[:, cols] += value

    def finish(l):
        settle("n1")
        settle("rs1")

        def body(rr, base):
            total = normed_v[rr] + acc_v[rr] + db_ref[l:l + 1]
            value = norm_rows(total, gain2_ref[l:l + 1], b2_ref[l:l + 1], rr, 1)
            state_v[rr] = value
            xb_v[rr] = value.astype(BF16)
        rows_loop(body)
        save("n1", n_v.at[1], s_n.at[l, 1], save_sem.at[4])
        save("rs1", rs_v.at[1], s_rs.at[l, 1], save_sem.at[5])

    for l in range(LAYERS):
        for copy in own_in(l):
            copy.start()
    for copy in small_in:
        copy.start()
    cot_in = pltpu.make_async_copy(cot_ref.at[z], cot_v, save_sem.at[7])
    cot_in.start()
    greet(near_x, near_y, twin, s, z)
    small_in[0].wait()
    for l in range(LAYERS):
        dn_v[l] = down_v[l].T
    for l in range(LAYERS):
        for copy in own_in(l):
            copy.wait()
        for copy in own_out(l):
            copy.start()
    greeted()
    at_send(0, 0)
    tok_copies, tok_here = row_copies(tokens_ref, tok_v, tok_s, tok_r)
    for copy in tok_copies:
        go(copy)
    tok_own = pltpu.make_async_copy(tokens_ref.at[z], tok_here, tok_s.at[0])
    tok_own.start()
    own_out(0)[0].wait()
    own_out(0)[3].wait()
    ff_send(0)
    own_out(0)[1].wait()
    at_pass(0, 0, 0)
    at_send(1, 1)
    ff_spread(0, 0, 1)
    at_send(0, 1)
    own_out(1)[0].wait()
    own_out(1)[3].wait()
    ff_send(1)
    at_pass(0, 0, 1)
    ff_spread(0, 1, 1)
    ff_spread(0, 0, 0)
    at_send(1, 0)
    ff_cross(0, 0, 1, 1)
    ff_spread(0, 1, 0)
    ff_relay(0, 2, 0, 1)
    for copy in small_in[1:]:
        copy.wait()
    tok_own.wait()
    for copy in tok_copies:
        copy.wait_recv()
    start_state()
    own_out(0)[2].wait()
    at_pass(0, 1, 0)
    ff_relay(0, 1, 0, 0)
    ff_relay(0, 1, 0, 1)
    at_share(0, 0, 1)
    ff_relay(0, 1, 1, 0)
    ff_cross(0, 1, 0, 1)
    ff_relay(0, 1, 1, 1)
    ff_cross(0, 1, 1, 0)
    ff_cross(0, 2, 0, 1)
    ff_cross(0, 0, 1, 0)
    ff_relay(0, 2, 0, 0)
    ff_cross(0, 2, 0, 0)
    ff_cross(0, 0, 0, 0)
    ff_cross(0, 0, 0, 1)
    at_pass(0, 1, 1)
    ff_relay(0, 2, 1, 1)
    at_share(0, 0, 0)
    ff_relay(0, 2, 1, 0)
    ff_cross(0, 2, 1, 1)
    ff_relay(0, 3, 0, 0)
    ff_relay(0, 3, 0, 1)
    ff_share(0, 2, 0, 0)
    ff_hold(0, 2, 0, 0)
    ff_share(0, 0, 1, 1)
    ff_hold(0, 0, 1, 1)
    ff_cross(0, 1, 1, 1)
    ff_share(0, 1, 1, 0)
    ff_hold(0, 1, 1, 0)
    ff_cross(0, 1, 0, 0)
    ff_relay(0, 3, 1, 0)
    ff_cross(0, 3, 1, 0)
    ff_cross(0, 3, 0, 0)
    ff_share(0, 1, 0, 1)
    ff_hold(0, 1, 0, 1)
    ff_cross(0, 3, 0, 1)
    ff_spread(1, 0, 0)
    at_ready(0, 0)
    project(0)
    ff_cross(0, 2, 1, 0)
    ff_relay(0, 3, 1, 1)
    own_out(1)[1].wait()
    at_pass(1, 0, 1)
    ff_spread(1, 1, 1)
    attend(0, 0, 2)
    ff_share(0, 0, 0, 0)
    ff_hold(0, 0, 0, 0)
    at_pass(1, 0, 0)
    at_share(0, 1, 0)
    at_share(0, 1, 1)
    ff_share(0, 1, 1, 1)
    ff_hold(0, 1, 1, 1)
    ff_share(0, 0, 1, 0)
    ff_hold(0, 0, 1, 0)
    ff_spread(1, 0, 1)
    ff_cross(0, 3, 1, 1)
    ff_relay(1, 1, 0, 0)
    attend(0, 2, 4)
    attend(0, 4, 6)
    ff_cross(1, 0, 0, 0)
    attend(0, 6, 8)
    ff_share(0, 0, 0, 1)
    ff_hold(0, 0, 0, 1)
    ff_share(0, 3, 1, 0)
    ff_hold(0, 3, 1, 0)
    at_ready(0, 1)
    attention_out(0)
    ff_take(0, 0, 0)
    ff_relay(1, 2, 0, 0)
    ff_share(0, 2, 1, 0)
    ff_hold(0, 2, 1, 0)
    ff_share(0, 1, 0, 0)
    ff_hold(0, 1, 0, 0)
    feed_up(0, 0)
    ff_spread(1, 1, 0)
    ff_cross(1, 0, 0, 1)
    ff_share(0, 3, 0, 1)
    ff_hold(0, 3, 0, 1)
    ff_take(0, 2, 0)
    ff_take(0, 1, 0)
    ff_take(0, 1, 1)
    ff_share(0, 2, 0, 1)
    ff_hold(0, 2, 0, 1)
    ff_relay(1, 1, 1, 1)
    ff_cross(1, 0, 1, 1)
    ff_share(0, 3, 0, 0)
    ff_hold(0, 3, 0, 0)
    ff_share(0, 2, 1, 1)
    ff_hold(0, 2, 1, 1)
    ff_take(0, 0, 1)
    feed_down(0, 0)
    ff_cross(1, 0, 1, 0)
    ff_relay(1, 1, 0, 1)
    ff_cross(1, 1, 0, 1)
    ff_relay(1, 2, 0, 1)
    own_out(1)[2].wait()
    at_pass(1, 1, 0)
    ff_take(0, 3, 0)
    feed_up(0, 1)
    at_share(1, 0, 1)
    at_pass(1, 1, 1)
    feed_down(0, 1)
    ff_take(0, 2, 1)
    ff_share(0, 3, 1, 1)
    ff_hold(0, 3, 1, 1)
    ff_cross(1, 1, 0, 0)
    ff_relay(1, 2, 1, 1)
    ff_relay(1, 1, 1, 0)
    ff_cross(1, 1, 1, 1)
    feed_up(0, 2)
    ff_cross(1, 1, 1, 0)
    ff_take(0, 3, 1)
    at_share(1, 0, 0)
    feed_down(0, 2)
    ff_cross(1, 2, 0, 0)
    feed_up(0, 3)
    ff_relay(1, 2, 1, 0)
    ff_share(1, 0, 0, 0)
    ff_hold(1, 0, 0, 0)
    feed_down(0, 3)
    ff_share(1, 0, 1, 1)
    ff_hold(1, 0, 1, 1)
    finish(0)
    ff_share(1, 0, 1, 0)
    ff_hold(1, 0, 1, 0)
    ff_relay(1, 3, 0, 0)
    at_ready(1, 0)
    project(1)
    ff_cross(1, 2, 1, 1)
    ff_relay(1, 3, 1, 0)
    ff_share(1, 1, 0, 1)
    ff_hold(1, 1, 0, 1)
    ff_cross(1, 2, 0, 1)
    settle("mix")
    attend(1, 0, 2)
    at_share(1, 1, 1)
    ff_cross(1, 2, 1, 0)
    ff_share(1, 0, 0, 1)
    ff_hold(1, 0, 0, 1)
    attend(1, 2, 4)
    at_share(1, 1, 0)
    ff_relay(1, 3, 1, 1)
    attend(1, 4, 6)
    ff_share(1, 1, 1, 1)
    ff_hold(1, 1, 1, 1)
    ff_cross(1, 3, 1, 0)
    attend(1, 6, 8)
    ff_relay(1, 3, 0, 1)
    ff_take(1, 0, 0)
    ff_cross(1, 3, 0, 0)
    cot_copies, cot_here = row_copies(cot_ref, cot_row, cot_s, cot_r)
    for copy in cot_copies:
        go(copy)
    cot_in.wait()
    cot_own = pltpu.make_async_copy(cot_v, cot_here, cot_s.at[0])
    cot_own.start()
    ff_share(1, 1, 0, 0)
    ff_hold(1, 1, 0, 0)
    ff_take(1, 0, 1)
    ff_share(1, 2, 0, 0)
    ff_hold(1, 2, 0, 0)
    ff_cross(1, 3, 1, 1)
    ff_take(1, 1, 1)
    ff_cross(1, 3, 0, 1)
    ff_share(1, 1, 1, 0)
    ff_hold(1, 1, 1, 0)
    ff_share(1, 2, 1, 1)
    ff_hold(1, 2, 1, 1)
    at_ready(1, 1)
    attention_out(1)
    feed_up(1, 0)
    ff_share(1, 2, 0, 1)
    ff_hold(1, 2, 0, 1)
    ff_take(1, 1, 0)
    ff_share(1, 2, 1, 0)
    ff_hold(1, 2, 1, 0)
    feed_down(1, 0)
    ff_share(1, 3, 0, 0)
    ff_hold(1, 3, 0, 0)
    ff_share(1, 3, 1, 0)
    ff_hold(1, 3, 1, 0)
    feed_up(1, 1)
    ff_take(1, 2, 0)
    feed_down(1, 1)
    ff_take(1, 2, 1)
    ff_share(1, 3, 0, 1)
    ff_hold(1, 3, 0, 1)
    ff_share(1, 3, 1, 1)
    ff_hold(1, 3, 1, 1)
    feed_up(1, 2)
    ff_take(1, 3, 0)
    feed_down(1, 2)
    ff_take(1, 3, 1)
    feed_up(1, 3)
    feed_down(1, 3)
    finish(1)
    save("act", xb_v, act_row, save_sem.at[6])
    for key in list(saves):
        settle(key)
    cot_own.wait()
    for copy in cot_copies:
        copy.wait_recv()
    for copy in sent:
        copy.wait_send()
    ff_drain()


def forward(lengths, separators, tokens, cotangent, project_in, project_out, up, down, small):
    shape = jax.ShapeDtypeStruct
    dma = pltpu.SemaphoreType.DMA
    vmem = lambda *dims_type: pltpu.VMEM(dims_type[:-1], dims_type[-1])
    L = LAYERS
    pairs = WIDTH // (2 * HEAD_DIM)
    out_shape = (
        shape((L, 2, 2, 2, QUARTER, 3 * WIDTH), BF16),
        shape((L, 2, 2, 2, QUARTER, WIDTH), BF16),
        shape((L, RING, 2, 2, 2, 2, QUARTER, WIDTH), BF16),
        shape((SLOTS, WIDTH), BF16),
        shape((SLOTS, WIDTH), BF16),
        shape((L, SLOTS, 3 * WIDTH), BF16),
        shape((L, SLOTS, WIDTH), F32),
        shape((L, pairs, 2, SLOTS, SLOTS), BF16),
        shape((L, pairs, SLOTS, 2 * HEAD_DIM), F32),
        shape((L, 2, SLOTS, WIDTH), BF16),
        shape((L, 2, SLOTS, 128), F32),
        shape((L, RING, SLOTS, WIDTH), BF16),
    )
    anywhere = pl.BlockSpec(memory_space=pl.ANY)
    scalar = pl.BlockSpec(memory_space=pltpu.SMEM)
    return pl.pallas_call(
        forward_kernel,
        out_shape=out_shape,
        in_specs=[scalar] * 2 + [anywhere] * (6 + len(small)),
        out_specs=[anywhere] * len(out_shape),
        scratch_shapes=[vmem(*a.shape, F32) for a in small] + [
            vmem(*down.shape, BF16), vmem(SLOTS, WIDTH, BF16), vmem(SLOTS, WIDTH, F32), vmem(SLOTS, WIDTH, BF16),
            vmem(SLOTS, 3 * WIDTH, BF16), vmem(SLOTS, WIDTH, BF16), vmem(SLOTS, WIDTH, F32),
            vmem(2, SLOTS, WIDTH, BF16), vmem(2, SLOTS, 128, F32), vmem(SLOTS, WIDTH, F32), vmem(SLOTS, WIDTH, F32),
            vmem(SLOTS, WIDTH, BF16), vmem(2, SLOTS, WIDTH, BF16), vmem(2, 2, SLOTS, SLOTS, BF16),
            vmem(2, SLOTS, 2 * HEAD_DIM, F32), vmem(4, 2, 2, 2, QUARTER, WIDTH, BF16),
            vmem(2, RING, 2, 2, 2, QUARTER, WIDTH, BF16),
            vmem(L, QUARTER, WIDTH, BF16), vmem(L, QUARTER, WIDTH, BF16), vmem(L, QUARTER, 3 * WIDTH, BF16),
            vmem(L, QUARTER, WIDTH, BF16), vmem(QUARTER, WIDTH, BF16),
            dma((RING,)), dma((RING,)), dma((RING,)), dma((RING,)),
            dma((L, 2, 6)), dma((L, 2, 6)), dma((L, 2, 2)), dma((L, 2, 2)),
            dma((2,)), dma((L, RING, 2, 2)), dma((1,)), dma((L, RING, 2, 2)),
            dma((1,)), dma((L, RING, 2, 2)),
            dma((1 + len(small),)), dma((L, 3)), dma((L, 4)), dma((2, RING, 2, 2)), dma((4,)), dma((8,)), dma((2, 2)), dma((2,)),
        ],
        compiler_params=pltpu.CompilerParams(
            collective_id=0, has_side_effects=True, vmem_limit_bytes=60 << 20
        ),
        cost_estimate=pl.CostEstimate(flops=30 * 10**9, bytes_accessed=150 << 20, transcendentals=10**7),
    )(lengths, separators, tokens, cotangent, project_in, project_out, up, down, *small)


TOTAL_ROWS = 32


def sum_row(l, kind):
    if l == 0:
        return kind if kind < 2 else 6 + kind
    return 16 + kind


def backward_kernel(
    gain1_ref, gain2_ref,
    w_in, w_out, w_ff, cot_row, act_row, s_qkv, s_mix, s_expo, s_inv, s_n, s_rs, s_gp,
    act_out, grad_out, sums_out,
    g_v, gs_v, acc_v, low_v, gh_v, gm_v, gp_v, gproj_v, out_v, n_v, rs_v, slope_v, qkv_v, mix_v, e_v, inv_v,
    ff_v, wout_v, win_v, part_v, sum_v, got_v,
    a_s, a_r, o_s, o_r, r_s, r_r,
    ff_sem, w_sem, n_sem, slope_sem, e_sem, row_sem, own_sem,
):
    s, z, c, x, y = place()
    near_x, near_y, twin = peers(s, z, c, x, y)
    wide = 2 * HEAD_DIM
    pairs = WIDTH // wide
    sent = []

    def remote(src, dst, ss, rs, device):
        return pltpu.make_async_remote_copy(
            src_ref=src, dst_ref=dst, send_sem=ss, recv_sem=rs, device_id=device, device_id_type=MESH
        )

    def go(copy):
        copy.start()
        sent.append(copy)

    def fetch(src, dst, sem):
        return pltpu.make_async_copy(src, dst, sem)

    layers = list(reversed(range(LAYERS)))

    def norm_loads(l):
        return [fetch(s_n.at[l, k], n_v.at[k], n_sem.at[k]) for k in range(2)] + [
            fetch(s_rs.at[l, k], rs_v.at[k], n_sem.at[2 + k]) for k in range(2)
        ]

    def block_loads(l, i):
        slot = i % 2
        return [
            fetch(w_ff.at[l, i, 1], ff_v.at[slot, 1], ff_sem.at[slot, 1]),
            fetch(s_gp.at[l, i], slope_v.at[slot], slope_sem.at[slot]),
            fetch(w_ff.at[l, i, 0], ff_v.at[slot, 0], ff_sem.at[slot, 0]),
        ]

    def out_load(l):
        return fetch(w_out.at[l], wout_v, w_sem.at[0])

    def in_load(l):
        return fetch(w_in.at[l], win_v, w_sem.at[1])

    def row_loads(l):
        return [fetch(s_qkv.at[l], qkv_v, row_sem.at[0]), fetch(s_mix.at[l], mix_v, row_sem.at[1])]

    depth = 4

    def expo_loads(step):
        l, p, slot = LAYERS - 1 - lax.div(step, pairs), lax.rem(step, pairs), lax.rem(step, depth)
        return (
            fetch(s_expo.at[l, p], e_v.at[slot], e_sem.at[slot, 0]),
            fetch(s_inv.at[l, p], inv_v.at[slot], e_sem.at[slot, 1]),
        )

    def start(copies):
        for copy in copies:
            copy.start()

    def wait(copies):
        for copy in copies:
            copy.wait()

    near_z, far_z = (s, z + 1 - 2 * lax.rem(z, 2)), (s, lax.rem(z + 2, RING))
    partners = (near_z, far_z, twin, near_x, near_y)

    early, late, every = pl.ds(8, TOTAL_ROWS - 8), pl.ds(0, 8), pl.ds(0, TOTAL_ROWS)

    def swap(here, stage):
        which = 1 if here is late else 0
        return remote(sum_v.at[stage, here], got_v.at[stage, here], r_s.at[which, stage], r_r.at[which, stage],
                      partners[stage])

    def take(here, stage):
        swap(here, stage).wait_recv()
        sum_v[stage + 1, here] = sum_v[stage, here] + got_v[stage, here]

    def fold(value):
        total = value[0:8]
        for k in range(1, value.shape[0] // 8):
            total = total + value[8 * k:8 * k + 8]
        return total

    def rows_loop(body, rows=64):
        def step(r, carry):
            body(pl.ds(pl.multiple_of(r * rows, rows), rows))
            return carry
        lax.fori_loop(0, SLOTS // rows, step, 0)

    def put(at, value):
        sum_v[0, pl.ds(at, 1)] = value

    def norm_back(grad, gain, which, rr):
        n = n_v[which, rr].astype(F32)
        u = grad * gain
        mean = jnp.sum(u, -1, keepdims=True) * (1.0 / WIDTH)
        tilt = jnp.sum(u * n, -1, keepdims=True) * (1.0 / WIDTH)
        return (u - mean - n * tilt) * rs_v[which, rr, 0:1]

    def layer_back(l, last):
        row = functools.partial(sum_row, l)
        wait(norm_loads(l)[1::2])
        part_v[...] = jnp.zeros_like(part_v)

        def second(rr):
            grad = out_v[rr].astype(F32) if l == layers[0] else g_v[rr]
            part_v[0] += fold(grad)
            out = norm_back(grad, gain2_ref[l:l + 1], 1, rr)
            part_v[1] += fold(out)
            gs_v[rr] = out
            low_v[rr] = out.astype(BF16)
        rows_loop(second)
        put(row(5), jnp.sum(part_v[0], 0, keepdims=True))
        put(row(4), jnp.sum(part_v[1], 0, keepdims=True))

        for i in range(RING):
            slot = i % 2
            loads = block_loads(l, i)
            wait(loads[:2])
            for k in range(WIDTH // CHUNK):
                cols = pl.ds(k * CHUNK, CHUNK)
                value = nn(low_v[...], ff_v[slot, 1, :, cols]) * slope_v[slot, :, cols].astype(F32)
                sum_v[0, pl.ds(row(6 + i), 1), cols] = jnp.sum(value, 0, keepdims=True)
                gh_v[:, cols] = value.astype(BF16)
            loads[2].wait()
            for k in range(2):
                cols = pl.ds(k * SLOTS, SLOTS)
                value = nt(gh_v[...], ff_v[slot, 0, pl.ds(k * SLOTS, SLOTS)])
                if i == 0:
                    acc_v[:, cols] = value
                else:
                    acc_v[:, cols] += value
            if i + 2 < RING:
                start(block_loads(l, i + 2))
            if i == 0 and l == layers[0]:
                greeted()
                for step in range(1, RING):
                    go(act_copy(step))
            if i == 1:
                start(norm_loads(l)[0::2])
                out_load(l).start()
            elif i == 2:
                start(row_loads(l))
            elif i == 3 and l == layers[0]:
                for step in range(depth):
                    start(expo_loads(jnp.int32(step)))

        if l == layers[0]:
            act_own()[0].wait()
            act_own()[1].start()
            act_own()[1].wait()
        wait(norm_loads(l)[0::2])
        part_v[...] = jnp.zeros_like(part_v)

        def first(rr):
            grad = gs_v[rr] + acc_v[rr]
            part_v[0] += fold(grad)
            out = norm_back(grad, gain1_ref[l:l + 1], 0, rr)
            part_v[1] += fold(out)
            gs_v[rr] = out
            low_v[rr] = out.astype(BF16)
        rows_loop(first)
        put(row(3), jnp.sum(part_v[0], 0, keepdims=True))
        put(row(2), jnp.sum(part_v[1], 0, keepdims=True))
        in_load(l).start()
        out_load(l).wait()
        for k in range(2):
            gm_v[:, pl.ds(k * SLOTS, SLOTS)] = nt(low_v[...], wout_v[pl.ds(k * SLOTS, SLOTS)]).astype(BF16)
        wait(row_loads(l))
        lane = lax.broadcasted_iota(jnp.int32, (SLOTS, wide), 1) < HEAD_DIM
        offset = layers.index(l) * pairs

        def attend(p, carry):
            step = offset + p
            slot = lax.rem(step, depth)
            for copy in expo_loads(step):
                copy.wait()
            at = lambda k: pl.ds(pl.multiple_of(k * WIDTH + p * wide, wide), wide)
            q, k, v = qkv_v[:, at(0)], qkv_v[:, at(1)], qkv_v[:, at(2)]
            gm = gm_v[:, at(0)].astype(F32) * inv_v[slot]
            mixed = mix_v[:, at(0)]
            mine = (lane, jnp.logical_not(lane))
            low = [jnp.where(m, gm, 0.0).astype(BF16) for m in mine]
            inner = [jnp.sum(part.astype(F32) * mixed, -1, keepdims=True) for part in low]
            gs = [
                (e_v[slot, h].astype(F32) * (nt(low[h], v) - inner[h])).astype(BF16) for h in range(2)
            ]
            both = jnp.concatenate([jnp.where(m, q, jnp.zeros_like(q)) for m in mine], 0)
            gk = tn(jnp.concatenate(gs, 0), both)
            gv = tn(e_v[slot].reshape(2 * SLOTS, SLOTS), jnp.concatenate(low, 0)).astype(BF16)
            gq = (jnp.where(lane, nn(gs[0], k), nn(gs[1], k)) * (HEAD_DIM ** -0.5)).astype(BF16)
            gproj_v[:, at(0)] = gq
            gproj_v[:, at(1)] = gk.astype(BF16)
            gproj_v[:, at(2)] = gv
            sum_v[0, pl.ds(row(0), 1), at(0)] = jnp.sum(gq.astype(F32), 0, keepdims=True)
            sum_v[0, pl.ds(row(1), 1), at(0)] = jnp.sum(gv.astype(F32), 0, keepdims=True)

            @pl.when(step + depth < LAYERS * pairs)
            def _():
                for copy in expo_loads(step + depth):
                    copy.start()
            return carry

        if not last:
            lax.fori_loop(0, pairs // 2, attend, 0)
            start(norm_loads(l - 1)[1::2])
            start(block_loads(l - 1, 0))
            lax.fori_loop(pairs // 2, pairs, attend, 0)
            start(block_loads(l - 1, 1))
            in_load(l).wait()
            for k in range(WIDTH // CHUNK):
                cols = pl.ds(k * CHUNK, CHUNK)
                g_v[:, cols] = gs_v[:, cols] + nt(gproj_v[...], win_v[pl.ds(k * CHUNK, CHUNK)])
        else:
            go(swap(early, 0))
            lax.fori_loop(0, pairs // 2, attend, 0)
            take(early, 0)
            go(swap(early, 1))
            lax.fori_loop(pairs // 2, pairs, attend, 0)
            go(swap(late, 0))
            in_load(l).wait()
            for k in range(WIDTH // CHUNK):
                cols = pl.ds(k * CHUNK, CHUNK)
                out_v[:, cols] = (gs_v[:, cols] + nt(gproj_v[...], win_v[pl.ds(k * CHUNK, CHUNK)])).astype(BF16)
                for step in range(1, RING):
                    grad_copy(step, k).start()
                grad_own(k).start()
                if k == 0:
                    take(late, 0)
                    go(swap(late, 1))
            take(early, 1)
            take(late, 1)
            for stage in range(2, 5):
                go(swap(every, stage))
                take(every, stage)
            sums_out[...] = sum_v[5]

    def part(to):
        return pl.ds(pl.multiple_of(to * QUARTER, QUARTER), QUARTER)

    def act_copy(step):
        to = lax.rem(z + step, RING)
        return remote(act_row.at[part(to)], act_out.at[z], a_s.at[step], a_r.at[step], (s, to))

    def act_own():
        held = gm_v.at[pl.ds(0, QUARTER)]
        return fetch(act_row.at[part(z)], held, own_sem.at[0]), fetch(held, act_out.at[z], own_sem.at[0])

    def grad_copy(step, k):
        to, cols = lax.rem(z + step, RING), pl.ds(k * CHUNK, CHUNK)
        return remote(out_v.at[part(to), cols], grad_out.at[z, :, cols], o_s.at[0], o_r.at[step, k], (s, to))

    def grad_own(k):
        cols = pl.ds(k * CHUNK, CHUNK)
        return fetch(out_v.at[part(z), cols], grad_out.at[z, :, cols], own_sem.at[1 + k])

    top = LAYERS - 1
    cot = fetch(cot_row, out_v, row_sem.at[2])
    cot.start()
    start(norm_loads(top)[1::2])
    start(block_loads(top, 0))
    start(block_loads(top, 1))
    greet(near_x, near_y, twin, s, z)
    act_own()[0].start()
    sum_v[0] = jnp.zeros((TOTAL_ROWS, WIDTH), F32)
    cot.wait()
    for l in layers:
        layer_back(l, l == 0)
    for step in range(1, RING):
        act_copy(step).wait_recv()
    for k in range(WIDTH // CHUNK):
        grad_own(k).wait()
        for step in range(1, RING):
            grad_copy(step, k).wait_recv()
    for copy in sent:
        copy.wait_send()
    whole = out_v.at[pl.ds(0, SLOTS - QUARTER)]
    remote(whole, whole, o_s.at[0], o_r.at[1, 0], twin).wait_send()


def backward(gains, weights, saved, cot_row, act_row):
    shape = jax.ShapeDtypeStruct
    dma = pltpu.SemaphoreType.DMA
    vmem = lambda *dims_type: pltpu.VMEM(dims_type[:-1], dims_type[-1])
    rows = TOTAL_ROWS
    chunks = WIDTH // CHUNK
    anywhere = pl.BlockSpec(memory_space=pl.ANY)
    inside = pl.BlockSpec(memory_space=pltpu.VMEM)
    return pl.pallas_call(
        backward_kernel,
        out_shape=(
            shape((RING, QUARTER, WIDTH), BF16), shape((RING, QUARTER, WIDTH), BF16), shape((rows, WIDTH), F32),
        ),
        in_specs=[inside] * 2 + [anywhere] * 12,
        out_specs=[anywhere, anywhere, inside],
        scratch_shapes=[
            vmem(SLOTS, WIDTH, F32), vmem(SLOTS, WIDTH, F32), vmem(SLOTS, WIDTH, F32),
            vmem(SLOTS, WIDTH, BF16), vmem(SLOTS, WIDTH, BF16), vmem(SLOTS, WIDTH, BF16), vmem(8, 128, BF16),
            vmem(SLOTS, 3 * WIDTH, BF16), vmem(SLOTS, WIDTH, BF16),
            vmem(2, SLOTS, WIDTH, BF16), vmem(2, SLOTS, 128, F32), vmem(2, SLOTS, WIDTH, BF16),
            vmem(SLOTS, 3 * WIDTH, BF16), vmem(SLOTS, WIDTH, F32),
            vmem(4, 2, SLOTS, SLOTS, BF16), vmem(4, SLOTS, 128, F32),
            vmem(2, 2, WIDTH, WIDTH, BF16), vmem(WIDTH, WIDTH, BF16), vmem(WIDTH, 3 * WIDTH, BF16),
            vmem(2, 8, WIDTH, F32), vmem(6, rows, WIDTH, F32), vmem(5, rows, WIDTH, F32),
            dma((RING,)), dma((RING,)), dma((1,)), dma((RING, chunks)),
            dma((2, 5)), dma((2, 5)),
            dma((2, 2)), dma((2,)), dma((4,)), dma((2,)), dma((4, 2)), dma((3,)), dma((1 + chunks,)),
        ],
        compiler_params=pltpu.CompilerParams(
            collective_id=1, has_side_effects=True, vmem_limit_bytes=60 << 20
        ),
        cost_estimate=pl.CostEstimate(flops=40 * 10**9, bytes_accessed=100 << 20, transcendentals=10**6),
    )(*gains, *weights, cot_row, act_row, *saved)


def deliver_kernel(act_ref, grad_ref, sums_ref, act_out, grad_out, *small_outs):
    act_out[...] = act_ref[...]
    grad_out[...] = grad_ref[...].astype(F32)

    @pl.when(pl.program_id(0) == 0)
    def _():
        for out, kind in zip(small_outs, (0, 1, 2, 3, 6, 4, 5)):
            for l in range(LAYERS):
                for k in range(out.shape[1] // WIDTH):
                    at = sum_row(l, kind + k)
                    out[l:l + 1, k * WIDTH:(k + 1) * WIDTH] = sums_ref[at:at + 1]


def deliver(activations, grad, sums):
    shape = jax.ShapeDtypeStruct
    whole = lambda *dims: pl.BlockSpec(dims, lambda i: (0,) * len(dims))
    block = pl.BlockSpec((RING // 2, QUARTER, WIDTH), lambda i: (i, 0, 0))
    widths = [WIDTH] * 4 + [RING * WIDTH] + [WIDTH] * 2
    return pl.pallas_call(
        deliver_kernel,
        grid=(2,),
        out_shape=[shape(grad.shape, BF16), shape(grad.shape, F32)] + [shape((LAYERS, w), F32) for w in widths],
        in_specs=[block, block, whole(TOTAL_ROWS, WIDTH)],
        out_specs=[block, block] + [whole(LAYERS, w) for w in widths],
    )(activations, grad, sums)


def whole_rows(
    tokens, lengths, separators, type_table, project_in, project_out, up_weight, down_weight, first_norm_gain,
    second_norm_gain, query_bias, value_bias, output_bias, first_norm_bias, hidden_bias, down_bias,
    second_norm_bias, cotangent,
):
    small = (
        type_table, first_norm_gain, second_norm_gain, query_bias, value_bias, output_bias, first_norm_bias,
        hidden_bias, down_bias, second_norm_bias,
    )
    g_in, g_out, g_ff, cot_row, act_row, *saved = forward(
        lengths, separators, tokens, cotangent, project_in, project_out, up_weight, down_weight, small
    )
    weights = (
        g_in.reshape(LAYERS, WIDTH, 3 * WIDTH),
        g_out.reshape(LAYERS, WIDTH, WIDTH),
        g_ff.reshape(LAYERS, RING, 2, WIDTH, WIDTH),
    )
    return tuple(deliver(*backward((first_norm_gain, second_norm_gain), weights, saved, cot_row, act_row)))


def layer_norm(total, gain, bias):
    mean = jnp.mean(total, -1, keepdims=True)
    centered = total - mean
    spread = jnp.mean(centered * centered, -1, keepdims=True)
    return centered * lax.rsqrt(spread + EPS) * gain + bias


def gelu_exact(value):
    return jax.nn.gelu(value, approximate=False)


def contract_last(left, right):
    return lax.dot_general(
        left, right, (((1,), (1,)), ((), ())), preferred_element_type=jnp.float32
    )


def split_heads(block):
    return block.reshape(block.shape[0], -1, HEAD_DIM)


def masked_scores(queries, keys, length):
    scores = jnp.einsum(
        "qhd,khd->hqk", queries, keys, preferred_element_type=jnp.float32
    ) * HEAD_DIM ** (-0.5)
    valid = jnp.arange(keys.shape[0]) < length
    return jnp.where(valid[None, None, :], scores, MASKED)


def attend_forward(packed):
    projected, length = packed
    slots = projected.shape[0]
    queries = split_heads(projected[:, 0])
    keys = split_heads(projected[:, 1])
    values = split_heads(projected[:, 2])
    scores = masked_scores(queries, keys, length)
    peak = jnp.max(scores, -1, keepdims=True)
    expo = jnp.exp(scores - peak)
    total = jnp.sum(expo, -1, keepdims=True)
    probs = (expo / total).astype(jnp.bfloat16)
    mixed = jnp.einsum("hqk,khd->qhd", probs, values, preferred_element_type=jnp.float32)
    return (mixed.astype(jnp.bfloat16).reshape(slots, -1), (peak + jnp.log(total))[:, :, 0])


def attend_backward(packed):
    projected, length, log_total, grad_mixed = packed
    slots = projected.shape[0]
    queries = split_heads(projected[:, 0])
    keys = split_heads(projected[:, 1])
    values = split_heads(projected[:, 2])
    scores = masked_scores(queries, keys, length)
    probs = jnp.exp(scores - log_total[:, :, None])
    grad_out = split_heads(grad_mixed)
    grad_probs = jnp.einsum("qhd,khd->hqk", grad_out, values, preferred_element_type=jnp.float32)
    inner = jnp.sum(grad_probs * probs, -1, keepdims=True)
    grad_scores = (probs * (grad_probs - inner)).astype(jnp.bfloat16)
    scale = HEAD_DIM ** (-0.5)
    grad_queries = (
        jnp.einsum("hqk,khd->qhd", grad_scores, keys, preferred_element_type=jnp.float32) * scale
    )
    grad_keys = (
        jnp.einsum("hqk,qhd->khd", grad_scores, queries, preferred_element_type=jnp.float32) * scale
    )
    grad_values = jnp.einsum(
        "hqk,qhd->khd", probs.astype(jnp.bfloat16), grad_out, preferred_element_type=jnp.float32
    )
    stacked = jnp.stack([grad_queries, grad_keys, grad_values], 1)
    return stacked.reshape(slots, 3, -1).astype(jnp.bfloat16)


def feed_forward(rows, up_part, down_part, bias_part):
    hidden = jnp.dot(rows, up_part, preferred_element_type=jnp.float32) + bias_part
    active = gelu_exact(hidden).astype(jnp.bfloat16)
    return jnp.dot(active, down_part, preferred_element_type=jnp.float32)


def split_heads_plan(
    tokens,
    lengths,
    separators,
    type_table,
    project_in,
    project_out,
    up_weight,
    down_weight,
    first_norm_gain,
    second_norm_gain,
    query_bias,
    value_bias,
    output_bias,
    first_norm_bias,
    hidden_bias,
    down_bias,
    second_norm_bias,
    cotangent,
):
    row_count, slot_part, width = tokens.shape
    token_count = row_count * slot_part
    hidden_part = up_weight.shape[2]
    offset = lax.axis_index("head") * hidden_part
    positions = lax.axis_index("head") * slot_part + jnp.arange(slot_part)
    second = (positions[None, :] > separators[:, None]) & (positions[None, :] < lengths[:, None])
    state = tokens.astype(jnp.float32) + jnp.where(second[:, :, None], type_table[1], type_table[0])
    state = state.reshape(token_count, width)

    def fetch(layer):
        gathered = (
            lax.all_gather(project_in[layer], "seq", axis=0, tiled=True),
            lax.all_gather(project_out[layer], "seq", axis=0, tiled=True),
            lax.all_gather(up_weight[layer], "seq", axis=0, tiled=True),
            lax.all_gather(down_weight[layer], "seq", axis=1, tiled=True),
        )
        return (gathered[0], gathered[1], gathered[2], gathered[3])

    def layer_hidden_bias(layer):
        return lax.dynamic_slice_in_dim(hidden_bias[layer], offset, hidden_part, 0)

    saved = []
    for layer in range(LAYERS):
        weights = fetch(layer)
        inner_in, inner_out, up_part, down_part = weights
        joined = jnp.concatenate(
            [query_bias[layer], jnp.zeros_like(query_bias[layer]), value_bias[layer]]
        )
        projected = (
            jnp.dot(state.astype(jnp.bfloat16), inner_in, preferred_element_type=jnp.float32)
            + joined
        ).astype(jnp.bfloat16)
        heads = lax.all_to_all(
            projected.reshape(row_count, slot_part, 3, width),
            "head",
            split_axis=3,
            concat_axis=1,
            tiled=True,
        )
        mixed, log_total = lax.map(attend_forward, (heads, lengths))
        mixed = lax.all_to_all(mixed, "head", split_axis=1, concat_axis=2, tiled=True).reshape(
            token_count, width
        )
        first_sum = (
            state
            + jnp.dot(mixed, inner_out, preferred_element_type=jnp.float32)
            + output_bias[layer]
        )
        normed = layer_norm(first_sum, first_norm_gain[layer], first_norm_bias[layer])
        normed_low = normed.astype(jnp.bfloat16)
        bias_part = layer_hidden_bias(layer)
        rows_all = lax.all_gather(normed_low[None], "head", axis=0, tiled=True).reshape(-1, width)
        branch_out = lax.psum_scatter(
            feed_forward(rows_all, up_part, down_part, bias_part).astype(jnp.bfloat16),
            "head",
            scatter_dimension=0,
            tiled=True,
        ).astype(jnp.float32)
        second_sum = normed + branch_out + down_bias[layer]
        saved.append((heads, log_total, first_sum, second_sum, rows_all))
        state = layer_norm(second_sum, second_norm_gain[layer], second_norm_bias[layer])
    activations = state.astype(jnp.bfloat16).reshape(row_count, slot_part, width)
    grad = cotangent.astype(jnp.float32).reshape(token_count, width)
    query_grads = [None] * LAYERS
    value_grads = [None] * LAYERS
    output_grads = [None] * LAYERS
    first_grads = [None] * LAYERS
    hidden_grads = [None] * LAYERS
    down_grads = [None] * LAYERS
    second_grads = [None] * LAYERS
    for layer in reversed(range(LAYERS)):
        heads, log_total, first_sum, second_sum, rows_all = saved[layer]
        weights = fetch(layer)
        inner_in, inner_out, up_part, down_part = weights
        second_grads[layer] = jnp.sum(grad, 0)
        _, norm_back = jax.vjp(
            functools.partial(layer_norm, gain=second_norm_gain[layer], bias=second_norm_bias[layer]),
            second_sum,
        )
        grad_second = norm_back(grad)[0]
        down_grads[layer] = jnp.sum(grad_second, 0)
        grad_low = grad_second.astype(jnp.bfloat16)
        bias_part = layer_hidden_bias(layer)
        grad_rows = lax.all_gather(grad_low[None], "head", axis=0, tiled=True).reshape(-1, width)
        hidden = jnp.dot(rows_all, up_part, preferred_element_type=jnp.float32) + bias_part
        grad_active = contract_last(grad_rows, down_part)
        _, gelu_back = jax.vjp(gelu_exact, hidden)
        grad_hidden = gelu_back(grad_active)[0]
        hidden_local = jnp.sum(grad_hidden, 0)
        grad_hidden_low = grad_hidden.astype(jnp.bfloat16)
        hidden_grads[layer] = lax.dynamic_update_slice_in_dim(
            jnp.zeros_like(hidden_bias[layer]), hidden_local, offset, 0
        )
        grad_normed = grad_second + lax.psum_scatter(
            contract_last(grad_hidden_low, up_part).astype(jnp.bfloat16),
            "head",
            scatter_dimension=0,
            tiled=True,
        ).astype(jnp.float32)
        first_grads[layer] = jnp.sum(grad_normed, 0)
        _, norm_back = jax.vjp(
            functools.partial(layer_norm, gain=first_norm_gain[layer], bias=first_norm_bias[layer]), first_sum
        )
        grad_first = norm_back(grad_normed)[0]
        output_grads[layer] = jnp.sum(grad_first, 0)
        grad_mixed = contract_last(grad_first.astype(jnp.bfloat16), inner_out).astype(jnp.bfloat16)
        grad_heads = lax.all_to_all(
            grad_mixed.reshape(row_count, slot_part, width),
            "head",
            split_axis=2,
            concat_axis=1,
            tiled=True,
        )
        grad_projected = lax.map(attend_backward, (heads, lengths, log_total, grad_heads))
        grad_projected = lax.all_to_all(
            grad_projected, "head", split_axis=1, concat_axis=3, tiled=True
        ).reshape(token_count, 3 * width)
        query_grads[layer] = jnp.sum(grad_projected[:, :width], 0, dtype=jnp.float32)
        value_grads[layer] = jnp.sum(grad_projected[:, 2 * width :], 0, dtype=jnp.float32)
        grad = grad_first + contract_last(grad_projected, inner_in)
    summed = lax.psum(
        (
            jnp.stack(query_grads),
            jnp.stack(value_grads),
            jnp.stack(output_grads),
            jnp.stack(first_grads),
            jnp.stack(hidden_grads),
            jnp.stack(down_grads),
            jnp.stack(second_grads),
        ),
        ("seq", "head"),
    )
    input_grad = grad.reshape(row_count, slot_part, width)
    return (
        activations,
        input_grad,
        summed[0],
        summed[1],
        summed[2],
        summed[3],
        summed[4],
        summed[5],
        summed[6],
    )


def solution(mesh):
    placed = (
        P("seq", "head", None),
        P("seq"),
        P("seq"),
        P(),
        P(None, "seq", None),
        P(None, "seq", None),
        P(None, "seq", "head"),
        P(None, "head", "seq"),
        P(),
        P(),
        P(),
        P(),
        P(),
        P(),
        P(),
        P(),
        P(),
        P("seq", "head", None),
    )
    shape = dict(mesh.shape)
    fits = shape == {"seq": 8, "head": RING}
    return jax.shard_map(
        whole_rows if fits else split_heads_plan,
        mesh=mesh,
        in_specs=placed,
        out_specs=(
            P("seq", "head", None),
            P("seq", "head", None),
            P(),
            P(),
            P(),
            P(),
            P(),
            P(),
            P(),
        ),
        check_vma=False,
    )
```

```python
import functools

import jax
import jax.numpy as jnp
from jax import lax
from jax.experimental import pallas as pl
from jax.experimental.pallas import tpu as pltpu
from jax.sharding import PartitionSpec as P

F32 = jnp.float32
BF16 = jnp.bfloat16
MESH = pl.DeviceIdType.MESH
HEAD_DIM = 64
LAYERS = 2
EPS = 1e-06
MASKED = -1000000000.0
ROOT_HALF = 0.7071067811865476
ROOT_TAU = 0.3989422804014327
RING = 4
WIDTH = 1024
SLOTS = 512
QUARTER = SLOTS // RING
CHUNK = 256


def nn(left, right):
    return jnp.dot(left, right, preferred_element_type=F32)


def nt(left, right):
    return lax.dot_general(left, right, (((1,), (1,)), ((), ())), preferred_element_type=F32)


def tn(left, right):
    return lax.dot_general(left, right, (((0,), (0,)), ((), ())), preferred_element_type=F32)


def place():
    s, z = lax.axis_index("seq"), lax.axis_index("head")
    c, x, y = lax.rem(s, 2), lax.rem(lax.div(s, 2), 2), lax.div(s, 4)
    return s, z, c, x, y


def peers(s, z, c, x, y):
    return (s + 2 - 4 * x, z), (s + 4 - 8 * y, z), (s + 1 - 2 * c, z)


def greet(near_x, near_y, twin, s, z):
    barrier = pltpu.get_barrier_semaphore()
    for device in [(s, lax.rem(z + step, RING)) for step in (2, 1, 3)] + [near_x, near_y, twin]:
        pl.semaphore_signal(barrier, inc=1, device_id=device, device_id_type=MESH)


def greeted():
    pl.semaphore_wait(pltpu.get_barrier_semaphore(), 3 + RING - 1)


def forward_kernel(
    lengths_ref, separators_ref,
    tokens_ref, cot_ref, in_ref, out_ref, up_ref, down_ref,
    table_in, gain1_in, gain2_in, qb_in, vb_in, ob_in, b1_in, hb_in, db_in, b2_in,
    g_in, g_out, g_ff, cot_row, act_row, s_qkv, s_mix, s_expo, s_inv, s_n, s_rs, s_gp,
    table_ref, gain1_ref, gain2_ref, qb_ref, vb_ref, ob_ref, b1_ref, hb_ref, db_ref, b2_ref, down_v,
    tok_v, state_v, xb_v, qkv_v, mix_v, mixed_v, n_v, rs_v, normed_v, acc_v, active_v, gp_v, e_v, inv_v, w_v, f_v, dn_v, up_v, in_v, out_v, cot_v,
    tok_s, tok_r, cot_s, cot_r, at_s, at_r, ff_s, ff_r, z_s, z_r, f_s, f_r, cc_s, cc_r,
    small_sem, own_sem, put_sem, ld_sem, w_sem, save_sem, e_sem, gp_sem,
):
    s, z, c, x, y = place()
    near_x, near_y, twin = peers(s, z, c, x, y)
    half = QUARTER // 2
    A, B = pl.ds(0, half), pl.ds(half, half)
    every = slice(None)
    sent = []

    def remote(src, dst, ss, rs, device):
        return pltpu.make_async_remote_copy(
            src_ref=src, dst_ref=dst, send_sem=ss, recv_sem=rs, device_id=device, device_id_type=MESH
        )

    def go(copy):
        copy.start()
        sent.append(copy)

    small_in = [
        pltpu.make_async_copy(src, dst, small_sem.at[k]) for k, (src, dst) in enumerate((
            (down_ref, down_v), (table_in, table_ref), (gain1_in, gain1_ref), (gain2_in, gain2_ref),
            (qb_in, qb_ref), (vb_in, vb_ref), (ob_in, ob_ref), (b1_in, b1_ref), (hb_in, hb_ref),
            (db_in, db_ref), (b2_in, b2_ref),
        ))
    ]

    def own_in(l):
        return [
            pltpu.make_async_copy(ref.at[l], held.at[l], own_sem.at[l, t])
            for t, (ref, held) in enumerate(((up_ref, up_v), (in_ref, in_v), (out_ref, out_v)))
        ]

    def own_out(l):
        places = (
            (up_v, g_ff.at[l, z, 0, y, x, c]), (in_v, g_in.at[l, y, x, c]), (out_v, g_out.at[l, y, x, c]),
            (dn_v, g_ff.at[l, z, 1, y, x, c]),
        )
        return [pltpu.make_async_copy(held.at[l], dst, put_sem.at[l, t]) for t, (held, dst) in enumerate(places)]

    gathered = (g_in, g_out)
    shard = (in_ref, out_ref)

    def at_first(l, t):
        g = gathered[t]
        return (
            remote(shard[t].at[l, A], g.at[l, y, x, c, A], at_s.at[l, t, 0], at_r.at[l, t, 0], near_x),
            remote(shard[t].at[l, B], g.at[l, y, x, c, B], at_s.at[l, t, 1], at_r.at[l, t, 1], near_y),
        )

    def at_last(l, t):
        g = gathered[t]
        pair, pile = g.at[l, y, every, c, A], g.at[l, every, x, c, B]
        return (
            remote(pair, pair, at_s.at[l, t, 2], at_r.at[l, t, 2], near_y),
            remote(pile, pile, at_s.at[l, t, 3], at_r.at[l, t, 3], near_x),
        )

    def at_core(l, t, side):
        part = gathered[t].at[l, every, every, c, (A, B)[side]]
        return remote(part, part, at_s.at[l, t, 4 + side], at_r.at[l, t, 4 + side], twin)

    def at_send(l, t):
        for copy in at_first(l, t):
            go(copy)

    def at_pass(l, t, side):
        at_first(l, t)[side].wait_recv()
        go(at_last(l, t)[side])

    def at_share(l, t, side):
        at_last(l, t)[side].wait_recv()
        go(at_core(l, t, side))

    def at_ready(l, t):
        for side in range(2):
            at_core(l, t, side).wait_recv()

    def rank(i):
        near = z if i == 0 else None
        if i == 0:
            return near
        low = jnp.where(z < 2, z, RING - 1 - z)
        block = (1 - low) if i == 1 else i
        return jnp.where(z < 2, block, RING - 1 - block)

    def ff_part(l, block, side, kind):
        return g_ff.at[l, block, kind, y, every, c, A] if side == 0 else g_ff.at[l, block, kind, every, x, c, B]

    def ff_first(l, side, kind):
        part = g_ff.at[l, z, kind, y, x, c, (A, B)[side]]
        return remote(part, part, ff_s.at[l, side, kind], ff_r.at[l, side, kind], (near_x, near_y)[side])

    def ff_z(l, block, side, kind, way):
        part = ff_part(l, block, side, kind)
        beside = lax.rem(z + 1, RING) if way == 0 else lax.rem(z + RING - 1, RING)
        return remote(part, part, z_s.at[way], z_r.at[l, block, side, kind], (s, beside))

    def ff_last(l, block, side, kind):
        part = ff_part(l, block, side, kind)
        return remote(part, part, f_s.at[0], f_r.at[l, block, side, kind], (near_y, near_x)[side])

    def ff_core(l, block, side, kind):
        part = g_ff.at[l, block, kind, every, every, c, (A, B)[side]]
        return remote(part, part, cc_s.at[0], cc_r.at[l, block, side, kind], twin)

    right = z < RING - 1
    left = z > 0

    def ff_send(l):
        for kind in range(2):
            for side in range(2):
                go(ff_first(l, side, kind))

    def ff_spread(l, side, kind):
        ff_first(l, side, kind).wait_recv()
        pl.when(right)(ff_z(l, z, side, kind, 0).start)
        pl.when(left)(ff_z(l, z, side, kind, 1).start)

    def ff_cross(l, i, side, kind):
        ff_last(l, rank(i), side, kind).start()

    def ff_relay(l, i, side, kind):
        block = rank(i)
        ff_z(l, block, side, kind, 0).wait_recv()
        pl.when(jnp.logical_and(block < z, right))(ff_z(l, block, side, kind, 0).start)
        pl.when(jnp.logical_and(block > z, left))(ff_z(l, block, side, kind, 1).start)

    def ff_share(l, i, side, kind):
        ff_last(l, rank(i), side, kind).wait_recv()
        ff_core(l, rank(i), side, kind).start()

    def ff_load(l, i, side, kind, parity):
        part = (every, every, c if parity == 0 else 1 - c, (A, B)[side])
        return pltpu.make_async_copy(
            g_ff.at[(l, rank(i), kind) + part], f_v.at[(kind, i) + part], ld_sem.at[kind, i, side, parity]
        )

    def ff_hold(l, i, side, kind):
        ff_load(l, i, side, kind, 0).start()

    def ff_take(l, i, kind):
        for side in range(2):
            ff_core(l, rank(i), side, kind).wait_recv()
            ff_load(l, i, side, kind, 1).start()

    def ff_held(l, i, kind):
        for side in range(2):
            for parity in range(2):
                ff_load(l, i, side, kind, parity).wait()

    def ff_drain():
        def drain(part, sem):
            remote(part, part, sem, z_r.at[0, 0, 0, 0], twin).wait_send()

        drain(g_ff.at[0, every, 0], f_s.at[0])
        drain(g_ff.at[0], cc_s.at[0])
        for blocks in range(1, RING):
            pl.when(z == blocks - 1)(functools.partial(drain, g_ff.at[0, pl.ds(0, blocks), 0], z_s.at[0]))
            pl.when(z == RING - blocks)(functools.partial(drain, g_ff.at[0, pl.ds(0, blocks), 0], z_s.at[1]))

    def row_copies(src, dst, ss, rs):
        here = dst.at[pl.ds(pl.multiple_of(z * QUARTER, QUARTER), QUARTER)]
        copies = []
        for step in range(1, RING):
            to = lax.rem(z + step, RING)
            copies.append(remote(src.at[to], here, ss.at[step], rs.at[step], (s, to)))
        return copies, here

    def load(slot, src, width=WIDTH):
        copy = pltpu.make_async_copy(src, w_v.at[slot], w_sem.at[slot])
        copy.start()
        return copy

    def weight(slot, cols):
        return w_v[slot, :, :, :, :, cols].reshape(WIDTH, CHUNK)

    saves = {}

    def save(key, src, dst, sem):
        copy = pltpu.make_async_copy(src, dst, sem)
        copy.start()
        saves[key] = copy

    def settle(key):
        if key in saves:
            saves.pop(key).wait()

    def rows_loop(body, rows=64):
        def step(r, carry):
            body(pl.ds(pl.multiple_of(r * rows, rows), rows), r * rows)
            return carry
        lax.fori_loop(0, SLOTS // rows, step, 0)

    def norm_rows(total, gain, bias, rr, which):
        mean = jnp.sum(total, -1, keepdims=True) * (1.0 / WIDTH)
        centered = total - mean
        rs = lax.rsqrt(jnp.sum(centered * centered, -1, keepdims=True) * (1.0 / WIDTH) + EPS)
        n = centered * rs
        n_v[which, rr] = n.astype(BF16)
        rs_v[which, rr] = rs + jnp.zeros((64, 128), F32)
        return n * gain + bias

    def start_state():
        length, split = lengths_ref[z], separators_ref[z]

        def body(rr, base):
            pos = lax.broadcasted_iota(jnp.int32, (64, 1), 0) + base
            second = jnp.logical_and(pos > split, pos < length)
            kind = jnp.where(second, table_ref[1:2], table_ref[0:1])
            value = tok_v[rr].astype(F32) + kind
            state_v[rr] = value
            xb_v[rr] = value.astype(BF16)
        rows_loop(body)

    loading = {}

    def fetch_in(l):
        at_ready(l, 0)
        loading["in"] = [load(j, g_in.at[l, :, :, :, :, pl.ds(j * WIDTH, WIDTH)]) for j in range(3)]

    def fetch_out(l):
        at_ready(l, 1)
        loading["out"] = load(3, g_out.at[l])

    def project(l):
        settle("qkv")
        loads = loading.pop("in")
        for j in range(3):
            loads[j].wait()
            for k in range(WIDTH // CHUNK):
                cols = pl.ds(k * CHUNK, CHUNK)
                value = nn(xb_v[...], weight(j, cols))
                if j == 0:
                    value = (value + qb_ref[l:l + 1, k * CHUNK:(k + 1) * CHUNK]).astype(BF16) * BF16(HEAD_DIM ** -0.5)
                elif j == 2:
                    value = value + vb_ref[l:l + 1, k * CHUNK:(k + 1) * CHUNK]
                qkv_v[:, pl.ds(j * WIDTH + k * CHUNK, CHUNK)] = value.astype(BF16)
        save("qkv", qkv_v, s_qkv.at[l], save_sem.at[0])

    pairs = WIDTH // (2 * HEAD_DIM)
    wide = 2 * HEAD_DIM

    def attend(l, first, last):
        bias = jnp.where(
            lax.broadcasted_iota(jnp.int32, (1, SLOTS), 1) < lengths_ref[z], 0.0, MASKED
        ).astype(F32)
        lane = lax.broadcasted_iota(jnp.int32, (SLOTS, wide), 1) < HEAD_DIM

        def e_save(p, slot):
            return (
                pltpu.make_async_copy(e_v.at[slot], s_expo.at[l, p], e_sem.at[slot, 0]),
                pltpu.make_async_copy(inv_v.at[slot], s_inv.at[l, p], e_sem.at[slot, 1]),
            )

        def step(p, carry):
            slot = lax.rem(p, 2)

            @pl.when(p >= 2)
            def _():
                for copy in e_save(p - 2, slot):
                    copy.wait()

            q = qkv_v[:, pl.ds(pl.multiple_of(p * wide, wide), wide)]
            k = qkv_v[:, pl.ds(pl.multiple_of(WIDTH + p * wide, wide), wide)]
            v = qkv_v[:, pl.ds(pl.multiple_of(2 * WIDTH + p * wide, wide), wide)]
            mine = (jnp.where(lane, q, jnp.zeros_like(q)), jnp.where(lane, jnp.zeros_like(q), q))
            scores = [nt(mine[h], k) + bias for h in range(2)]
            expo = [jnp.exp(part - jnp.max(part, -1, keepdims=True)) for part in scores]
            invs = [1.0 / jnp.sum(part, -1, keepdims=True) for part in expo]
            expo = [part.astype(BF16) for part in expo]
            for h in range(2):
                e_v[slot, h] = expo[h]
            outs = [nn(expo[h], v) * invs[h] for h in range(2)]
            inv_v[slot] = jnp.where(lane, invs[0], invs[1])
            mixed = jnp.where(lane, outs[0], outs[1])
            mixed_v[:, pl.ds(pl.multiple_of(p * wide, wide), wide)] = mixed
            mix_v[:, pl.ds(pl.multiple_of(p * wide, wide), wide)] = mixed.astype(BF16)
            for copy in e_save(p, slot):
                copy.start()
            return carry

        lax.fori_loop(first, last, step, 0)
        if last == pairs:
            for p in (pairs - 2, pairs - 1):
                for copy in e_save(p, p % 2):
                    copy.wait()

    def attention_out(l):
        loading.pop("out").wait()
        for k in range(WIDTH // CHUNK):
            cols = pl.ds(k * CHUNK, CHUNK)
            acc_v[:, cols] = nn(mix_v[...], weight(3, cols))
        settle("mix")
        save("mix", mixed_v, s_mix.at[l], save_sem.at[1])
        settle("n0")
        settle("rs0")

        def body(rr, base):
            total = state_v[rr] + acc_v[rr] + ob_ref[l:l + 1]
            value = norm_rows(total, gain1_ref[l:l + 1], b1_ref[l:l + 1], rr, 0)
            normed_v[rr] = value
            xb_v[rr] = value.astype(BF16)
        rows_loop(body)
        save("n0", n_v.at[0], s_n.at[l, 0], save_sem.at[2])
        save("rs0", rs_v.at[0], s_rs.at[l, 0], save_sem.at[3])

    def feed_up(l, i):
        block = rank(i)
        ff_held(l, i, 0)
        settle(("gp", i % 2))
        for k in range(WIDTH // CHUNK):
            cols = pl.ds(k * CHUNK, CHUNK)
            shift = hb_ref[l:l + 1, pl.ds(pl.multiple_of(block * WIDTH + k * CHUNK, CHUNK), CHUNK)]
            hidden = nn(xb_v[...], f_v[0, i, :, :, :, :, cols].reshape(WIDTH, CHUNK)) + shift
            share = 0.5 + 0.5 * lax.erf(hidden * ROOT_HALF)
            active_v[:, cols] = (hidden * share).astype(BF16)
            slope = share + hidden * (jnp.exp(hidden * hidden * -0.5) * ROOT_TAU)
            gp_v[i % 2, :, cols] = slope.astype(BF16)
        save(("gp", i % 2), gp_v.at[i % 2], s_gp.at[l, block], gp_sem.at[i % 2])

    def feed_down(l, i):
        ff_held(l, i, 1)
        for k in range(2):
            cols = pl.ds(k * SLOTS, SLOTS)
            value = nt(active_v[...], f_v[1, i, k].reshape(SLOTS, WIDTH))
            if i == 0:
                acc_v[:, cols] = value
            else:
                acc_v[:, cols] += value

    def finish(l):
        settle("n1")
        settle("rs1")

        def body(rr, base):
            total = normed_v[rr] + acc_v[rr] + db_ref[l:l + 1]
            value = norm_rows(total, gain2_ref[l:l + 1], b2_ref[l:l + 1], rr, 1)
            state_v[rr] = value
            xb_v[rr] = value.astype(BF16)
        rows_loop(body)
        save("n1", n_v.at[1], s_n.at[l, 1], save_sem.at[4])
        save("rs1", rs_v.at[1], s_rs.at[l, 1], save_sem.at[5])

    for l in range(LAYERS):
        for copy in own_in(l):
            copy.start()
    for copy in small_in:
        copy.start()
    cot_in = pltpu.make_async_copy(cot_ref.at[z], cot_v, save_sem.at[7])
    cot_in.start()
    greet(near_x, near_y, twin, s, z)
    small_in[0].wait()
    for l in range(LAYERS):
        dn_v[l] = down_v[l].T
    for l in range(LAYERS):
        for copy in own_in(l):
            copy.wait()
        for copy in own_out(l):
            copy.start()
    greeted()
    at_send(0, 0)
    at_send(0, 1)
    tok_copies, tok_here = row_copies(tokens_ref, tok_v, tok_s, tok_r)
    for copy in tok_copies:
        go(copy)
    tok_own = pltpu.make_async_copy(tokens_ref.at[z], tok_here, tok_s.at[0])
    tok_own.start()
    own_out(0)[0].wait()
    own_out(0)[3].wait()
    ff_send(0)
    own_out(0)[1].wait()
    at_pass(0, 0, 0)
    at_send(1, 1)
    ff_spread(0, 0, 1)
    own_out(1)[0].wait()
    own_out(1)[3].wait()
    ff_send(1)
    at_pass(0, 0, 1)
    ff_spread(0, 1, 1)
    ff_spread(0, 0, 0)
    at_send(1, 0)
    ff_cross(0, 0, 1, 1)
    ff_spread(0, 1, 0)
    ff_relay(0, 2, 0, 1)
    for copy in small_in[1:]:
        copy.wait()
    tok_own.wait()
    for copy in tok_copies:
        copy.wait_recv()
    start_state()
    own_out(0)[2].wait()
    at_pass(0, 1, 0)
    ff_relay(0, 1, 0, 0)
    ff_relay(0, 1, 0, 1)
    at_share(0, 0, 1)
    ff_relay(0, 1, 1, 0)
    ff_cross(0, 1, 0, 1)
    ff_relay(0, 1, 1, 1)
    ff_relay(0, 2, 0, 0)
    ff_cross(0, 2, 0, 0)
    ff_cross(0, 0, 0, 0)
    ff_cross(0, 1, 1, 0)
    ff_cross(0, 2, 0, 1)
    ff_cross(0, 0, 1, 0)
    ff_cross(0, 0, 0, 1)
    at_pass(0, 1, 1)
    ff_relay(0, 2, 1, 1)
    at_share(0, 0, 0)
    ff_relay(0, 2, 1, 0)
    ff_cross(0, 2, 1, 1)
    ff_relay(0, 3, 0, 0)
    ff_relay(0, 3, 0, 1)
    ff_share(0, 2, 0, 0)
    ff_hold(0, 2, 0, 0)
    ff_share(0, 0, 1, 1)
    ff_hold(0, 0, 1, 1)
    ff_cross(0, 1, 1, 1)
    ff_share(0, 1, 1, 0)
    ff_hold(0, 1, 1, 0)
    ff_cross(0, 1, 0, 0)
    ff_relay(0, 3, 1, 0)
    ff_cross(0, 3, 1, 0)
    ff_cross(0, 3, 0, 0)
    ff_share(0, 1, 0, 1)
    ff_hold(0, 1, 0, 1)
    ff_cross(0, 3, 0, 1)
    ff_spread(1, 0, 0)
    fetch_in(0)
    project(0)
    ff_cross(0, 2, 1, 0)
    ff_relay(0, 3, 1, 1)
    own_out(1)[1].wait()
    at_pass(1, 0, 1)
    ff_spread(1, 1, 1)
    attend(0, 0, 2)
    ff_share(0, 0, 0, 0)
    ff_hold(0, 0, 0, 0)
    at_pass(1, 0, 0)
    at_share(0, 1, 0)
    at_share(0, 1, 1)
    ff_share(0, 1, 1, 1)
    ff_hold(0, 1, 1, 1)
    ff_share(0, 0, 1, 0)
    ff_hold(0, 0, 1, 0)
    ff_spread(1, 0, 1)
    ff_cross(0, 3, 1, 1)
    ff_relay(1, 1, 0, 0)
    attend(0, 2, 4)
    attend(0, 4, 6)
    ff_cross(1, 0, 0, 0)
    fetch_out(0)
    attend(0, 6, 8)
    ff_share(0, 0, 0, 1)
    ff_hold(0, 0, 0, 1)
    ff_share(0, 3, 1, 0)
    ff_hold(0, 3, 1, 0)
    attention_out(0)
    ff_take(0, 0, 0)
    ff_relay(1, 2, 0, 0)
    ff_share(0, 2, 1, 0)
    ff_hold(0, 2, 1, 0)
    ff_share(0, 1, 0, 0)
    ff_hold(0, 1, 0, 0)
    feed_up(0, 0)
    ff_spread(1, 1, 0)
    ff_cross(1, 0, 0, 1)
    ff_share(0, 3, 0, 1)
    ff_hold(0, 3, 0, 1)
    ff_take(0, 2, 0)
    ff_take(0, 1, 0)
    ff_take(0, 1, 1)
    ff_share(0, 2, 0, 1)
    ff_hold(0, 2, 0, 1)
    ff_relay(1, 1, 1, 1)
    ff_cross(1, 0, 1, 1)
    ff_share(0, 3, 0, 0)
    ff_hold(0, 3, 0, 0)
    ff_share(0, 2, 1, 1)
    ff_hold(0, 2, 1, 1)
    ff_take(0, 0, 1)
    feed_down(0, 0)
    ff_cross(1, 0, 1, 0)
    ff_relay(1, 1, 0, 1)
    ff_cross(1, 1, 0, 1)
    ff_relay(1, 2, 0, 1)
    own_out(1)[2].wait()
    at_pass(1, 1, 0)
    ff_take(0, 3, 0)
    feed_up(0, 1)
    at_share(1, 0, 1)
    at_pass(1, 1, 1)
    feed_down(0, 1)
    ff_take(0, 2, 1)
    ff_share(0, 3, 1, 1)
    ff_hold(0, 3, 1, 1)
    ff_cross(1, 1, 0, 0)
    ff_relay(1, 2, 1, 1)
    ff_relay(1, 1, 1, 0)
    ff_cross(1, 1, 1, 1)
    feed_up(0, 2)
    ff_cross(1, 1, 1, 0)
    ff_take(0, 3, 1)
    at_share(1, 0, 0)
    feed_down(0, 2)
    ff_cross(1, 2, 0, 0)
    feed_up(0, 3)
    ff_relay(1, 2, 1, 0)
    ff_share(1, 0, 0, 0)
    ff_hold(1, 0, 0, 0)
    feed_down(0, 3)
    ff_share(1, 0, 1, 1)
    ff_hold(1, 0, 1, 1)
    fetch_in(1)
    finish(0)
    ff_share(1, 0, 1, 0)
    ff_hold(1, 0, 1, 0)
    ff_relay(1, 3, 0, 0)
    project(1)
    ff_cross(1, 2, 1, 1)
    ff_relay(1, 3, 1, 0)
    ff_share(1, 1, 0, 1)
    ff_hold(1, 1, 0, 1)
    ff_cross(1, 2, 0, 1)
    settle("mix")
    attend(1, 0, 2)
    at_share(1, 1, 1)
    ff_cross(1, 2, 1, 0)
    ff_share(1, 0, 0, 1)
    ff_hold(1, 0, 0, 1)
    attend(1, 2, 4)
    at_share(1, 1, 0)
    ff_relay(1, 3, 1, 1)
    attend(1, 4, 6)
    ff_share(1, 1, 1, 1)
    ff_hold(1, 1, 1, 1)
    ff_cross(1, 3, 1, 0)
    fetch_out(1)
    attend(1, 6, 8)
    ff_relay(1, 3, 0, 1)
    ff_take(1, 0, 0)
    ff_cross(1, 3, 0, 0)
    cot_copies, cot_here = row_copies(cot_ref, cot_row, cot_s, cot_r)
    for copy in cot_copies:
        go(copy)
    cot_in.wait()
    cot_own = pltpu.make_async_copy(cot_v, cot_here, cot_s.at[0])
    cot_own.start()
    ff_share(1, 1, 0, 0)
    ff_hold(1, 1, 0, 0)
    ff_take(1, 0, 1)
    ff_share(1, 2, 0, 0)
    ff_hold(1, 2, 0, 0)
    ff_cross(1, 3, 1, 1)
    ff_share(1, 1, 1, 0)
    ff_hold(1, 1, 1, 0)
    ff_share(1, 2, 1, 1)
    ff_hold(1, 2, 1, 1)
    attention_out(1)
    ff_take(1, 1, 1)
    ff_take(1, 1, 0)
    ff_cross(1, 3, 0, 1)
    feed_up(1, 0)
    ff_share(1, 2, 0, 1)
    ff_hold(1, 2, 0, 1)
    ff_share(1, 2, 1, 0)
    ff_hold(1, 2, 1, 0)
    feed_down(1, 0)
    ff_share(1, 3, 0, 0)
    ff_hold(1, 3, 0, 0)
    ff_share(1, 3, 1, 0)
    ff_hold(1, 3, 1, 0)
    feed_up(1, 1)
    ff_take(1, 2, 0)
    feed_down(1, 1)
    ff_take(1, 2, 1)
    ff_share(1, 3, 0, 1)
    ff_hold(1, 3, 0, 1)
    ff_share(1, 3, 1, 1)
    ff_hold(1, 3, 1, 1)
    feed_up(1, 2)
    ff_take(1, 3, 0)
    feed_down(1, 2)
    ff_take(1, 3, 1)
    feed_up(1, 3)
    feed_down(1, 3)
    finish(1)
    save("act", xb_v, act_row, save_sem.at[6])
    for key in list(saves):
        settle(key)
    cot_own.wait()
    for copy in cot_copies:
        copy.wait_recv()
    for copy in sent:
        copy.wait_send()
    ff_drain()


def forward(lengths, separators, tokens, cotangent, project_in, project_out, up, down, small):
    shape = jax.ShapeDtypeStruct
    dma = pltpu.SemaphoreType.DMA
    vmem = lambda *dims_type: pltpu.VMEM(dims_type[:-1], dims_type[-1])
    L = LAYERS
    pairs = WIDTH // (2 * HEAD_DIM)
    out_shape = (
        shape((L, 2, 2, 2, QUARTER, 3 * WIDTH), BF16),
        shape((L, 2, 2, 2, QUARTER, WIDTH), BF16),
        shape((L, RING, 2, 2, 2, 2, QUARTER, WIDTH), BF16),
        shape((SLOTS, WIDTH), BF16),
        shape((SLOTS, WIDTH), BF16),
        shape((L, SLOTS, 3 * WIDTH), BF16),
        shape((L, SLOTS, WIDTH), F32),
        shape((L, pairs, 2, SLOTS, SLOTS), BF16),
        shape((L, pairs, SLOTS, 2 * HEAD_DIM), F32),
        shape((L, 2, SLOTS, WIDTH), BF16),
        shape((L, 2, SLOTS, 128), F32),
        shape((L, RING, SLOTS, WIDTH), BF16),
    )
    anywhere = pl.BlockSpec(memory_space=pl.ANY)
    scalar = pl.BlockSpec(memory_space=pltpu.SMEM)
    return pl.pallas_call(
        forward_kernel,
        out_shape=out_shape,
        in_specs=[scalar] * 2 + [anywhere] * (6 + len(small)),
        out_specs=[anywhere] * len(out_shape),
        scratch_shapes=[vmem(*a.shape, F32) for a in small] + [
            vmem(*down.shape, BF16), vmem(SLOTS, WIDTH, BF16), vmem(SLOTS, WIDTH, F32), vmem(SLOTS, WIDTH, BF16),
            vmem(SLOTS, 3 * WIDTH, BF16), vmem(SLOTS, WIDTH, BF16), vmem(SLOTS, WIDTH, F32),
            vmem(2, SLOTS, WIDTH, BF16), vmem(2, SLOTS, 128, F32), vmem(SLOTS, WIDTH, F32), vmem(SLOTS, WIDTH, F32),
            vmem(SLOTS, WIDTH, BF16), vmem(2, SLOTS, WIDTH, BF16), vmem(2, 2, SLOTS, SLOTS, BF16),
            vmem(2, SLOTS, 2 * HEAD_DIM, F32), vmem(4, 2, 2, 2, QUARTER, WIDTH, BF16),
            vmem(2, RING, 2, 2, 2, QUARTER, WIDTH, BF16),
            vmem(L, QUARTER, WIDTH, BF16), vmem(L, QUARTER, WIDTH, BF16), vmem(L, QUARTER, 3 * WIDTH, BF16),
            vmem(L, QUARTER, WIDTH, BF16), vmem(QUARTER, WIDTH, BF16),
            dma((RING,)), dma((RING,)), dma((RING,)), dma((RING,)),
            dma((L, 2, 6)), dma((L, 2, 6)), dma((L, 2, 2)), dma((L, 2, 2)),
            dma((2,)), dma((L, RING, 2, 2)), dma((1,)), dma((L, RING, 2, 2)),
            dma((1,)), dma((L, RING, 2, 2)),
            dma((1 + len(small),)), dma((L, 3)), dma((L, 4)), dma((2, RING, 2, 2)), dma((4,)), dma((8,)), dma((2, 2)), dma((2,)),
        ],
        compiler_params=pltpu.CompilerParams(
            collective_id=0, has_side_effects=True, vmem_limit_bytes=60 << 20
        ),
        cost_estimate=pl.CostEstimate(flops=30 * 10**9, bytes_accessed=150 << 20, transcendentals=10**7),
    )(lengths, separators, tokens, cotangent, project_in, project_out, up, down, *small)


TOTAL_ROWS = 32


def sum_row(l, kind):
    if l == 0:
        return kind if kind < 2 else 6 + kind
    return 16 + kind


def backward_kernel(
    gain1_ref, gain2_ref,
    w_in, w_out, w_ff, cot_row, act_row, s_qkv, s_mix, s_expo, s_inv, s_n, s_rs, s_gp,
    act_out, grad_out, sums_out,
    g_v, gs_v, acc_v, low_v, gh_v, gm_v, gp_v, gproj_v, out_v, n_v, rs_v, slope_v, qkv_v, mix_v, e_v, inv_v,
    ff_v, wout_v, win_v, part_v, sum_v, got_v,
    a_s, a_r, o_s, o_r, r_s, r_r,
    ff_sem, w_sem, n_sem, slope_sem, e_sem, row_sem, own_sem,
):
    s, z, c, x, y = place()
    near_x, near_y, twin = peers(s, z, c, x, y)
    wide = 2 * HEAD_DIM
    pairs = WIDTH // wide
    sent = []

    def remote(src, dst, ss, rs, device):
        return pltpu.make_async_remote_copy(
            src_ref=src, dst_ref=dst, send_sem=ss, recv_sem=rs, device_id=device, device_id_type=MESH
        )

    def go(copy):
        copy.start()
        sent.append(copy)

    def fetch(src, dst, sem):
        return pltpu.make_async_copy(src, dst, sem)

    layers = list(reversed(range(LAYERS)))

    def norm_loads(l):
        return [fetch(s_n.at[l, k], n_v.at[k], n_sem.at[k]) for k in range(2)] + [
            fetch(s_rs.at[l, k], rs_v.at[k], n_sem.at[2 + k]) for k in range(2)
        ]

    def block_loads(l, i):
        slot = i % 2
        return [
            fetch(w_ff.at[l, i, 1], ff_v.at[slot, 1], ff_sem.at[slot, 1]),
            fetch(s_gp.at[l, i], slope_v.at[slot], slope_sem.at[slot]),
            fetch(w_ff.at[l, i, 0], ff_v.at[slot, 0], ff_sem.at[slot, 0]),
        ]

    def out_load(l):
        return fetch(w_out.at[l], wout_v, w_sem.at[0])

    def in_load(l):
        return fetch(w_in.at[l], win_v, w_sem.at[1])

    def row_loads(l):
        return [fetch(s_qkv.at[l], qkv_v, row_sem.at[0]), fetch(s_mix.at[l], mix_v, row_sem.at[1])]

    depth = 4

    def expo_loads(step):
        l, p, slot = LAYERS - 1 - lax.div(step, pairs), lax.rem(step, pairs), lax.rem(step, depth)
        return (
            fetch(s_expo.at[l, p], e_v.at[slot], e_sem.at[slot, 0]),
            fetch(s_inv.at[l, p], inv_v.at[slot], e_sem.at[slot, 1]),
        )

    def start(copies):
        for copy in copies:
            copy.start()

    def wait(copies):
        for copy in copies:
            copy.wait()

    near_z, far_z = (s, z + 1 - 2 * lax.rem(z, 2)), (s, lax.rem(z + 2, RING))
    partners = (near_z, far_z, twin, near_x, near_y)

    early, late, every = pl.ds(8, TOTAL_ROWS - 8), pl.ds(0, 8), pl.ds(0, TOTAL_ROWS)

    def swap(here, stage):
        which = 1 if here is late else 0
        return remote(sum_v.at[stage, here], got_v.at[stage, here], r_s.at[which, stage], r_r.at[which, stage],
                      partners[stage])

    def take(here, stage):
        swap(here, stage).wait_recv()
        sum_v[stage + 1, here] = sum_v[stage, here] + got_v[stage, here]

    def fold(value):
        total = value[0:8]
        for k in range(1, value.shape[0] // 8):
            total = total + value[8 * k:8 * k + 8]
        return total

    def rows_loop(body, rows=64):
        def step(r, carry):
            body(pl.ds(pl.multiple_of(r * rows, rows), rows))
            return carry
        lax.fori_loop(0, SLOTS // rows, step, 0)

    def put(at, value):
        sum_v[0, pl.ds(at, 1)] = value

    def norm_back(grad, gain, which, rr):
        n = n_v[which, rr].astype(F32)
        u = grad * gain
        mean = jnp.sum(u, -1, keepdims=True) * (1.0 / WIDTH)
        tilt = jnp.sum(u * n, -1, keepdims=True) * (1.0 / WIDTH)
        return (u - mean - n * tilt) * rs_v[which, rr, 0:1]

    def layer_back(l, last):
        row = functools.partial(sum_row, l)
        wait(norm_loads(l)[1::2])
        part_v[...] = jnp.zeros_like(part_v)

        def second(rr):
            grad = out_v[rr].astype(F32) if l == layers[0] else g_v[rr]
            part_v[0] += fold(grad)
            out = norm_back(grad, gain2_ref[l:l + 1], 1, rr)
            part_v[1] += fold(out)
            gs_v[rr] = out
            low_v[rr] = out.astype(BF16)
        rows_loop(second)
        put(row(5), jnp.sum(part_v[0], 0, keepdims=True))
        put(row(4), jnp.sum(part_v[1], 0, keepdims=True))

        for i in range(RING):
            slot = i % 2
            loads = block_loads(l, i)
            wait(loads[:2])
            for k in range(WIDTH // CHUNK):
                cols = pl.ds(k * CHUNK, CHUNK)
                value = nn(low_v[...], ff_v[slot, 1, :, cols]) * slope_v[slot, :, cols].astype(F32)
                sum_v[0, pl.ds(row(6 + i), 1), cols] = jnp.sum(value, 0, keepdims=True)
                gh_v[:, cols] = value.astype(BF16)
            loads[2].wait()
            for k in range(2):
                cols = pl.ds(k * SLOTS, SLOTS)
                value = nt(gh_v[...], ff_v[slot, 0, pl.ds(k * SLOTS, SLOTS)])
                if i == 0:
                    acc_v[:, cols] = value
                else:
                    acc_v[:, cols] += value
            if i + 2 < RING:
                start(block_loads(l, i + 2))
            if i == 0 and l == layers[0]:
                greeted()
                for step in range(1, RING):
                    go(act_copy(step))
            if i == 1:
                start(norm_loads(l)[0::2])
                out_load(l).start()
            elif i == 2:
                start(row_loads(l))
            elif i == 3 and l == layers[0]:
                for step in range(depth):
                    start(expo_loads(jnp.int32(step)))

        if l == layers[0]:
            act_own()[0].wait()
            act_own()[1].start()
            act_own()[1].wait()
        wait(norm_loads(l)[0::2])
        part_v[...] = jnp.zeros_like(part_v)

        def first(rr):
            grad = gs_v[rr] + acc_v[rr]
            part_v[0] += fold(grad)
            out = norm_back(grad, gain1_ref[l:l + 1], 0, rr)
            part_v[1] += fold(out)
            gs_v[rr] = out
            low_v[rr] = out.astype(BF16)
        rows_loop(first)
        put(row(3), jnp.sum(part_v[0], 0, keepdims=True))
        put(row(2), jnp.sum(part_v[1], 0, keepdims=True))
        in_load(l).start()
        out_load(l).wait()
        for k in range(2):
            gm_v[:, pl.ds(k * SLOTS, SLOTS)] = nt(low_v[...], wout_v[pl.ds(k * SLOTS, SLOTS)]).astype(BF16)
        wait(row_loads(l))
        lane = lax.broadcasted_iota(jnp.int32, (SLOTS, wide), 1) < HEAD_DIM
        offset = layers.index(l) * pairs

        def attend(p, carry):
            step = offset + p
            slot = lax.rem(step, depth)
            for copy in expo_loads(step):
                copy.wait()
            at = lambda k: pl.ds(pl.multiple_of(k * WIDTH + p * wide, wide), wide)
            q, k, v = qkv_v[:, at(0)], qkv_v[:, at(1)], qkv_v[:, at(2)]
            gm = gm_v[:, at(0)].astype(F32) * inv_v[slot]
            mixed = mix_v[:, at(0)]
            mine = (lane, jnp.logical_not(lane))
            low = [jnp.where(m, gm, 0.0).astype(BF16) for m in mine]
            inner = [jnp.sum(part.astype(F32) * mixed, -1, keepdims=True) for part in low]
            gs = [
                (e_v[slot, h].astype(F32) * (nt(low[h], v) - inner[h])).astype(BF16) for h in range(2)
            ]
            both = jnp.concatenate([jnp.where(m, q, jnp.zeros_like(q)) for m in mine], 0)
            gk = tn(jnp.concatenate(gs, 0), both)
            gv = tn(e_v[slot].reshape(2 * SLOTS, SLOTS), jnp.concatenate(low, 0)).astype(BF16)
            gq = (jnp.where(lane, nn(gs[0], k), nn(gs[1], k)) * (HEAD_DIM ** -0.5)).astype(BF16)
            gproj_v[:, at(0)] = gq
            gproj_v[:, at(1)] = gk.astype(BF16)
            gproj_v[:, at(2)] = gv
            sum_v[0, pl.ds(row(0), 1), at(0)] = jnp.sum(gq.astype(F32), 0, keepdims=True)
            sum_v[0, pl.ds(row(1), 1), at(0)] = jnp.sum(gv.astype(F32), 0, keepdims=True)

            @pl.when(step + depth < LAYERS * pairs)
            def _():
                for copy in expo_loads(step + depth):
                    copy.start()
            return carry

        if not last:
            lax.fori_loop(0, pairs // 2, attend, 0)
            start(norm_loads(l - 1)[1::2])
            start(block_loads(l - 1, 0))
            lax.fori_loop(pairs // 2, pairs, attend, 0)
            start(block_loads(l - 1, 1))
            in_load(l).wait()
            for k in range(WIDTH // CHUNK):
                cols = pl.ds(k * CHUNK, CHUNK)
                g_v[:, cols] = gs_v[:, cols] + nt(gproj_v[...], win_v[pl.ds(k * CHUNK, CHUNK)])
        else:
            go(swap(early, 0))
            lax.fori_loop(0, pairs // 2, attend, 0)
            take(early, 0)
            go(swap(early, 1))
            lax.fori_loop(pairs // 2, pairs, attend, 0)
            go(swap(late, 0))
            in_load(l).wait()
            for k in range(WIDTH // CHUNK):
                cols = pl.ds(k * CHUNK, CHUNK)
                out_v[:, cols] = (gs_v[:, cols] + nt(gproj_v[...], win_v[pl.ds(k * CHUNK, CHUNK)])).astype(BF16)
                for step in range(1, RING):
                    grad_copy(step, k).start()
                grad_own(k).start()
                if k == 0:
                    take(late, 0)
                    go(swap(late, 1))
            take(early, 1)
            take(late, 1)
            for stage in range(2, 5):
                go(swap(every, stage))
                take(every, stage)
            sums_out[...] = sum_v[5]

    def part(to):
        return pl.ds(pl.multiple_of(to * QUARTER, QUARTER), QUARTER)

    def act_copy(step):
        to = lax.rem(z + step, RING)
        return remote(act_row.at[part(to)], act_out.at[z], a_s.at[step], a_r.at[step], (s, to))

    def act_own():
        held = gm_v.at[pl.ds(0, QUARTER)]
        return fetch(act_row.at[part(z)], held, own_sem.at[0]), fetch(held, act_out.at[z], own_sem.at[0])

    def grad_copy(step, k):
        to, cols = lax.rem(z + step, RING), pl.ds(k * CHUNK, CHUNK)
        return remote(out_v.at[part(to), cols], grad_out.at[z, :, cols], o_s.at[0], o_r.at[step, k], (s, to))

    def grad_own(k):
        cols = pl.ds(k * CHUNK, CHUNK)
        return fetch(out_v.at[part(z), cols], grad_out.at[z, :, cols], own_sem.at[1 + k])

    top = LAYERS - 1
    cot = fetch(cot_row, out_v, row_sem.at[2])
    cot.start()
    start(norm_loads(top)[1::2])
    start(block_loads(top, 0))
    start(block_loads(top, 1))
    greet(near_x, near_y, twin, s, z)
    act_own()[0].start()
    sum_v[0] = jnp.zeros((TOTAL_ROWS, WIDTH), F32)
    cot.wait()
    for l in layers:
        layer_back(l, l == 0)
    for step in range(1, RING):
        act_copy(step).wait_recv()
    for k in range(WIDTH // CHUNK):
        grad_own(k).wait()
        for step in range(1, RING):
            grad_copy(step, k).wait_recv()
    for copy in sent:
        copy.wait_send()
    whole = out_v.at[pl.ds(0, SLOTS - QUARTER)]
    remote(whole, whole, o_s.at[0], o_r.at[1, 0], twin).wait_send()


def backward(gains, weights, saved, cot_row, act_row):
    shape = jax.ShapeDtypeStruct
    dma = pltpu.SemaphoreType.DMA
    vmem = lambda *dims_type: pltpu.VMEM(dims_type[:-1], dims_type[-1])
    rows = TOTAL_ROWS
    chunks = WIDTH // CHUNK
    anywhere = pl.BlockSpec(memory_space=pl.ANY)
    inside = pl.BlockSpec(memory_space=pltpu.VMEM)
    return pl.pallas_call(
        backward_kernel,
        out_shape=(
            shape((RING, QUARTER, WIDTH), BF16), shape((RING, QUARTER, WIDTH), BF16), shape((rows, WIDTH), F32),
        ),
        in_specs=[inside] * 2 + [anywhere] * 12,
        out_specs=[anywhere, anywhere, inside],
        scratch_shapes=[
            vmem(SLOTS, WIDTH, F32), vmem(SLOTS, WIDTH, F32), vmem(SLOTS, WIDTH, F32),
            vmem(SLOTS, WIDTH, BF16), vmem(SLOTS, WIDTH, BF16), vmem(SLOTS, WIDTH, BF16), vmem(8, 128, BF16),
            vmem(SLOTS, 3 * WIDTH, BF16), vmem(SLOTS, WIDTH, BF16),
            vmem(2, SLOTS, WIDTH, BF16), vmem(2, SLOTS, 128, F32), vmem(2, SLOTS, WIDTH, BF16),
            vmem(SLOTS, 3 * WIDTH, BF16), vmem(SLOTS, WIDTH, F32),
            vmem(4, 2, SLOTS, SLOTS, BF16), vmem(4, SLOTS, 128, F32),
            vmem(2, 2, WIDTH, WIDTH, BF16), vmem(WIDTH, WIDTH, BF16), vmem(WIDTH, 3 * WIDTH, BF16),
            vmem(2, 8, WIDTH, F32), vmem(6, rows, WIDTH, F32), vmem(5, rows, WIDTH, F32),
            dma((RING,)), dma((RING,)), dma((1,)), dma((RING, chunks)),
            dma((2, 5)), dma((2, 5)),
            dma((2, 2)), dma((2,)), dma((4,)), dma((2,)), dma((4, 2)), dma((3,)), dma((1 + chunks,)),
        ],
        compiler_params=pltpu.CompilerParams(
            collective_id=1, has_side_effects=True, vmem_limit_bytes=60 << 20
        ),
        cost_estimate=pl.CostEstimate(flops=40 * 10**9, bytes_accessed=100 << 20, transcendentals=10**6),
    )(*gains, *weights, cot_row, act_row, *saved)


def deliver_kernel(act_ref, grad_ref, sums_ref, act_out, grad_out, *small_outs):
    act_out[...] = act_ref[...]
    grad_out[...] = grad_ref[...].astype(F32)

    @pl.when(pl.program_id(0) == 0)
    def _():
        for out, kind in zip(small_outs, (0, 1, 2, 3, 6, 4, 5)):
            for l in range(LAYERS):
                for k in range(out.shape[1] // WIDTH):
                    at = sum_row(l, kind + k)
                    out[l:l + 1, k * WIDTH:(k + 1) * WIDTH] = sums_ref[at:at + 1]


def deliver(activations, grad, sums):
    shape = jax.ShapeDtypeStruct
    whole = lambda *dims: pl.BlockSpec(dims, lambda i: (0,) * len(dims))
    block = pl.BlockSpec((RING // 2, QUARTER, WIDTH), lambda i: (i, 0, 0))
    widths = [WIDTH] * 4 + [RING * WIDTH] + [WIDTH] * 2
    return pl.pallas_call(
        deliver_kernel,
        grid=(2,),
        out_shape=[shape(grad.shape, BF16), shape(grad.shape, F32)] + [shape((LAYERS, w), F32) for w in widths],
        in_specs=[block, block, whole(TOTAL_ROWS, WIDTH)],
        out_specs=[block, block] + [whole(LAYERS, w) for w in widths],
    )(activations, grad, sums)


def whole_rows(
    tokens, lengths, separators, type_table, project_in, project_out, up_weight, down_weight, first_norm_gain,
    second_norm_gain, query_bias, value_bias, output_bias, first_norm_bias, hidden_bias, down_bias,
    second_norm_bias, cotangent,
):
    small = (
        type_table, first_norm_gain, second_norm_gain, query_bias, value_bias, output_bias, first_norm_bias,
        hidden_bias, down_bias, second_norm_bias,
    )
    g_in, g_out, g_ff, cot_row, act_row, *saved = forward(
        lengths, separators, tokens, cotangent, project_in, project_out, up_weight, down_weight, small
    )
    weights = (
        g_in.reshape(LAYERS, WIDTH, 3 * WIDTH),
        g_out.reshape(LAYERS, WIDTH, WIDTH),
        g_ff.reshape(LAYERS, RING, 2, WIDTH, WIDTH),
    )
    return tuple(deliver(*backward((first_norm_gain, second_norm_gain), weights, saved, cot_row, act_row)))


def layer_norm(total, gain, bias):
    mean = jnp.mean(total, -1, keepdims=True)
    centered = total - mean
    spread = jnp.mean(centered * centered, -1, keepdims=True)
    return centered * lax.rsqrt(spread + EPS) * gain + bias


def gelu_exact(value):
    return jax.nn.gelu(value, approximate=False)


def contract_last(left, right):
    return lax.dot_general(
        left, right, (((1,), (1,)), ((), ())), preferred_element_type=jnp.float32
    )


def split_heads(block):
    return block.reshape(block.shape[0], -1, HEAD_DIM)


def masked_scores(queries, keys, length):
    scores = jnp.einsum(
        "qhd,khd->hqk", queries, keys, preferred_element_type=jnp.float32
    ) * HEAD_DIM ** (-0.5)
    valid = jnp.arange(keys.shape[0]) < length
    return jnp.where(valid[None, None, :], scores, MASKED)


def attend_forward(packed):
    projected, length = packed
    slots = projected.shape[0]
    queries = split_heads(projected[:, 0])
    keys = split_heads(projected[:, 1])
    values = split_heads(projected[:, 2])
    scores = masked_scores(queries, keys, length)
    peak = jnp.max(scores, -1, keepdims=True)
    expo = jnp.exp(scores - peak)
    total = jnp.sum(expo, -1, keepdims=True)
    probs = (expo / total).astype(jnp.bfloat16)
    mixed = jnp.einsum("hqk,khd->qhd", probs, values, preferred_element_type=jnp.float32)
    return (mixed.astype(jnp.bfloat16).reshape(slots, -1), (peak + jnp.log(total))[:, :, 0])


def attend_backward(packed):
    projected, length, log_total, grad_mixed = packed
    slots = projected.shape[0]
    queries = split_heads(projected[:, 0])
    keys = split_heads(projected[:, 1])
    values = split_heads(projected[:, 2])
    scores = masked_scores(queries, keys, length)
    probs = jnp.exp(scores - log_total[:, :, None])
    grad_out = split_heads(grad_mixed)
    grad_probs = jnp.einsum("qhd,khd->hqk", grad_out, values, preferred_element_type=jnp.float32)
    inner = jnp.sum(grad_probs * probs, -1, keepdims=True)
    grad_scores = (probs * (grad_probs - inner)).astype(jnp.bfloat16)
    scale = HEAD_DIM ** (-0.5)
    grad_queries = (
        jnp.einsum("hqk,khd->qhd", grad_scores, keys, preferred_element_type=jnp.float32) * scale
    )
    grad_keys = (
        jnp.einsum("hqk,qhd->khd", grad_scores, queries, preferred_element_type=jnp.float32) * scale
    )
    grad_values = jnp.einsum(
        "hqk,qhd->khd", probs.astype(jnp.bfloat16), grad_out, preferred_element_type=jnp.float32
    )
    stacked = jnp.stack([grad_queries, grad_keys, grad_values], 1)
    return stacked.reshape(slots, 3, -1).astype(jnp.bfloat16)


def feed_forward(rows, up_part, down_part, bias_part):
    hidden = jnp.dot(rows, up_part, preferred_element_type=jnp.float32) + bias_part
    active = gelu_exact(hidden).astype(jnp.bfloat16)
    return jnp.dot(active, down_part, preferred_element_type=jnp.float32)


def split_heads_plan(
    tokens,
    lengths,
    separators,
    type_table,
    project_in,
    project_out,
    up_weight,
    down_weight,
    first_norm_gain,
    second_norm_gain,
    query_bias,
    value_bias,
    output_bias,
    first_norm_bias,
    hidden_bias,
    down_bias,
    second_norm_bias,
    cotangent,
):
    row_count, slot_part, width = tokens.shape
    token_count = row_count * slot_part
    hidden_part = up_weight.shape[2]
    offset = lax.axis_index("head") * hidden_part
    positions = lax.axis_index("head") * slot_part + jnp.arange(slot_part)
    second = (positions[None, :] > separators[:, None]) & (positions[None, :] < lengths[:, None])
    state = tokens.astype(jnp.float32) + jnp.where(second[:, :, None], type_table[1], type_table[0])
    state = state.reshape(token_count, width)

    def fetch(layer):
        gathered = (
            lax.all_gather(project_in[layer], "seq", axis=0, tiled=True),
            lax.all_gather(project_out[layer], "seq", axis=0, tiled=True),
            lax.all_gather(up_weight[layer], "seq", axis=0, tiled=True),
            lax.all_gather(down_weight[layer], "seq", axis=1, tiled=True),
        )
        return (gathered[0], gathered[1], gathered[2], gathered[3])

    def layer_hidden_bias(layer):
        return lax.dynamic_slice_in_dim(hidden_bias[layer], offset, hidden_part, 0)

    saved = []
    for layer in range(LAYERS):
        weights = fetch(layer)
        inner_in, inner_out, up_part, down_part = weights
        joined = jnp.concatenate(
            [query_bias[layer], jnp.zeros_like(query_bias[layer]), value_bias[layer]]
        )
        projected = (
            jnp.dot(state.astype(jnp.bfloat16), inner_in, preferred_element_type=jnp.float32)
            + joined
        ).astype(jnp.bfloat16)
        heads = lax.all_to_all(
            projected.reshape(row_count, slot_part, 3, width),
            "head",
            split_axis=3,
            concat_axis=1,
            tiled=True,
        )
        mixed, log_total = lax.map(attend_forward, (heads, lengths))
        mixed = lax.all_to_all(mixed, "head", split_axis=1, concat_axis=2, tiled=True).reshape(
            token_count, width
        )
        first_sum = (
            state
            + jnp.dot(mixed, inner_out, preferred_element_type=jnp.float32)
            + output_bias[layer]
        )
        normed = layer_norm(first_sum, first_norm_gain[layer], first_norm_bias[layer])
        normed_low = normed.astype(jnp.bfloat16)
        bias_part = layer_hidden_bias(layer)
        rows_all = lax.all_gather(normed_low[None], "head", axis=0, tiled=True).reshape(-1, width)
        branch_out = lax.psum_scatter(
            feed_forward(rows_all, up_part, down_part, bias_part).astype(jnp.bfloat16),
            "head",
            scatter_dimension=0,
            tiled=True,
        ).astype(jnp.float32)
        second_sum = normed + branch_out + down_bias[layer]
        saved.append((heads, log_total, first_sum, second_sum, rows_all))
        state = layer_norm(second_sum, second_norm_gain[layer], second_norm_bias[layer])
    activations = state.astype(jnp.bfloat16).reshape(row_count, slot_part, width)
    grad = cotangent.astype(jnp.float32).reshape(token_count, width)
    query_grads = [None] * LAYERS
    value_grads = [None] * LAYERS
    output_grads = [None] * LAYERS
    first_grads = [None] * LAYERS
    hidden_grads = [None] * LAYERS
    down_grads = [None] * LAYERS
    second_grads = [None] * LAYERS
    for layer in reversed(range(LAYERS)):
        heads, log_total, first_sum, second_sum, rows_all = saved[layer]
        weights = fetch(layer)
        inner_in, inner_out, up_part, down_part = weights
        second_grads[layer] = jnp.sum(grad, 0)
        _, norm_back = jax.vjp(
            functools.partial(layer_norm, gain=second_norm_gain[layer], bias=second_norm_bias[layer]),
            second_sum,
        )
        grad_second = norm_back(grad)[0]
        down_grads[layer] = jnp.sum(grad_second, 0)
        grad_low = grad_second.astype(jnp.bfloat16)
        bias_part = layer_hidden_bias(layer)
        grad_rows = lax.all_gather(grad_low[None], "head", axis=0, tiled=True).reshape(-1, width)
        hidden = jnp.dot(rows_all, up_part, preferred_element_type=jnp.float32) + bias_part
        grad_active = contract_last(grad_rows, down_part)
        _, gelu_back = jax.vjp(gelu_exact, hidden)
        grad_hidden = gelu_back(grad_active)[0]
        hidden_local = jnp.sum(grad_hidden, 0)
        grad_hidden_low = grad_hidden.astype(jnp.bfloat16)
        hidden_grads[layer] = lax.dynamic_update_slice_in_dim(
            jnp.zeros_like(hidden_bias[layer]), hidden_local, offset, 0
        )
        grad_normed = grad_second + lax.psum_scatter(
            contract_last(grad_hidden_low, up_part).astype(jnp.bfloat16),
            "head",
            scatter_dimension=0,
            tiled=True,
        ).astype(jnp.float32)
        first_grads[layer] = jnp.sum(grad_normed, 0)
        _, norm_back = jax.vjp(
            functools.partial(layer_norm, gain=first_norm_gain[layer], bias=first_norm_bias[layer]), first_sum
        )
        grad_first = norm_back(grad_normed)[0]
        output_grads[layer] = jnp.sum(grad_first, 0)
        grad_mixed = contract_last(grad_first.astype(jnp.bfloat16), inner_out).astype(jnp.bfloat16)
        grad_heads = lax.all_to_all(
            grad_mixed.reshape(row_count, slot_part, width),
            "head",
            split_axis=2,
            concat_axis=1,
            tiled=True,
        )
        grad_projected = lax.map(attend_backward, (heads, lengths, log_total, grad_heads))
        grad_projected = lax.all_to_all(
            grad_projected, "head", split_axis=1, concat_axis=3, tiled=True
        ).reshape(token_count, 3 * width)
        query_grads[layer] = jnp.sum(grad_projected[:, :width], 0, dtype=jnp.float32)
        value_grads[layer] = jnp.sum(grad_projected[:, 2 * width :], 0, dtype=jnp.float32)
        grad = grad_first + contract_last(grad_projected, inner_in)
    summed = lax.psum(
        (
            jnp.stack(query_grads),
            jnp.stack(value_grads),
            jnp.stack(output_grads),
            jnp.stack(first_grads),
            jnp.stack(hidden_grads),
            jnp.stack(down_grads),
            jnp.stack(second_grads),
        ),
        ("seq", "head"),
    )
    input_grad = grad.reshape(row_count, slot_part, width)
    return (
        activations,
        input_grad,
        summed[0],
        summed[1],
        summed[2],
        summed[3],
        summed[4],
        summed[5],
        summed[6],
    )


def solution(mesh):
    placed = (
        P("seq", "head", None),
        P("seq"),
        P("seq"),
        P(),
        P(None, "seq", None),
        P(None, "seq", None),
        P(None, "seq", "head"),
        P(None, "head", "seq"),
        P(),
        P(),
        P(),
        P(),
        P(),
        P(),
        P(),
        P(),
        P(),
        P("seq", "head", None),
    )
    shape = dict(mesh.shape)
    fits = shape == {"seq": 8, "head": RING}
    return jax.shard_map(
        whole_rows if fits else split_heads_plan,
        mesh=mesh,
        in_specs=placed,
        out_specs=(
            P("seq", "head", None),
            P("seq", "head", None),
            P(),
            P(),
            P(),
            P(),
            P(),
            P(),
            P(),
        ),
        check_vma=False,
    )
```

```python
import functools

import jax
import jax.numpy as jnp
from jax import lax
from jax.experimental import pallas as pl
from jax.experimental.pallas import tpu as pltpu
from jax.sharding import PartitionSpec as P

F32 = jnp.float32
BF16 = jnp.bfloat16
MESH = pl.DeviceIdType.MESH
HEAD_DIM = 64
LAYERS = 2
EPS = 1e-06
MASKED = -1000000000.0
ROOT_HALF = 0.7071067811865476
ROOT_TAU = 0.3989422804014327
RING = 4
WIDTH = 1024
SLOTS = 512
QUARTER = SLOTS // RING
CHUNK = 256


def nn(left, right):
    return jnp.dot(left, right, preferred_element_type=F32)


def nt(left, right):
    return lax.dot_general(left, right, (((1,), (1,)), ((), ())), preferred_element_type=F32)


def tn(left, right):
    return lax.dot_general(left, right, (((0,), (0,)), ((), ())), preferred_element_type=F32)


def place():
    s, z = lax.axis_index("seq"), lax.axis_index("head")
    c, x, y = lax.rem(s, 2), lax.rem(lax.div(s, 2), 2), lax.div(s, 4)
    return s, z, c, x, y


def peers(s, z, c, x, y):
    return (s + 2 - 4 * x, z), (s + 4 - 8 * y, z), (s + 1 - 2 * c, z)


def greet(near_x, near_y, twin, s, z):
    barrier = pltpu.get_barrier_semaphore()
    for device in [(s, lax.rem(z + step, RING)) for step in (2, 1, 3)] + [near_x, near_y, twin]:
        pl.semaphore_signal(barrier, inc=1, device_id=device, device_id_type=MESH)


def greeted():
    pl.semaphore_wait(pltpu.get_barrier_semaphore(), 3 + RING - 1)


def forward_kernel(
    lengths_ref, separators_ref,
    tokens_ref, cot_ref, in_ref, out_ref, up_ref, down_ref,
    table_in, gain1_in, gain2_in, qb_in, vb_in, ob_in, b1_in, hb_in, db_in, b2_in,
    g_in, g_out, g_ff, cot_row, act_row, s_qkv, s_mix, s_expo, s_inv, s_n, s_rs, s_gp,
    table_ref, gain1_ref, gain2_ref, qb_ref, vb_ref, ob_ref, b1_ref, hb_ref, db_ref, b2_ref, down_v,
    tok_v, state_v, xb_v, qkv_v, mix_v, mixed_v, n_v, rs_v, normed_v, acc_v, active_v, gp_v, e_v, inv_v, w_v, f_v, dn_v, up_v, in_v, out_v, cot_v,
    tok_s, tok_r, cot_s, cot_r, at_s, at_r, ff_s, ff_r, z_s, z_r, f_s, f_r, cc_s, cc_r,
    small_sem, own_sem, put_sem, ld_sem, w_sem, save_sem, e_sem, gp_sem,
):
    s, z, c, x, y = place()
    near_x, near_y, twin = peers(s, z, c, x, y)
    half = QUARTER // 2
    A, B = pl.ds(0, half), pl.ds(half, half)
    every = slice(None)
    sent = []

    def remote(src, dst, ss, rs, device):
        return pltpu.make_async_remote_copy(
            src_ref=src, dst_ref=dst, send_sem=ss, recv_sem=rs, device_id=device, device_id_type=MESH
        )

    def go(copy):
        copy.start()
        sent.append(copy)

    small_in = [
        pltpu.make_async_copy(src, dst, small_sem.at[k]) for k, (src, dst) in enumerate((
            (down_ref, down_v), (table_in, table_ref), (gain1_in, gain1_ref), (gain2_in, gain2_ref),
            (qb_in, qb_ref), (vb_in, vb_ref), (ob_in, ob_ref), (b1_in, b1_ref), (hb_in, hb_ref),
            (db_in, db_ref), (b2_in, b2_ref),
        ))
    ]

    def own_in(l):
        return [
            pltpu.make_async_copy(ref.at[l], held.at[l], own_sem.at[l, t])
            for t, (ref, held) in enumerate(((up_ref, up_v), (in_ref, in_v), (out_ref, out_v)))
        ]

    def own_out(l):
        places = (
            (up_v, g_ff.at[l, z, 0, y, x, c]), (in_v, g_in.at[l, y, x, c]), (out_v, g_out.at[l, y, x, c]),
            (dn_v, g_ff.at[l, z, 1, y, x, c]),
        )
        return [pltpu.make_async_copy(held.at[l], dst, put_sem.at[l, t]) for t, (held, dst) in enumerate(places)]

    gathered = (g_in, g_out)
    shard = (in_ref, out_ref)

    def at_first(l, t):
        g = gathered[t]
        return (
            remote(shard[t].at[l, A], g.at[l, y, x, c, A], at_s.at[l, t, 0], at_r.at[l, t, 0], near_x),
            remote(shard[t].at[l, B], g.at[l, y, x, c, B], at_s.at[l, t, 1], at_r.at[l, t, 1], near_y),
        )

    def at_last(l, t):
        g = gathered[t]
        pair, pile = g.at[l, y, every, c, A], g.at[l, every, x, c, B]
        return (
            remote(pair, pair, at_s.at[l, t, 2], at_r.at[l, t, 2], near_y),
            remote(pile, pile, at_s.at[l, t, 3], at_r.at[l, t, 3], near_x),
        )

    def at_core(l, t, side):
        part = gathered[t].at[l, every, every, c, (A, B)[side]]
        return remote(part, part, at_s.at[l, t, 4 + side], at_r.at[l, t, 4 + side], twin)

    def at_send(l, t):
        for copy in at_first(l, t):
            go(copy)

    def at_pass(l, t, side):
        at_first(l, t)[side].wait_recv()
        go(at_last(l, t)[side])

    def at_share(l, t, side):
        at_last(l, t)[side].wait_recv()
        go(at_core(l, t, side))

    def at_ready(l, t):
        for side in range(2):
            at_core(l, t, side).wait_recv()

    def rank(i):
        near = z if i == 0 else None
        if i == 0:
            return near
        low = jnp.where(z < 2, z, RING - 1 - z)
        block = (1 - low) if i == 1 else i
        return jnp.where(z < 2, block, RING - 1 - block)

    def ff_part(l, block, side, kind):
        return g_ff.at[l, block, kind, y, every, c, A] if side == 0 else g_ff.at[l, block, kind, every, x, c, B]

    def ff_first(l, side, kind):
        part = g_ff.at[l, z, kind, y, x, c, (A, B)[side]]
        return remote(part, part, ff_s.at[l, side, kind], ff_r.at[l, side, kind], (near_x, near_y)[side])

    def ff_z(l, block, side, kind, way):
        part = ff_part(l, block, side, kind)
        beside = lax.rem(z + 1, RING) if way == 0 else lax.rem(z + RING - 1, RING)
        return remote(part, part, z_s.at[way], z_r.at[l, block, side, kind], (s, beside))

    def ff_last(l, block, side, kind):
        part = ff_part(l, block, side, kind)
        return remote(part, part, f_s.at[0], f_r.at[l, block, side, kind], (near_y, near_x)[side])

    def ff_core(l, block, side, kind):
        part = g_ff.at[l, block, kind, every, every, c, (A, B)[side]]
        return remote(part, part, cc_s.at[0], cc_r.at[l, block, side, kind], twin)

    right = z < RING - 1
    left = z > 0

    def ff_send(l):
        for kind in range(2):
            for side in range(2):
                go(ff_first(l, side, kind))

    def ff_spread(l, side, kind):
        ff_first(l, side, kind).wait_recv()
        pl.when(right)(ff_z(l, z, side, kind, 0).start)
        pl.when(left)(ff_z(l, z, side, kind, 1).start)

    def ff_cross(l, i, side, kind):
        ff_last(l, rank(i), side, kind).start()

    def ff_relay(l, i, side, kind):
        block = rank(i)
        ff_z(l, block, side, kind, 0).wait_recv()
        pl.when(jnp.logical_and(block < z, right))(ff_z(l, block, side, kind, 0).start)
        pl.when(jnp.logical_and(block > z, left))(ff_z(l, block, side, kind, 1).start)

    def ff_share(l, i, side, kind):
        ff_last(l, rank(i), side, kind).wait_recv()
        ff_core(l, rank(i), side, kind).start()

    def ff_load(l, i, side, kind, parity):
        part = (every, every, c if parity == 0 else 1 - c, (A, B)[side])
        return pltpu.make_async_copy(
            g_ff.at[(l, rank(i), kind) + part], f_v.at[(kind, i) + part], ld_sem.at[kind, i, side, parity]
        )

    def ff_hold(l, i, side, kind):
        ff_load(l, i, side, kind, 0).start()

    def ff_take(l, i, kind):
        for side in range(2):
            ff_core(l, rank(i), side, kind).wait_recv()
            ff_load(l, i, side, kind, 1).start()

    def ff_held(l, i, kind):
        for side in range(2):
            for parity in range(2):
                ff_load(l, i, side, kind, parity).wait()

    def ff_drain():
        def drain(part, sem):
            remote(part, part, sem, z_r.at[0, 0, 0, 0], twin).wait_send()

        drain(g_ff.at[0, every, 0], f_s.at[0])
        drain(g_ff.at[0], cc_s.at[0])
        for blocks in range(1, RING):
            pl.when(z == blocks - 1)(functools.partial(drain, g_ff.at[0, pl.ds(0, blocks), 0], z_s.at[0]))
            pl.when(z == RING - blocks)(functools.partial(drain, g_ff.at[0, pl.ds(0, blocks), 0], z_s.at[1]))

    def row_copies(src, dst, ss, rs):
        here = dst.at[pl.ds(pl.multiple_of(z * QUARTER, QUARTER), QUARTER)]
        copies = []
        for step in range(1, RING):
            to = lax.rem(z + step, RING)
            copies.append(remote(src.at[to], here, ss.at[step], rs.at[step], (s, to)))
        return copies, here

    def load(slot, src, width=WIDTH):
        copy = pltpu.make_async_copy(src, w_v.at[slot], w_sem.at[slot])
        copy.start()
        return copy

    def weight(slot, cols):
        return w_v[slot, :, :, :, :, cols].reshape(WIDTH, CHUNK)

    saves = {}

    def save(key, src, dst, sem):
        copy = pltpu.make_async_copy(src, dst, sem)
        copy.start()
        saves[key] = copy

    def settle(key):
        if key in saves:
            saves.pop(key).wait()

    def rows_loop(body, rows=64):
        def step(r, carry):
            body(pl.ds(pl.multiple_of(r * rows, rows), rows), r * rows)
            return carry
        lax.fori_loop(0, SLOTS // rows, step, 0)

    def norm_rows(total, gain, bias, rr, which):
        mean = jnp.sum(total, -1, keepdims=True) * (1.0 / WIDTH)
        centered = total - mean
        rs = lax.rsqrt(jnp.sum(centered * centered, -1, keepdims=True) * (1.0 / WIDTH) + EPS)
        n = centered * rs
        n_v[which, rr] = n.astype(BF16)
        rs_v[which, rr] = rs + jnp.zeros((64, 128), F32)
        return n * gain + bias

    def start_state():
        length, split = lengths_ref[z], separators_ref[z]

        def body(rr, base):
            pos = lax.broadcasted_iota(jnp.int32, (64, 1), 0) + base
            second = jnp.logical_and(pos > split, pos < length)
            kind = jnp.where(second, table_ref[1:2], table_ref[0:1])
            value = tok_v[rr].astype(F32) + kind
            state_v[rr] = value
            xb_v[rr] = value.astype(BF16)
        rows_loop(body)

    loading = {}

    def fetch_in(l):
        at_ready(l, 0)
        loading["in"] = [load(j, g_in.at[l, :, :, :, :, pl.ds(j * WIDTH, WIDTH)]) for j in range(3)]

    def fetch_out(l):
        at_ready(l, 1)
        loading["out"] = load(3, g_out.at[l])

    def project(l):
        settle("qkv")
        loads = loading.pop("in")
        for j in range(3):
            loads[j].wait()
            for k in range(WIDTH // CHUNK):
                cols = pl.ds(k * CHUNK, CHUNK)
                value = nn(xb_v[...], weight(j, cols))
                if j == 0:
                    value = (value + qb_ref[l:l + 1, k * CHUNK:(k + 1) * CHUNK]).astype(BF16) * BF16(HEAD_DIM ** -0.5)
                elif j == 2:
                    value = value + vb_ref[l:l + 1, k * CHUNK:(k + 1) * CHUNK]
                qkv_v[:, pl.ds(j * WIDTH + k * CHUNK, CHUNK)] = value.astype(BF16)
        save("qkv", qkv_v, s_qkv.at[l], save_sem.at[0])

    pairs = WIDTH // (2 * HEAD_DIM)
    wide = 2 * HEAD_DIM

    def attend(l, first, last):
        bias = jnp.where(
            lax.broadcasted_iota(jnp.int32, (1, SLOTS), 1) < lengths_ref[z], 0.0, MASKED
        ).astype(F32)
        lane = lax.broadcasted_iota(jnp.int32, (SLOTS, wide), 1) < HEAD_DIM

        def e_save(p, slot):
            return (
                pltpu.make_async_copy(e_v.at[slot], s_expo.at[l, p], e_sem.at[slot, 0]),
                pltpu.make_async_copy(inv_v.at[slot], s_inv.at[l, p], e_sem.at[slot, 1]),
            )

        def step(p, carry):
            slot = lax.rem(p, 2)

            @pl.when(p >= 2)
            def _():
                for copy in e_save(p - 2, slot):
                    copy.wait()

            q = qkv_v[:, pl.ds(pl.multiple_of(p * wide, wide), wide)]
            k = qkv_v[:, pl.ds(pl.multiple_of(WIDTH + p * wide, wide), wide)]
            v = qkv_v[:, pl.ds(pl.multiple_of(2 * WIDTH + p * wide, wide), wide)]
            mine = (jnp.where(lane, q, jnp.zeros_like(q)), jnp.where(lane, jnp.zeros_like(q), q))
            scores = [nt(mine[h], k) + bias for h in range(2)]
            expo = [jnp.exp(part - jnp.max(part, -1, keepdims=True)) for part in scores]
            invs = [1.0 / jnp.sum(part, -1, keepdims=True) for part in expo]
            expo = [part.astype(BF16) for part in expo]
            for h in range(2):
                e_v[slot, h] = expo[h]
            outs = [nn(expo[h], v) * invs[h] for h in range(2)]
            inv_v[slot] = jnp.where(lane, invs[0], invs[1])
            mixed = jnp.where(lane, outs[0], outs[1])
            mixed_v[:, pl.ds(pl.multiple_of(p * wide, wide), wide)] = mixed
            mix_v[:, pl.ds(pl.multiple_of(p * wide, wide), wide)] = mixed.astype(BF16)
            for copy in e_save(p, slot):
                copy.start()
            return carry

        lax.fori_loop(first, last, step, 0)
        if last == pairs:
            for p in (pairs - 2, pairs - 1):
                for copy in e_save(p, p % 2):
                    copy.wait()

    def attention_out(l):
        loading.pop("out").wait()
        for k in range(WIDTH // CHUNK):
            cols = pl.ds(k * CHUNK, CHUNK)
            acc_v[:, cols] = nn(mix_v[...], weight(3, cols))
        settle("mix")
        save("mix", mixed_v, s_mix.at[l], save_sem.at[1])
        settle("n0")
        settle("rs0")

        def body(rr, base):
            total = state_v[rr] + acc_v[rr] + ob_ref[l:l + 1]
            value = norm_rows(total, gain1_ref[l:l + 1], b1_ref[l:l + 1], rr, 0)
            normed_v[rr] = value
            xb_v[rr] = value.astype(BF16)
        rows_loop(body)
        save("n0", n_v.at[0], s_n.at[l, 0], save_sem.at[2])
        save("rs0", rs_v.at[0], s_rs.at[l, 0], save_sem.at[3])

    def feed_up(l, i):
        block = rank(i)
        ff_held(l, i, 0)
        settle(("gp", i % 2))
        for k in range(WIDTH // CHUNK):
            cols = pl.ds(k * CHUNK, CHUNK)
            shift = hb_ref[l:l + 1, pl.ds(pl.multiple_of(block * WIDTH + k * CHUNK, CHUNK), CHUNK)]
            hidden = nn(xb_v[...], f_v[0, i, :, :, :, :, cols].reshape(WIDTH, CHUNK)) + shift
            share = 0.5 + 0.5 * lax.erf(hidden * ROOT_HALF)
            active_v[:, cols] = (hidden * share).astype(BF16)
            slope = share + hidden * (jnp.exp(hidden * hidden * -0.5) * ROOT_TAU)
            gp_v[i % 2, :, cols] = slope.astype(BF16)
        save(("gp", i % 2), gp_v.at[i % 2], s_gp.at[l, block], gp_sem.at[i % 2])

    def feed_down(l, i):
        ff_held(l, i, 1)
        for k in range(2):
            cols = pl.ds(k * SLOTS, SLOTS)
            value = nt(active_v[...], f_v[1, i, k].reshape(SLOTS, WIDTH))
            if i == 0:
                acc_v[:, cols] = value
            else:
                acc_v[:, cols] += value

    def finish(l):
        settle("n1")
        settle("rs1")

        def body(rr, base):
            total = normed_v[rr] + acc_v[rr] + db_ref[l:l + 1]
            value = norm_rows(total, gain2_ref[l:l + 1], b2_ref[l:l + 1], rr, 1)
            state_v[rr] = value
            xb_v[rr] = value.astype(BF16)
        rows_loop(body)
        save("n1", n_v.at[1], s_n.at[l, 1], save_sem.at[4])
        save("rs1", rs_v.at[1], s_rs.at[l, 1], save_sem.at[5])

    for l in range(LAYERS):
        for copy in own_in(l):
            copy.start()
    for copy in small_in:
        copy.start()
    cot_in = pltpu.make_async_copy(cot_ref.at[z], cot_v, save_sem.at[7])
    cot_in.start()
    greet(near_x, near_y, twin, s, z)
    small_in[0].wait()
    for l in range(LAYERS):
        dn_v[l] = down_v[l].T
    for l in range(LAYERS):
        for copy in own_in(l):
            copy.wait()
        for copy in own_out(l):
            copy.start()
    greeted()
    at_send(0, 0)
    at_send(0, 1)
    tok_copies, tok_here = row_copies(tokens_ref, tok_v, tok_s, tok_r)
    for copy in tok_copies:
        go(copy)
    tok_own = pltpu.make_async_copy(tokens_ref.at[z], tok_here, tok_s.at[0])
    tok_own.start()
    own_out(0)[0].wait()
    own_out(0)[3].wait()
    ff_send(0)
    own_out(0)[1].wait()
    at_pass(0, 0, 0)
    at_send(1, 1)
    ff_spread(0, 0, 1)
    own_out(1)[0].wait()
    own_out(1)[3].wait()
    ff_send(1)
    at_pass(0, 0, 1)
    ff_spread(0, 1, 1)
    ff_spread(0, 0, 0)
    at_send(1, 0)
    ff_cross(0, 0, 1, 1)
    ff_spread(0, 1, 0)
    ff_relay(0, 2, 0, 1)
    for copy in small_in[1:]:
        copy.wait()
    tok_own.wait()
    for copy in tok_copies:
        copy.wait_recv()
    start_state()
    own_out(0)[2].wait()
    at_pass(0, 1, 0)
    ff_relay(0, 1, 0, 0)
    ff_relay(0, 1, 0, 1)
    at_share(0, 0, 1)
    ff_relay(0, 1, 1, 0)
    ff_cross(0, 1, 0, 1)
    ff_relay(0, 1, 1, 1)
    ff_relay(0, 2, 0, 0)
    ff_cross(0, 2, 0, 0)
    ff_cross(0, 0, 0, 0)
    ff_cross(0, 1, 1, 0)
    ff_cross(0, 2, 0, 1)
    ff_cross(0, 0, 1, 0)
    ff_cross(0, 0, 0, 1)
    at_pass(0, 1, 1)
    ff_relay(0, 2, 1, 1)
    at_share(0, 0, 0)
    ff_relay(0, 2, 1, 0)
    ff_cross(0, 2, 1, 1)
    ff_relay(0, 3, 0, 0)
    ff_relay(0, 3, 0, 1)
    ff_share(0, 2, 0, 0)
    ff_hold(0, 2, 0, 0)
    ff_share(0, 0, 1, 1)
    ff_hold(0, 0, 1, 1)
    ff_cross(0, 1, 1, 1)
    ff_share(0, 1, 1, 0)
    ff_hold(0, 1, 1, 0)
    ff_cross(0, 1, 0, 0)
    ff_relay(0, 3, 1, 0)
    ff_cross(0, 3, 1, 0)
    ff_cross(0, 3, 0, 0)
    ff_share(0, 1, 0, 1)
    ff_hold(0, 1, 0, 1)
    ff_cross(0, 3, 0, 1)
    ff_spread(1, 0, 0)
    fetch_in(0)
    project(0)
    ff_cross(0, 2, 1, 0)
    ff_relay(0, 3, 1, 1)
    own_out(1)[1].wait()
    at_pass(1, 0, 1)
    ff_spread(1, 1, 1)
    attend(0, 0, 2)
    ff_share(0, 0, 0, 0)
    ff_hold(0, 0, 0, 0)
    at_pass(1, 0, 0)
    at_share(0, 1, 0)
    at_share(0, 1, 1)
    ff_share(0, 1, 1, 1)
    ff_hold(0, 1, 1, 1)
    ff_share(0, 0, 1, 0)
    ff_hold(0, 0, 1, 0)
    ff_spread(1, 0, 1)
    ff_cross(0, 3, 1, 1)
    ff_relay(1, 1, 0, 0)
    attend(0, 2, 4)
    attend(0, 4, 6)
    ff_cross(1, 0, 0, 0)
    fetch_out(0)
    attend(0, 6, 8)
    ff_share(0, 0, 0, 1)
    ff_hold(0, 0, 0, 1)
    ff_share(0, 3, 1, 0)
    ff_hold(0, 3, 1, 0)
    attention_out(0)
    ff_take(0, 0, 0)
    ff_relay(1, 2, 0, 0)
    ff_share(0, 2, 1, 0)
    ff_hold(0, 2, 1, 0)
    ff_share(0, 1, 0, 0)
    ff_hold(0, 1, 0, 0)
    feed_up(0, 0)
    ff_spread(1, 1, 0)
    ff_cross(1, 0, 0, 1)
    ff_share(0, 3, 0, 1)
    ff_hold(0, 3, 0, 1)
    ff_take(0, 2, 0)
    ff_take(0, 1, 0)
    ff_take(0, 1, 1)
    ff_share(0, 2, 0, 1)
    ff_hold(0, 2, 0, 1)
    ff_relay(1, 1, 1, 1)
    ff_cross(1, 0, 1, 1)
    ff_share(0, 3, 0, 0)
    ff_hold(0, 3, 0, 0)
    ff_share(0, 2, 1, 1)
    ff_hold(0, 2, 1, 1)
    ff_take(0, 0, 1)
    feed_down(0, 0)
    ff_cross(1, 0, 1, 0)
    ff_relay(1, 1, 0, 1)
    ff_cross(1, 1, 0, 1)
    ff_relay(1, 2, 0, 1)
    own_out(1)[2].wait()
    at_pass(1, 1, 0)
    ff_take(0, 3, 0)
    feed_up(0, 1)
    at_share(1, 0, 1)
    at_pass(1, 1, 1)
    feed_down(0, 1)
    ff_take(0, 2, 1)
    ff_share(0, 3, 1, 1)
    ff_hold(0, 3, 1, 1)
    ff_cross(1, 1, 0, 0)
    ff_relay(1, 2, 1, 1)
    ff_relay(1, 1, 1, 0)
    ff_cross(1, 1, 1, 1)
    feed_up(0, 2)
    ff_cross(1, 1, 1, 0)
    ff_take(0, 3, 1)
    at_share(1, 0, 0)
    feed_down(0, 2)
    ff_cross(1, 2, 0, 0)
    feed_up(0, 3)
    ff_relay(1, 2, 1, 0)
    ff_share(1, 0, 0, 0)
    ff_hold(1, 0, 0, 0)
    feed_down(0, 3)
    ff_share(1, 0, 1, 1)
    ff_hold(1, 0, 1, 1)
    fetch_in(1)
    finish(0)
    ff_share(1, 0, 1, 0)
    ff_hold(1, 0, 1, 0)
    ff_relay(1, 3, 0, 0)
    project(1)
    ff_cross(1, 2, 1, 1)
    ff_relay(1, 3, 1, 0)
    ff_share(1, 1, 0, 1)
    ff_hold(1, 1, 0, 1)
    ff_cross(1, 2, 0, 1)
    settle("mix")
    attend(1, 0, 2)
    at_share(1, 1, 1)
    ff_cross(1, 2, 1, 0)
    ff_share(1, 0, 0, 1)
    ff_hold(1, 0, 0, 1)
    attend(1, 2, 4)
    at_share(1, 1, 0)
    ff_relay(1, 3, 1, 1)
    attend(1, 4, 6)
    ff_share(1, 1, 1, 1)
    ff_hold(1, 1, 1, 1)
    ff_cross(1, 3, 1, 0)
    fetch_out(1)
    attend(1, 6, 8)
    ff_relay(1, 3, 0, 1)
    ff_take(1, 0, 0)
    ff_cross(1, 3, 0, 0)
    cot_copies, cot_here = row_copies(cot_ref, cot_row, cot_s, cot_r)
    for copy in cot_copies:
        go(copy)
    cot_in.wait()
    cot_own = pltpu.make_async_copy(cot_v, cot_here, cot_s.at[0])
    cot_own.start()
    ff_share(1, 1, 0, 0)
    ff_hold(1, 1, 0, 0)
    ff_take(1, 0, 1)
    ff_share(1, 2, 0, 0)
    ff_hold(1, 2, 0, 0)
    ff_cross(1, 3, 1, 1)
    ff_share(1, 1, 1, 0)
    ff_hold(1, 1, 1, 0)
    ff_share(1, 2, 1, 1)
    ff_hold(1, 2, 1, 1)
    attention_out(1)
    ff_take(1, 1, 1)
    ff_take(1, 1, 0)
    ff_cross(1, 3, 0, 1)
    feed_up(1, 0)
    ff_share(1, 2, 0, 1)
    ff_hold(1, 2, 0, 1)
    ff_share(1, 2, 1, 0)
    ff_hold(1, 2, 1, 0)
    feed_down(1, 0)
    ff_share(1, 3, 0, 0)
    ff_hold(1, 3, 0, 0)
    ff_share(1, 3, 1, 0)
    ff_hold(1, 3, 1, 0)
    feed_up(1, 1)
    ff_take(1, 2, 0)
    feed_down(1, 1)
    ff_take(1, 2, 1)
    ff_share(1, 3, 0, 1)
    ff_hold(1, 3, 0, 1)
    ff_share(1, 3, 1, 1)
    ff_hold(1, 3, 1, 1)
    feed_up(1, 2)
    ff_take(1, 3, 0)
    feed_down(1, 2)
    ff_take(1, 3, 1)
    feed_up(1, 3)
    feed_down(1, 3)
    finish(1)
    save("act", xb_v, act_row, save_sem.at[6])
    for key in list(saves):
        settle(key)
    cot_own.wait()
    for copy in cot_copies:
        copy.wait_recv()
    for copy in sent:
        copy.wait_send()
    ff_drain()


def forward(lengths, separators, tokens, cotangent, project_in, project_out, up, down, small):
    shape = jax.ShapeDtypeStruct
    dma = pltpu.SemaphoreType.DMA
    vmem = lambda *dims_type: pltpu.VMEM(dims_type[:-1], dims_type[-1])
    L = LAYERS
    pairs = WIDTH // (2 * HEAD_DIM)
    out_shape = (
        shape((L, 2, 2, 2, QUARTER, 3 * WIDTH), BF16),
        shape((L, 2, 2, 2, QUARTER, WIDTH), BF16),
        shape((L, RING, 2, 2, 2, 2, QUARTER, WIDTH), BF16),
        shape((SLOTS, WIDTH), BF16),
        shape((SLOTS, WIDTH), BF16),
        shape((L, SLOTS, 3 * WIDTH), BF16),
        shape((L, SLOTS, WIDTH), F32),
        shape((L, pairs, 2, SLOTS, SLOTS), BF16),
        shape((L, pairs, SLOTS, 2 * HEAD_DIM), F32),
        shape((L, 2, SLOTS, WIDTH), BF16),
        shape((L, 2, SLOTS, 128), F32),
        shape((L, RING, SLOTS, WIDTH), BF16),
    )
    anywhere = pl.BlockSpec(memory_space=pl.ANY)
    scalar = pl.BlockSpec(memory_space=pltpu.SMEM)
    return pl.pallas_call(
        forward_kernel,
        out_shape=out_shape,
        in_specs=[scalar] * 2 + [anywhere] * (6 + len(small)),
        out_specs=[anywhere] * len(out_shape),
        scratch_shapes=[vmem(*a.shape, F32) for a in small] + [
            vmem(*down.shape, BF16), vmem(SLOTS, WIDTH, BF16), vmem(SLOTS, WIDTH, F32), vmem(SLOTS, WIDTH, BF16),
            vmem(SLOTS, 3 * WIDTH, BF16), vmem(SLOTS, WIDTH, BF16), vmem(SLOTS, WIDTH, F32),
            vmem(2, SLOTS, WIDTH, BF16), vmem(2, SLOTS, 128, F32), vmem(SLOTS, WIDTH, F32), vmem(SLOTS, WIDTH, F32),
            vmem(SLOTS, WIDTH, BF16), vmem(2, SLOTS, WIDTH, BF16), vmem(2, 2, SLOTS, SLOTS, BF16),
            vmem(2, SLOTS, 2 * HEAD_DIM, F32), vmem(4, 2, 2, 2, QUARTER, WIDTH, BF16),
            vmem(2, RING, 2, 2, 2, QUARTER, WIDTH, BF16),
            vmem(L, QUARTER, WIDTH, BF16), vmem(L, QUARTER, WIDTH, BF16), vmem(L, QUARTER, 3 * WIDTH, BF16),
            vmem(L, QUARTER, WIDTH, BF16), vmem(QUARTER, WIDTH, BF16),
            dma((RING,)), dma((RING,)), dma((RING,)), dma((RING,)),
            dma((L, 2, 6)), dma((L, 2, 6)), dma((L, 2, 2)), dma((L, 2, 2)),
            dma((2,)), dma((L, RING, 2, 2)), dma((1,)), dma((L, RING, 2, 2)),
            dma((1,)), dma((L, RING, 2, 2)),
            dma((1 + len(small),)), dma((L, 3)), dma((L, 4)), dma((2, RING, 2, 2)), dma((4,)), dma((8,)), dma((2, 2)), dma((2,)),
        ],
        compiler_params=pltpu.CompilerParams(
            collective_id=0, has_side_effects=True, vmem_limit_bytes=60 << 20
        ),
        cost_estimate=pl.CostEstimate(flops=30 * 10**9, bytes_accessed=150 << 20, transcendentals=10**7),
    )(lengths, separators, tokens, cotangent, project_in, project_out, up, down, *small)


TOTAL_ROWS = 32


def sum_row(l, kind):
    if l == 0:
        return kind if kind < 2 else 6 + kind
    return 16 + kind


def backward_kernel(
    gain1_ref, gain2_ref,
    w_in, w_out, w_ff, cot_row, act_row, s_qkv, s_mix, s_expo, s_inv, s_n, s_rs, s_gp,
    act_out, grad_out, sums_out,
    g_v, gs_v, acc_v, low_v, gh_v, gm_v, gp_v, gproj_v, out_v, n_v, rs_v, slope_v, qkv_v, mix_v, e_v, inv_v,
    ff_v, wout_v, win_v, part_v, sum_v, got_v,
    a_s, a_r, o_s, o_r, r_s, r_r,
    ff_sem, w_sem, n_sem, slope_sem, e_sem, row_sem, own_sem,
):
    s, z, c, x, y = place()
    near_x, near_y, twin = peers(s, z, c, x, y)
    wide = 2 * HEAD_DIM
    pairs = WIDTH // wide
    sent = []

    def remote(src, dst, ss, rs, device):
        return pltpu.make_async_remote_copy(
            src_ref=src, dst_ref=dst, send_sem=ss, recv_sem=rs, device_id=device, device_id_type=MESH
        )

    def go(copy):
        copy.start()
        sent.append(copy)

    def fetch(src, dst, sem):
        return pltpu.make_async_copy(src, dst, sem)

    layers = list(reversed(range(LAYERS)))

    def norm_loads(l):
        return [fetch(s_n.at[l, k], n_v.at[k], n_sem.at[k]) for k in range(2)] + [
            fetch(s_rs.at[l, k], rs_v.at[k], n_sem.at[2 + k]) for k in range(2)
        ]

    def block_loads(l, i):
        slot = i % 2
        return [
            fetch(w_ff.at[l, i, 1], ff_v.at[slot, 1], ff_sem.at[slot, 1]),
            fetch(s_gp.at[l, i], slope_v.at[slot], slope_sem.at[slot]),
            fetch(w_ff.at[l, i, 0], ff_v.at[slot, 0], ff_sem.at[slot, 0]),
        ]

    def out_load(l):
        return fetch(w_out.at[l], wout_v, w_sem.at[0])

    def in_load(l):
        return fetch(w_in.at[l], win_v, w_sem.at[1])

    def row_loads(l):
        return [fetch(s_qkv.at[l], qkv_v, row_sem.at[0]), fetch(s_mix.at[l], mix_v, row_sem.at[1])]

    depth = 4

    def expo_loads(step):
        l, p, slot = LAYERS - 1 - lax.div(step, pairs), lax.rem(step, pairs), lax.rem(step, depth)
        return (
            fetch(s_expo.at[l, p], e_v.at[slot], e_sem.at[slot, 0]),
            fetch(s_inv.at[l, p], inv_v.at[slot], e_sem.at[slot, 1]),
        )

    def start(copies):
        for copy in copies:
            copy.start()

    def wait(copies):
        for copy in copies:
            copy.wait()

    near_z, far_z = (s, z + 1 - 2 * lax.rem(z, 2)), (s, lax.rem(z + 2, RING))
    partners = (near_z, far_z, twin, near_x, near_y)

    early, late, every = pl.ds(8, TOTAL_ROWS - 8), pl.ds(0, 8), pl.ds(0, TOTAL_ROWS)

    def swap(here, stage):
        which = 1 if here is late else 0
        return remote(sum_v.at[stage, here], got_v.at[stage, here], r_s.at[which, stage], r_r.at[which, stage],
                      partners[stage])

    def take(here, stage):
        swap(here, stage).wait_recv()
        sum_v[stage + 1, here] = sum_v[stage, here] + got_v[stage, here]

    def fold(value):
        total = value[0:8]
        for k in range(1, value.shape[0] // 8):
            total = total + value[8 * k:8 * k + 8]
        return total

    def rows_loop(body, rows=64):
        def step(r, carry):
            body(pl.ds(pl.multiple_of(r * rows, rows), rows))
            return carry
        lax.fori_loop(0, SLOTS // rows, step, 0)

    def put(at, value):
        sum_v[0, pl.ds(at, 1)] = value

    def norm_back(grad, gain, which, rr):
        n = n_v[which, rr].astype(F32)
        u = grad * gain
        mean = jnp.sum(u, -1, keepdims=True) * (1.0 / WIDTH)
        tilt = jnp.sum(u * n, -1, keepdims=True) * (1.0 / WIDTH)
        return (u - mean - n * tilt) * rs_v[which, rr, 0:1]

    def layer_back(l, last):
        row = functools.partial(sum_row, l)
        wait(norm_loads(l)[1::2])
        part_v[...] = jnp.zeros_like(part_v)

        def second(rr):
            grad = out_v[rr].astype(F32) if l == layers[0] else g_v[rr]
            part_v[0] += fold(grad)
            out = norm_back(grad, gain2_ref[l:l + 1], 1, rr)
            part_v[1] += fold(out)
            gs_v[rr] = out
            low_v[rr] = out.astype(BF16)
        rows_loop(second)
        put(row(5), jnp.sum(part_v[0], 0, keepdims=True))
        put(row(4), jnp.sum(part_v[1], 0, keepdims=True))

        for i in range(RING):
            slot = i % 2
            loads = block_loads(l, i)
            wait(loads[:2])
            for k in range(WIDTH // CHUNK):
                cols = pl.ds(k * CHUNK, CHUNK)
                value = nn(low_v[...], ff_v[slot, 1, :, cols]) * slope_v[slot, :, cols].astype(F32)
                sum_v[0, pl.ds(row(6 + i), 1), cols] = jnp.sum(value, 0, keepdims=True)
                gh_v[:, cols] = value.astype(BF16)
            loads[2].wait()
            for k in range(2):
                cols = pl.ds(k * SLOTS, SLOTS)
                value = nt(gh_v[...], ff_v[slot, 0, pl.ds(k * SLOTS, SLOTS)])
                if i == 0:
                    acc_v[:, cols] = value
                else:
                    acc_v[:, cols] += value
            if i + 2 < RING:
                start(block_loads(l, i + 2))
            if i == 0 and l == layers[0]:
                greeted()
                for step in range(1, RING):
                    go(act_copy(step))
            if i == 1:
                start(norm_loads(l)[0::2])
                out_load(l).start()
            elif i == 2:
                start(row_loads(l))
            elif i == 3 and l == layers[0]:
                for step in range(depth):
                    start(expo_loads(jnp.int32(step)))

        if l == layers[0]:
            act_own()[0].wait()
            act_own()[1].start()
            act_own()[1].wait()
        wait(norm_loads(l)[0::2])
        part_v[...] = jnp.zeros_like(part_v)

        def first(rr):
            grad = gs_v[rr] + acc_v[rr]
            part_v[0] += fold(grad)
            out = norm_back(grad, gain1_ref[l:l + 1], 0, rr)
            part_v[1] += fold(out)
            gs_v[rr] = out
            low_v[rr] = out.astype(BF16)
        rows_loop(first)
        put(row(3), jnp.sum(part_v[0], 0, keepdims=True))
        put(row(2), jnp.sum(part_v[1], 0, keepdims=True))
        in_load(l).start()
        out_load(l).wait()
        for k in range(2):
            gm_v[:, pl.ds(k * SLOTS, SLOTS)] = nt(low_v[...], wout_v[pl.ds(k * SLOTS, SLOTS)]).astype(BF16)
        wait(row_loads(l))
        lane = lax.broadcasted_iota(jnp.int32, (SLOTS, wide), 1) < HEAD_DIM
        offset = layers.index(l) * pairs

        def attend(p, carry):
            step = offset + p
            slot = lax.rem(step, depth)
            for copy in expo_loads(step):
                copy.wait()
            at = lambda k: pl.ds(pl.multiple_of(k * WIDTH + p * wide, wide), wide)
            q, k, v = qkv_v[:, at(0)], qkv_v[:, at(1)], qkv_v[:, at(2)]
            gm = gm_v[:, at(0)].astype(F32) * inv_v[slot]
            mixed = mix_v[:, at(0)]
            mine = (lane, jnp.logical_not(lane))
            low = [jnp.where(m, gm, 0.0).astype(BF16) for m in mine]
            inner = [jnp.sum(part.astype(F32) * mixed, -1, keepdims=True) for part in low]
            gs = [
                (e_v[slot, h].astype(F32) * (nt(low[h], v) - inner[h])).astype(BF16) for h in range(2)
            ]
            both = jnp.concatenate([jnp.where(m, q, jnp.zeros_like(q)) for m in mine], 0)
            gk = tn(jnp.concatenate(gs, 0), both)
            gv = tn(e_v[slot].reshape(2 * SLOTS, SLOTS), jnp.concatenate(low, 0)).astype(BF16)
            gq = (jnp.where(lane, nn(gs[0], k), nn(gs[1], k)) * (HEAD_DIM ** -0.5)).astype(BF16)
            gproj_v[:, at(0)] = gq
            gproj_v[:, at(1)] = gk.astype(BF16)
            gproj_v[:, at(2)] = gv
            sum_v[0, pl.ds(row(0), 1), at(0)] = jnp.sum(gq.astype(F32), 0, keepdims=True)
            sum_v[0, pl.ds(row(1), 1), at(0)] = jnp.sum(gv.astype(F32), 0, keepdims=True)

            @pl.when(step + depth < LAYERS * pairs)
            def _():
                for copy in expo_loads(step + depth):
                    copy.start()
            return carry

        if not last:
            lax.fori_loop(0, pairs // 2, attend, 0)
            start(norm_loads(l - 1)[1::2])
            start(block_loads(l - 1, 0))
            lax.fori_loop(pairs // 2, pairs, attend, 0)
            start(block_loads(l - 1, 1))
            in_load(l).wait()
            for k in range(WIDTH // CHUNK):
                cols = pl.ds(k * CHUNK, CHUNK)
                g_v[:, cols] = gs_v[:, cols] + nt(gproj_v[...], win_v[pl.ds(k * CHUNK, CHUNK)])
        else:
            go(swap(early, 0))
            lax.fori_loop(0, pairs // 2, attend, 0)
            take(early, 0)
            go(swap(early, 1))
            lax.fori_loop(pairs // 2, pairs, attend, 0)
            go(swap(late, 0))
            in_load(l).wait()
            for k in range(WIDTH // CHUNK):
                cols = pl.ds(k * CHUNK, CHUNK)
                out_v[:, cols] = (gs_v[:, cols] + nt(gproj_v[...], win_v[pl.ds(k * CHUNK, CHUNK)])).astype(BF16)
                far = jnp.where(z < 2, 3, 1)
                for step in (2, far, RING - far):
                    grad_copy(step, k).start()
                grad_own(k).start()
                if k == 0:
                    take(late, 0)
                    go(swap(late, 1))
            take(early, 1)
            take(late, 1)
            for stage in range(2, 5):
                go(swap(every, stage))
                take(every, stage)
            sums_out[...] = sum_v[5]

    def part(to):
        return pl.ds(pl.multiple_of(to * QUARTER, QUARTER), QUARTER)

    def act_copy(step):
        to = lax.rem(z + step, RING)
        return remote(act_row.at[part(to)], act_out.at[z], a_s.at[step], a_r.at[step], (s, to))

    def act_own():
        held = gm_v.at[pl.ds(0, QUARTER)]
        return fetch(act_row.at[part(z)], held, own_sem.at[0]), fetch(held, act_out.at[z], own_sem.at[0])

    def grad_copy(step, k):
        to, cols = lax.rem(z + step, RING), pl.ds(k * CHUNK, CHUNK)
        return remote(out_v.at[part(to), cols], grad_out.at[z, :, cols], o_s.at[0], o_r.at[step, k], (s, to))

    def grad_own(k):
        cols = pl.ds(k * CHUNK, CHUNK)
        return fetch(out_v.at[part(z), cols], grad_out.at[z, :, cols], own_sem.at[1 + k])

    top = LAYERS - 1
    cot = fetch(cot_row, out_v, row_sem.at[2])
    cot.start()
    start(norm_loads(top)[1::2])
    start(block_loads(top, 0))
    start(block_loads(top, 1))
    greet(near_x, near_y, twin, s, z)
    act_own()[0].start()
    sum_v[0] = jnp.zeros((TOTAL_ROWS, WIDTH), F32)
    cot.wait()
    for l in layers:
        layer_back(l, l == 0)
    for step in range(1, RING):
        act_copy(step).wait_recv()
    for k in range(WIDTH // CHUNK):
        grad_own(k).wait()
        for step in range(1, RING):
            grad_copy(step, k).wait_recv()
    for copy in sent:
        copy.wait_send()
    whole = out_v.at[pl.ds(0, SLOTS - QUARTER)]
    remote(whole, whole, o_s.at[0], o_r.at[1, 0], twin).wait_send()


def backward(gains, weights, saved, cot_row, act_row):
    shape = jax.ShapeDtypeStruct
    dma = pltpu.SemaphoreType.DMA
    vmem = lambda *dims_type: pltpu.VMEM(dims_type[:-1], dims_type[-1])
    rows = TOTAL_ROWS
    chunks = WIDTH // CHUNK
    anywhere = pl.BlockSpec(memory_space=pl.ANY)
    inside = pl.BlockSpec(memory_space=pltpu.VMEM)
    return pl.pallas_call(
        backward_kernel,
        out_shape=(
            shape((RING, QUARTER, WIDTH), BF16), shape((RING, QUARTER, WIDTH), BF16), shape((rows, WIDTH), F32),
        ),
        in_specs=[inside] * 2 + [anywhere] * 12,
        out_specs=[anywhere, anywhere, inside],
        scratch_shapes=[
            vmem(SLOTS, WIDTH, F32), vmem(SLOTS, WIDTH, F32), vmem(SLOTS, WIDTH, F32),
            vmem(SLOTS, WIDTH, BF16), vmem(SLOTS, WIDTH, BF16), vmem(SLOTS, WIDTH, BF16), vmem(8, 128, BF16),
            vmem(SLOTS, 3 * WIDTH, BF16), vmem(SLOTS, WIDTH, BF16),
            vmem(2, SLOTS, WIDTH, BF16), vmem(2, SLOTS, 128, F32), vmem(2, SLOTS, WIDTH, BF16),
            vmem(SLOTS, 3 * WIDTH, BF16), vmem(SLOTS, WIDTH, F32),
            vmem(4, 2, SLOTS, SLOTS, BF16), vmem(4, SLOTS, 128, F32),
            vmem(2, 2, WIDTH, WIDTH, BF16), vmem(WIDTH, WIDTH, BF16), vmem(WIDTH, 3 * WIDTH, BF16),
            vmem(2, 8, WIDTH, F32), vmem(6, rows, WIDTH, F32), vmem(5, rows, WIDTH, F32),
            dma((RING,)), dma((RING,)), dma((1,)), dma((RING, chunks)),
            dma((2, 5)), dma((2, 5)),
            dma((2, 2)), dma((2,)), dma((4,)), dma((2,)), dma((4, 2)), dma((3,)), dma((1 + chunks,)),
        ],
        compiler_params=pltpu.CompilerParams(
            collective_id=1, has_side_effects=True, vmem_limit_bytes=60 << 20
        ),
        cost_estimate=pl.CostEstimate(flops=40 * 10**9, bytes_accessed=100 << 20, transcendentals=10**6),
    )(*gains, *weights, cot_row, act_row, *saved)


def deliver_kernel(act_ref, grad_ref, sums_ref, act_out, grad_out, *small_outs):
    act_out[...] = act_ref[...]
    grad_out[...] = grad_ref[...].astype(F32)

    @pl.when(pl.program_id(0) == 0)
    def _():
        for out, kind in zip(small_outs, (0, 1, 2, 3, 6, 4, 5)):
            for l in range(LAYERS):
                for k in range(out.shape[1] // WIDTH):
                    at = sum_row(l, kind + k)
                    out[l:l + 1, k * WIDTH:(k + 1) * WIDTH] = sums_ref[at:at + 1]


def deliver(activations, grad, sums):
    shape = jax.ShapeDtypeStruct
    whole = lambda *dims: pl.BlockSpec(dims, lambda i: (0,) * len(dims))
    block = pl.BlockSpec((RING // 2, QUARTER, WIDTH), lambda i: (i, 0, 0))
    widths = [WIDTH] * 4 + [RING * WIDTH] + [WIDTH] * 2
    return pl.pallas_call(
        deliver_kernel,
        grid=(2,),
        out_shape=[shape(grad.shape, BF16), shape(grad.shape, F32)] + [shape((LAYERS, w), F32) for w in widths],
        in_specs=[block, block, whole(TOTAL_ROWS, WIDTH)],
        out_specs=[block, block] + [whole(LAYERS, w) for w in widths],
    )(activations, grad, sums)


def whole_rows(
    tokens, lengths, separators, type_table, project_in, project_out, up_weight, down_weight, first_norm_gain,
    second_norm_gain, query_bias, value_bias, output_bias, first_norm_bias, hidden_bias, down_bias,
    second_norm_bias, cotangent,
):
    small = (
        type_table, first_norm_gain, second_norm_gain, query_bias, value_bias, output_bias, first_norm_bias,
        hidden_bias, down_bias, second_norm_bias,
    )
    g_in, g_out, g_ff, cot_row, act_row, *saved = forward(
        lengths, separators, tokens, cotangent, project_in, project_out, up_weight, down_weight, small
    )
    weights = (
        g_in.reshape(LAYERS, WIDTH, 3 * WIDTH),
        g_out.reshape(LAYERS, WIDTH, WIDTH),
        g_ff.reshape(LAYERS, RING, 2, WIDTH, WIDTH),
    )
    return tuple(deliver(*backward((first_norm_gain, second_norm_gain), weights, saved, cot_row, act_row)))


def layer_norm(total, gain, bias):
    mean = jnp.mean(total, -1, keepdims=True)
    centered = total - mean
    spread = jnp.mean(centered * centered, -1, keepdims=True)
    return centered * lax.rsqrt(spread + EPS) * gain + bias


def gelu_exact(value):
    return jax.nn.gelu(value, approximate=False)


def contract_last(left, right):
    return lax.dot_general(
        left, right, (((1,), (1,)), ((), ())), preferred_element_type=jnp.float32
    )


def split_heads(block):
    return block.reshape(block.shape[0], -1, HEAD_DIM)


def masked_scores(queries, keys, length):
    scores = jnp.einsum(
        "qhd,khd->hqk", queries, keys, preferred_element_type=jnp.float32
    ) * HEAD_DIM ** (-0.5)
    valid = jnp.arange(keys.shape[0]) < length
    return jnp.where(valid[None, None, :], scores, MASKED)


def attend_forward(packed):
    projected, length = packed
    slots = projected.shape[0]
    queries = split_heads(projected[:, 0])
    keys = split_heads(projected[:, 1])
    values = split_heads(projected[:, 2])
    scores = masked_scores(queries, keys, length)
    peak = jnp.max(scores, -1, keepdims=True)
    expo = jnp.exp(scores - peak)
    total = jnp.sum(expo, -1, keepdims=True)
    probs = (expo / total).astype(jnp.bfloat16)
    mixed = jnp.einsum("hqk,khd->qhd", probs, values, preferred_element_type=jnp.float32)
    return (mixed.astype(jnp.bfloat16).reshape(slots, -1), (peak + jnp.log(total))[:, :, 0])


def attend_backward(packed):
    projected, length, log_total, grad_mixed = packed
    slots = projected.shape[0]
    queries = split_heads(projected[:, 0])
    keys = split_heads(projected[:, 1])
    values = split_heads(projected[:, 2])
    scores = masked_scores(queries, keys, length)
    probs = jnp.exp(scores - log_total[:, :, None])
    grad_out = split_heads(grad_mixed)
    grad_probs = jnp.einsum("qhd,khd->hqk", grad_out, values, preferred_element_type=jnp.float32)
    inner = jnp.sum(grad_probs * probs, -1, keepdims=True)
    grad_scores = (probs * (grad_probs - inner)).astype(jnp.bfloat16)
    scale = HEAD_DIM ** (-0.5)
    grad_queries = (
        jnp.einsum("hqk,khd->qhd", grad_scores, keys, preferred_element_type=jnp.float32) * scale
    )
    grad_keys = (
        jnp.einsum("hqk,qhd->khd", grad_scores, queries, preferred_element_type=jnp.float32) * scale
    )
    grad_values = jnp.einsum(
        "hqk,qhd->khd", probs.astype(jnp.bfloat16), grad_out, preferred_element_type=jnp.float32
    )
    stacked = jnp.stack([grad_queries, grad_keys, grad_values], 1)
    return stacked.reshape(slots, 3, -1).astype(jnp.bfloat16)


def feed_forward(rows, up_part, down_part, bias_part):
    hidden = jnp.dot(rows, up_part, preferred_element_type=jnp.float32) + bias_part
    active = gelu_exact(hidden).astype(jnp.bfloat16)
    return jnp.dot(active, down_part, preferred_element_type=jnp.float32)


def split_heads_plan(
    tokens,
    lengths,
    separators,
    type_table,
    project_in,
    project_out,
    up_weight,
    down_weight,
    first_norm_gain,
    second_norm_gain,
    query_bias,
    value_bias,
    output_bias,
    first_norm_bias,
    hidden_bias,
    down_bias,
    second_norm_bias,
    cotangent,
):
    row_count, slot_part, width = tokens.shape
    token_count = row_count * slot_part
    hidden_part = up_weight.shape[2]
    offset = lax.axis_index("head") * hidden_part
    positions = lax.axis_index("head") * slot_part + jnp.arange(slot_part)
    second = (positions[None, :] > separators[:, None]) & (positions[None, :] < lengths[:, None])
    state = tokens.astype(jnp.float32) + jnp.where(second[:, :, None], type_table[1], type_table[0])
    state = state.reshape(token_count, width)

    def fetch(layer):
        gathered = (
            lax.all_gather(project_in[layer], "seq", axis=0, tiled=True),
            lax.all_gather(project_out[layer], "seq", axis=0, tiled=True),
            lax.all_gather(up_weight[layer], "seq", axis=0, tiled=True),
            lax.all_gather(down_weight[layer], "seq", axis=1, tiled=True),
        )
        return (gathered[0], gathered[1], gathered[2], gathered[3])

    def layer_hidden_bias(layer):
        return lax.dynamic_slice_in_dim(hidden_bias[layer], offset, hidden_part, 0)

    saved = []
    for layer in range(LAYERS):
        weights = fetch(layer)
        inner_in, inner_out, up_part, down_part = weights
        joined = jnp.concatenate(
            [query_bias[layer], jnp.zeros_like(query_bias[layer]), value_bias[layer]]
        )
        projected = (
            jnp.dot(state.astype(jnp.bfloat16), inner_in, preferred_element_type=jnp.float32)
            + joined
        ).astype(jnp.bfloat16)
        heads = lax.all_to_all(
            projected.reshape(row_count, slot_part, 3, width),
            "head",
            split_axis=3,
            concat_axis=1,
            tiled=True,
        )
        mixed, log_total = lax.map(attend_forward, (heads, lengths))
        mixed = lax.all_to_all(mixed, "head", split_axis=1, concat_axis=2, tiled=True).reshape(
            token_count, width
        )
        first_sum = (
            state
            + jnp.dot(mixed, inner_out, preferred_element_type=jnp.float32)
            + output_bias[layer]
        )
        normed = layer_norm(first_sum, first_norm_gain[layer], first_norm_bias[layer])
        normed_low = normed.astype(jnp.bfloat16)
        bias_part = layer_hidden_bias(layer)
        rows_all = lax.all_gather(normed_low[None], "head", axis=0, tiled=True).reshape(-1, width)
        branch_out = lax.psum_scatter(
            feed_forward(rows_all, up_part, down_part, bias_part).astype(jnp.bfloat16),
            "head",
            scatter_dimension=0,
            tiled=True,
        ).astype(jnp.float32)
        second_sum = normed + branch_out + down_bias[layer]
        saved.append((heads, log_total, first_sum, second_sum, rows_all))
        state = layer_norm(second_sum, second_norm_gain[layer], second_norm_bias[layer])
    activations = state.astype(jnp.bfloat16).reshape(row_count, slot_part, width)
    grad = cotangent.astype(jnp.float32).reshape(token_count, width)
    query_grads = [None] * LAYERS
    value_grads = [None] * LAYERS
    output_grads = [None] * LAYERS
    first_grads = [None] * LAYERS
    hidden_grads = [None] * LAYERS
    down_grads = [None] * LAYERS
    second_grads = [None] * LAYERS
    for layer in reversed(range(LAYERS)):
        heads, log_total, first_sum, second_sum, rows_all = saved[layer]
        weights = fetch(layer)
        inner_in, inner_out, up_part, down_part = weights
        second_grads[layer] = jnp.sum(grad, 0)
        _, norm_back = jax.vjp(
            functools.partial(layer_norm, gain=second_norm_gain[layer], bias=second_norm_bias[layer]),
            second_sum,
        )
        grad_second = norm_back(grad)[0]
        down_grads[layer] = jnp.sum(grad_second, 0)
        grad_low = grad_second.astype(jnp.bfloat16)
        bias_part = layer_hidden_bias(layer)
        grad_rows = lax.all_gather(grad_low[None], "head", axis=0, tiled=True).reshape(-1, width)
        hidden = jnp.dot(rows_all, up_part, preferred_element_type=jnp.float32) + bias_part
        grad_active = contract_last(grad_rows, down_part)
        _, gelu_back = jax.vjp(gelu_exact, hidden)
        grad_hidden = gelu_back(grad_active)[0]
        hidden_local = jnp.sum(grad_hidden, 0)
        grad_hidden_low = grad_hidden.astype(jnp.bfloat16)
        hidden_grads[layer] = lax.dynamic_update_slice_in_dim(
            jnp.zeros_like(hidden_bias[layer]), hidden_local, offset, 0
        )
        grad_normed = grad_second + lax.psum_scatter(
            contract_last(grad_hidden_low, up_part).astype(jnp.bfloat16),
            "head",
            scatter_dimension=0,
            tiled=True,
        ).astype(jnp.float32)
        first_grads[layer] = jnp.sum(grad_normed, 0)
        _, norm_back = jax.vjp(
            functools.partial(layer_norm, gain=first_norm_gain[layer], bias=first_norm_bias[layer]), first_sum
        )
        grad_first = norm_back(grad_normed)[0]
        output_grads[layer] = jnp.sum(grad_first, 0)
        grad_mixed = contract_last(grad_first.astype(jnp.bfloat16), inner_out).astype(jnp.bfloat16)
        grad_heads = lax.all_to_all(
            grad_mixed.reshape(row_count, slot_part, width),
            "head",
            split_axis=2,
            concat_axis=1,
            tiled=True,
        )
        grad_projected = lax.map(attend_backward, (heads, lengths, log_total, grad_heads))
        grad_projected = lax.all_to_all(
            grad_projected, "head", split_axis=1, concat_axis=3, tiled=True
        ).reshape(token_count, 3 * width)
        query_grads[layer] = jnp.sum(grad_projected[:, :width], 0, dtype=jnp.float32)
        value_grads[layer] = jnp.sum(grad_projected[:, 2 * width :], 0, dtype=jnp.float32)
        grad = grad_first + contract_last(grad_projected, inner_in)
    summed = lax.psum(
        (
            jnp.stack(query_grads),
            jnp.stack(value_grads),
            jnp.stack(output_grads),
            jnp.stack(first_grads),
            jnp.stack(hidden_grads),
            jnp.stack(down_grads),
            jnp.stack(second_grads),
        ),
        ("seq", "head"),
    )
    input_grad = grad.reshape(row_count, slot_part, width)
    return (
        activations,
        input_grad,
        summed[0],
        summed[1],
        summed[2],
        summed[3],
        summed[4],
        summed[5],
        summed[6],
    )


def solution(mesh):
    placed = (
        P("seq", "head", None),
        P("seq"),
        P("seq"),
        P(),
        P(None, "seq", None),
        P(None, "seq", None),
        P(None, "seq", "head"),
        P(None, "head", "seq"),
        P(),
        P(),
        P(),
        P(),
        P(),
        P(),
        P(),
        P(),
        P(),
        P("seq", "head", None),
    )
    shape = dict(mesh.shape)
    fits = shape == {"seq": 8, "head": RING}
    return jax.shard_map(
        whole_rows if fits else split_heads_plan,
        mesh=mesh,
        in_specs=placed,
        out_specs=(
            P("seq", "head", None),
            P("seq", "head", None),
            P(),
            P(),
            P(),
            P(),
            P(),
            P(),
            P(),
        ),
        check_vma=False,
    )
```
